32 devices in a mesh: fsdp: 4 (over y, x), ctx: 4 (over z), tp: 2 (over core).
Axes of the slice: x: 2, y: 2, z: 4, core: 2. Of those that a mesh axis runs over, the one named last changes fastest.
Arguments:
- block_input: bfloat16 [4, 2048, 1536], P('fsdp', 'ctx'), may hold values from -6 to 6
- out_cotangent: bfloat16 [4, 2048, 1536], P('fsdp', 'ctx'), may hold values from -6 to 6
- block_ids: int32 [4, 2048], P('fsdp'), may hold values from 0 to 12, never falling along the last dimension, each value on 1 to 256 neighbouring positions
- expert_routes: int32 [4, 2048, 8], P('fsdp', 'ctx'), may hold values from 0 to 15, all different within a row; in each aligned block of 512 rows (0 to 511, 512 to 1023, ..., all dimensions but the last counted through in order) at most 384 rows name the same one
- norm_gains: float32 [2, 1536], P(None, 'fsdp'), may hold values from 0.5 to 1.5
- gains_first: float32 [2, 1536], P(None, 'fsdp'), may hold values from -128 to 128
- gains_second: float32 [2, 1536], P(None, 'fsdp'), may hold values from 1638.4 to 6553.6
- joint_weight: float32 [1536, 2560], P('fsdp', 'tp'), may hold values from -0.15625 to 0.15625
- joint_first: float32 [1536, 2560], P('fsdp', 'tp'), may hold values from -128 to 128
- joint_second: float32 [1536, 2560], P('fsdp', 'tp'), may hold values from 1720.32 to 6881.28
- output_weight: float32 [1536, 1536], P('fsdp', 'tp'), may hold values from -1.75 to 1.75
- output_first: float32 [1536, 1536], P('fsdp', 'tp'), may hold values from -6 to 6
- output_second: float32 [1536, 1536], P('fsdp', 'tp'), may hold values from 13.9264 to 55.7056
- router_weight: float32 [1536, 16], P('fsdp'), may hold values from -0.078125 to 0.078125
- router_first: float32 [1536, 16], P('fsdp'), may hold values from -448 to 448
- router_second: float32 [1536, 16], P('fsdp'), may hold values from 21708.8 to 86016
- expert_weight: float32 [1536, 16, 3, 512], P('fsdp', None, None, 'tp')
- expert_first: float32 [1536, 16, 3, 512], P('fsdp', None, None, 'tp')
- expert_second: float32 [1536, 16, 3, 512], P('fsdp', None, None, 'tp')
Outputs:
- block_output: bfloat16 [4, 2048, 1536], P('fsdp', 'ctx')
- input_grad: float32 [4, 2048, 1536], P('fsdp', 'ctx')
- gains_master: float32 [2, 1536], P(None, 'fsdp')
- gains_moment: float32 [2, 1536], P(None, 'fsdp')
- gains_square: float32 [2, 1536], P(None, 'fsdp')
- gains_rounded: bfloat16 [2, 1536], P(None, 'fsdp')
- joint_master: float32 [1536, 2560], P('fsdp', 'tp')
- joint_moment: float32 [1536, 2560], P('fsdp', 'tp')
- joint_square: float32 [1536, 2560], P('fsdp', 'tp')
- joint_rounded: bfloat16 [1536, 2560], P('fsdp', 'tp')
- output_master: float32 [1536, 1536], P('fsdp', 'tp')
- output_moment: float32 [1536, 1536], P('fsdp', 'tp')
- output_square: float32 [1536, 1536], P('fsdp', 'tp')
- output_rounded: bfloat16 [1536, 1536], P('fsdp', 'tp')
- router_master: float32 [1536, 16], P('fsdp')
- router_moment: float32 [1536, 16], P('fsdp')
- router_square: float32 [1536, 16], P('fsdp')
- router_rounded: bfloat16 [1536, 16], P('fsdp')
- expert_master: float32 [1536, 16, 3, 512], P('fsdp', None, None, 'tp')
- expert_moment: float32 [1536, 16, 3, 512], P('fsdp', None, None, 'tp')
- expert_square: float32 [1536, 16, 2, 512], P('fsdp', None, None, 'tp')
- down_square: float32 [1536, 16, 512], P('fsdp', None, 'tp')
- expert_rounded: bfloat16 [1536, 16, 3, 512], P('fsdp', None, None, 'tp')
The draws below stay inside these ranges and needn't reach their ends.
Inputs may be any that keep to these rules, and one draw needn't show every extreme that they name: `block_ids`: within a sequence the ids never fall along the positions, each id holds 1 to 256 positions, and one holds exactly 256. `expert_routes`: each row names 8 different experts. In each aligned block of 512 rows (the rows of one device) no expert is named by more than 384 rows, and in some blocks one expert is named by exactly 384.
All inputs are finite; a program needn't handle non-finite values.
Results may differ from the reference program's by a relative error of at most 0.025.
Values may be sent and summed in bfloat16 or wider, within the bound.
A program may use at most 448 MiB of HBM per device.

```python
import math
import jax
import jax.numpy as jnp
import numpy as np
from jax import lax

D = 1536
QUERY_HEADS = 24
KEY_VALUE_HEADS = 8
HEAD_SIZE = 64
FF = 512
TOPK = 8
E = 16
STEP = 10
TOK_DEV = 512
QKV = 2560
LEN = 2048
NSEQ = 4
TOKENS = 8192
CAP = 384
SPAN = 256
NBLK = 13


def unit_noise(key, shape):
    return jnp.clip(jax.random.normal(key, shape, jnp.float32), -6.0, 6.0)


def slot_column(entries):
    return jnp.array(entries, jnp.float32).reshape(1, 1, 3, 1)


def grad_scale():
    routed = math.sqrt(TOKENS * TOPK / E)
    return slot_column([0.6 * routed, 0.6 * routed, 0.074 * routed])


def draw_expert_weight(key, part):
    return unit_noise(key, (D, E, 3, FF)) * slot_column([D ** (-0.5), D ** (-0.5), (FF // 24) ** (-0.5)])


def draw_expert_first(key, part):
    return unit_noise(key, (D, E, 3, FF)) * (0.111 * grad_scale())


def draw_expert_second(key, part):
    levels = jnp.exp(jax.random.uniform(key, (D, E, 3, FF), jnp.float32, math.log(0.053), math.log(0.21)))
    scale_rows = grad_scale()
    return levels * scale_rows * scale_rows


def spiked(values, rng, source, target, parts, factor):
    def block_of(axis_at):
        return (jnp.arange(values.shape[axis_at]) // (values.shape[axis_at] // parts)).reshape((-1,) + (1,) * (values.ndim - 1 - axis_at))

    near = jax.random.permutation(rng, parts)[block_of(target)]
    far = (block_of(target) + parts // 2) % parts
    return jnp.where((block_of(source) == near) | (block_of(source) == far), factor * values, values)


def steps_of(stream_key, extent, cuts, least, largest):
    level = 1.0
    for dim, shards_of in cuts:
        draws = jax.random.uniform(jax.random.fold_in(jax.random.fold_in(stream_key, 6), dim), (shards_of,), jnp.float32, least / len(cuts), largest / len(cuts))
        level = level * jnp.repeat(jnp.exp(draws), extent[dim] // shards_of).reshape((-1,) + (1,) * (len(extent) - 1 - dim))
    return level


def split_up(number_of, total, most, lean):
    loads = [(1 << 20) // math.isqrt(rank ** lean) + 1 for rank in range(2, number_of + 1)]
    rest, given = total - most - (number_of - 1), [1] * (number_of - 1)
    while rest > 0:
        movable = [i for i in range(number_of - 1) if given[i] < most]
        mass, remaining = sum([loads[i] for i in movable]), rest
        for i in movable:
            extra = min(most - given[i], max(1, remaining * loads[i] // mass), rest)
            given[i] = given[i] + extra
            rest = rest - extra
    return np.array([most] + given)


def uneven_parts(own_key, count, total, bound, slope):
    if count == 2:
        one = jax.random.randint(own_key, (), max(1, total - bound), min(bound, total - 1) + 1)
        return jnp.stack([one, total - one])
    lengths = jnp.asarray(split_up(count, total, bound, slope), jnp.int32)
    pairs = (count - 1) // 2
    source_of, sink = lengths[1:1 + 2 * pairs:2], lengths[2:2 + 2 * pairs:2]
    margin = jnp.minimum(source_of - 1, bound - sink)
    shifted = jax.random.randint(jax.random.fold_in(own_key, 1), (pairs,), 0, 1 << 20) % (margin + 1)
    lengths = lengths.at[1:1 + 2 * pairs:2].set(source_of - shifted).at[2:2 + 2 * pairs:2].set(sink + shifted)
    return lengths[jax.random.permutation(jax.random.fold_in(own_key, 2), count)]


def shared_out(own_key, own, number, rows, number_of, top, reach, slope):
    order = jax.random.permutation(own_key, number_of)
    packed, ordinary = load_shares(number_of, rows * top, reach, slope, True), load_shares(number_of, rows * top, reach, slope, False)
    places = jnp.arange(number_of)

    def named(lengths, rotation):
        used = int((lengths > 0).sum())
        fixed = max(1, used // 4)
        shifted = fixed + (places - fixed + rotation * (used - fixed)) % max(1, number_of - fixed)
        return jnp.zeros((number_of,), jnp.int32).at[order[jnp.where(places < fixed, places, shifted)]].set(jnp.asarray(lengths, jnp.int32))

    lengths = jnp.where(number % 4 == 0, named(packed, number // 4), named(ordinary, number - number // 4 - 1))
    mixed = jax.random.permutation(jax.random.fold_in(own, 3), number_of)
    giver, receiver = mixed[0:number_of // 2 * 2:2], mixed[1:number_of // 2 * 2:2]
    slack = jnp.minimum(lengths[giver] - 1, reach - lengths[receiver]) // 2
    slack = jnp.where((giver == order[0]) | (receiver == order[0]) | (lengths[receiver] == 0), 0, jnp.maximum(slack, 0))
    shifted = jax.random.randint(jax.random.fold_in(own, 4), (number_of // 2,), 0, 1 << 20) % (slack + 1)
    lengths = lengths.at[giver].add(-shifted).at[receiver].add(shifted)
    items = jnp.searchsorted(jnp.cumsum(lengths), jnp.arange(rows * top), side="right").astype(jnp.int32)
    table = items.reshape(top, rows).T
    table = table[jax.random.permutation(jax.random.fold_in(own, 1), rows)]
    rotation = jax.random.randint(jax.random.fold_in(own, 2), (rows, 1), 0, top)
    return jnp.take_along_axis(table, (jnp.arange(top)[None, :] + rotation) % top, axis=1)


def load_shares(amount, total, limit, lean, full):
    loads = [(1 << 20) // math.isqrt(grade ** lean) + 1 for grade in range(1, amount + 1)]
    largest = limit if full else min(limit, max(-(-total // amount), total * loads[0] // sum(loads)))
    least = 1 if total - largest >= amount - 1 else 0
    given, surplus = [largest] + [least] * (amount - 1), total - largest - least * (amount - 1)
    while surplus > 0:
        movable = [i for i in range(1, amount) if given[i] < largest] or [i for i in range(1, amount) if given[i] < limit]
        mass, left = sum([loads[i] for i in movable]), surplus
        for i in movable:
            addition = min(limit - given[i], max(1, left * loads[i] // mass), surplus)
            given[i] = given[i] + addition
            surplus = surplus - addition
    return np.array(given)


def gaussian(key, extent, scale, reach, cuts=(), kind=jnp.bfloat16):
    level = steps_of(key, extent, cuts, -0.22, 0.18) if cuts else 1.0
    values = jax.random.normal(key, extent, jnp.float32) * scale * level
    return jnp.minimum(jnp.maximum(values, -reach), reach).astype(kind)


def bell_draw_with(own_key, shape, width, reach, pieces, heavy, held_as=jnp.bfloat16):
    drawn = width * jax.random.normal(own_key, shape, jnp.float32)
    if pieces:
        drawn = drawn * steps_of(own_key, shape, pieces, -0.22, 0.18)
    return jnp.clip(spiked(drawn, jax.random.fold_in(own_key, 3), *heavy), -reach, reach).astype(held_as)


def setup_inputs(seed: int = 0) -> dict:
    splits = jax.random.split(jax.random.key(seed), 20)
    block_input = bell_draw_with(splits[0], (NSEQ, LEN, D), 1.0, 6.0, ((0, 4), (1, 4)), (0, 2, 4, 2.0))
    out_cotangent = bell_draw_with(splits[1], (NSEQ, LEN, D), 1.0, 6.0, ((0, 4), (1, 4)), (0, 2, 4, 2.0))
    block_ids = jax.vmap(lambda own: jnp.searchsorted(jnp.cumsum(uneven_parts(own, NBLK, LEN, SPAN, 1)), jnp.arange(LEN), side="right"))(jax.random.split(splits[2], NSEQ)).reshape((NSEQ, LEN)).astype(jnp.int32)
    expert_routes_keys = jax.random.split(jax.random.fold_in(splits[3], 1), NSEQ * LEN // TOK_DEV)
    expert_routes_turns = jax.random.permutation(jax.random.fold_in(splits[3], 3), NSEQ * LEN // TOK_DEV)
    expert_routes = jax.vmap(lambda own, number: shared_out(jax.random.fold_in(splits[3], 2), own, number, TOK_DEV, E, TOPK, CAP, 2))(expert_routes_keys, expert_routes_turns).reshape((NSEQ, LEN, TOPK))
    norm_gains = jnp.clip(1.0 + 0.1 * jax.random.normal(splits[4], (2, D), jnp.float32), 0.5, 1.5)
    gains_first = gaussian(splits[5], (2, D), (0.22 * TOKENS ** 0.5), 128.0, ((1, 4),), jnp.float32)
    gains_second = jnp.clip(jnp.exp(math.log(6553.6) - 1.3862944 * jax.random.uniform(splits[6], (2, D), jnp.float32) ** steps_of(splits[6], (2, D), ((1, 4),), -0.2, 0.2)), 1638.4, 6553.6)
    joint_weight = gaussian(splits[7], (D, QKV), D ** -0.5, 0.15625, ((0, 4), (1, 2)), jnp.float32)
    joint_first = gaussian(splits[8], (D, QKV), (0.22 * TOKENS ** 0.5), 128.0, ((0, 4), (1, 2)), jnp.float32)
    joint_second = jnp.clip(jnp.exp(math.log(6881.28) - 1.3862944 * jax.random.uniform(splits[9], (D, QKV), jnp.float32) ** steps_of(splits[9], (D, QKV), ((0, 4), (1, 2)), -0.2, 0.2)), 1720.32, 6881.28)
    output_weight = gaussian(splits[10], (D, QUERY_HEADS * HEAD_SIZE), (max(1, QUERY_HEADS * HEAD_SIZE * 16 // LEN)) ** -0.5, 1.75, ((0, 4), (1, 2)), jnp.float32)
    output_first = gaussian(splits[11], (D, QUERY_HEADS * HEAD_SIZE), (0.02 * TOKENS ** 0.5), 6.0, ((0, 4), (1, 2)), jnp.float32)
    output_second = jnp.clip(jnp.exp(math.log(55.7056) - 1.3862944 * jax.random.uniform(splits[12], (D, QUERY_HEADS * HEAD_SIZE), jnp.float32) ** steps_of(splits[12], (D, QUERY_HEADS * HEAD_SIZE), ((0, 4), (1, 2)), -0.2, 0.2)), 13.9264, 55.7056)
    router_weight = gaussian(splits[13], (D, E), (4 * D) ** -0.5, 0.078125, ((0, 4),), jnp.float32)
    router_first = gaussian(splits[14], (D, E), (1.1 * (TOKENS * TOPK / E) ** 0.5), 448.0, ((0, 4),), jnp.float32)
    router_second = jnp.clip(jnp.exp(math.log(86016.0) - 1.3768156 * jax.random.uniform(splits[15], (D, E), jnp.float32) ** steps_of(splits[15], (D, E), ((0, 4),), -0.2, 0.2)), 21708.8, 86016.0)
    expert_weight = draw_expert_weight(jax.random.fold_in(splits[19], 71), 0)
    expert_first = draw_expert_first(jax.random.fold_in(splits[19], 71), 0)
    expert_second = draw_expert_second(jax.random.fold_in(splits[19], 71), 0)
    return {"block_input": block_input, "out_cotangent": out_cotangent, "block_ids": block_ids, "expert_routes": expert_routes, "norm_gains": norm_gains, "gains_first": gains_first, "gains_second": gains_second, "joint_weight": joint_weight, "joint_first": joint_first, "joint_second": joint_second, "output_weight": output_weight, "output_first": output_first, "output_second": output_second, "router_weight": router_weight, "router_first": router_first, "router_second": router_second, "expert_weight": expert_weight, "expert_first": expert_first, "expert_second": expert_second}


@jax.custom_vjp
def low(v):
    return lax.optimization_barrier(v.astype(jnp.bfloat16)).astype(jnp.float32)

@jax.custom_vjp
def low_back(v):
    return v

def low_keep(v):
    return (low(v), None)

def low_pass(kept, grad):
    return (grad,)

def back_keep(v):
    return (v, None)

def back_low(kept, grad):
    return (low(grad),)
low.defvjp(low_keep, low_pass)
low_back.defvjp(back_keep, back_low)

def inverse_rms(rows):
    return lax.rsqrt(lax.optimization_barrier(jnp.mean(rows * rows, axis=-1, keepdims=True)) + 1e-06)

def rotary_tables(positions):
    halves = jnp.arange(HEAD_SIZE // 2).astype(jnp.float32)
    frequency = jnp.exp(halves * (-2.0 * math.log(10000.0) / HEAD_SIZE))
    angles = positions[:, None] * frequency[None, :]
    return (jnp.cos(angles), jnp.sin(angles))

def rotate(vectors, cosine, sine_part, inverse):
    trailing = (1,) * (vectors.ndim - 2)
    cos_rows = cosine.reshape((cosine.shape[0],) + trailing + (cosine.shape[1],))
    sin_rows = sine_part.reshape((sine_part.shape[0],) + trailing + (sine_part.shape[1],))
    middle = vectors.shape[-1] // 2
    leading = vectors[..., :middle]
    ending = vectors[..., middle:]
    if inverse:
        return jnp.concatenate([leading * cos_rows + ending * sin_rows, ending * cos_rows - leading * sin_rows], axis=-1)
    return jnp.concatenate([leading * cos_rows - ending * sin_rows, ending * cos_rows + leading * sin_rows], axis=-1)

def slot_tables(route_rows):
    flat_routes = route_rows.reshape(-1)
    member = (flat_routes[:, None] == jnp.arange(E, dtype=jnp.int32)[None, :]).astype(jnp.int32)
    rank_rows = lax.optimization_barrier(jnp.sum((jnp.cumsum(member, axis=0) - 1) * member, axis=1)).astype(jnp.int32)
    slot_ids = (flat_routes * CAP + rank_rows).astype(jnp.int32)
    entry_ids = jnp.arange(flat_routes.shape[0], dtype=jnp.int32)
    owners = jnp.full((E * CAP,), route_rows.shape[0], jnp.int32).at[slot_ids].set(entry_ids // TOPK)
    entries = jnp.full((E * CAP,), flat_routes.shape[0], jnp.int32).at[slot_ids].set(entry_ids)
    return (slot_ids.reshape(route_rows.shape), owners, entries)

def sequence_rows(tokens, id_rows, route_rows, gains_low, joint_low, output_low, router_low, expert_low):
    sequence_length = tokens.shape[0]
    heads_per_group = QUERY_HEADS // KEY_VALUE_HEADS
    scale_factor = 1.0 / math.sqrt(HEAD_SIZE)
    inv_first = inverse_rms(tokens)
    normed_first = low(tokens * inv_first * gains_low[0])
    combined_rows = low_back(jnp.dot(normed_first, joint_low, precision=lax.Precision.HIGHEST))
    grouped_queries = combined_rows.reshape(sequence_length, KEY_VALUE_HEADS, heads_per_group + 2, HEAD_SIZE)
    cosine, sine_part = rotary_tables(jnp.arange(sequence_length).astype(jnp.float32))
    query_rows = low(rotate(grouped_queries[:, :, :heads_per_group], cosine, sine_part, False))
    key_rows = low(rotate(grouped_queries[:, :, heads_per_group], cosine, sine_part, False))
    value_rows = low(grouped_queries[:, :, heads_per_group + 1])
    query_block = min(sequence_length, 512)

    def attend(row_start):
        block_queries = lax.dynamic_slice_in_dim(query_rows, row_start, query_block, 0)
        query_ids = lax.dynamic_slice_in_dim(id_rows, row_start, query_block, 0)
        scores = jnp.einsum('qhgd,khd->hgqk', block_queries, key_rows, precision=lax.Precision.HIGHEST) * scale_factor
        scores = low_back(scores)
        visible = query_ids[:, None] >= id_rows[None, :]
        masked = jnp.where(visible[None, None], scores, -1e+30)
        row_max = lax.optimization_barrier(jnp.max(masked, axis=-1, keepdims=True))
        exponent = jnp.exp(masked - row_max)
        probabilities = low(exponent / lax.optimization_barrier(jnp.sum(exponent, axis=-1, keepdims=True)))
        return jnp.einsum('hgqk,khd->qhgd', probabilities, value_rows, precision=lax.Precision.HIGHEST)
    block_starts = (jnp.arange(sequence_length // query_block) * query_block).astype(jnp.int32)
    attended = lax.map(jax.checkpoint(attend), block_starts).reshape(sequence_length, QUERY_HEADS * HEAD_SIZE)
    attended = low_back(low(attended))
    attn_out = low_back(jnp.dot(attended, output_low.T, precision=lax.Precision.HIGHEST))
    residual = tokens + attn_out
    inv_second = inverse_rms(residual)
    normed_second = low(residual * inv_second * gains_low[1])
    logits = low_back(jnp.dot(normed_second, router_low, precision=lax.Precision.HIGHEST))
    chosen = jnp.take_along_axis(logits, route_rows, axis=1)
    exponent = jnp.exp(chosen - lax.optimization_barrier(jnp.max(chosen, axis=1, keepdims=True)))
    gates = exponent / lax.optimization_barrier(jnp.sum(exponent, axis=1, keepdims=True))
    block_total = sequence_length // TOK_DEV
    normed_blocks = normed_second.reshape(block_total, TOK_DEV, D)
    route_blocks = route_rows.reshape(block_total, TOK_DEV, TOPK)
    slot_ids, owners, unused = jax.vmap(slot_tables)(route_blocks)
    padded_rows = jnp.concatenate([normed_blocks, jnp.zeros((block_total, 1, D), jnp.float32)], axis=1)
    dispatched = jax.vmap(lambda rows_here, owner_ids: rows_here[owner_ids])(padded_rows, owners)
    dispatched = dispatched.reshape(block_total, E, CAP, D)
    gate_up = low_back(jnp.einsum('becd,dejf->becjf', dispatched, expert_low[:, :, 0:2], precision=lax.Precision.HIGHEST))
    gate_part = gate_up[:, :, :, 0]
    hidden = low(gate_part * jax.nn.sigmoid(gate_part) * gate_up[:, :, :, 1])
    expert_out = low_back(jnp.einsum('becf,def->becd', hidden, expert_low[:, :, 2], precision=lax.Precision.HIGHEST))
    expert_out = expert_out.reshape(block_total, E * CAP, D)
    picked = jax.vmap(lambda rows_here, slot_here: rows_here[slot_here])(expert_out, slot_ids)
    moe_out = lax.optimization_barrier(jnp.sum(picked * gates.reshape(block_total, TOK_DEV, TOPK, 1), axis=2)).reshape(sequence_length, D)
    return residual + moe_out

def adamw(master, first_moment, second_moment, gradient, rate, decay):
    moment_new = 0.9 * first_moment + 0.1 * gradient
    square_new = 0.95 * second_moment + 0.05 * gradient * gradient
    corrected = moment_new / (1.0 - 0.9 ** STEP) / (jnp.sqrt(square_new / (1.0 - 0.95 ** STEP)) + 1e-08)
    master_new = master - rate * (corrected + decay * master)
    return (master_new, moment_new, square_new, master_new.astype(jnp.bfloat16))

def reference(block_input, out_cotangent, block_ids, expert_routes, norm_gains, gains_first, gains_second, joint_weight, joint_first, joint_second, output_weight, output_first, output_second, router_weight, router_first, router_second, expert_weight, expert_first, expert_second):

    def forward(tokens, gain_rows, joint_matrix, output_matrix, router_matrix, expert_matrix):
        gains_low = low(gain_rows)
        joint_low = low(joint_matrix)
        output_low = low(output_matrix)
        router_low = low(router_matrix)
        expert_low = low(expert_matrix)

        def one_sequence(carried, inputs):
            result_rows = sequence_rows(inputs[0], inputs[1], inputs[2], gains_low, joint_low, output_low, router_low, expert_low)
            return (carried, result_rows)
        unused, results = lax.scan(jax.checkpoint(one_sequence), jnp.zeros((), jnp.float32), (tokens, block_ids, expert_routes))
        return results
    tokens = block_input.astype(jnp.float32)
    results, pullback = jax.vjp(forward, tokens, norm_gains, joint_weight, output_weight, router_weight, expert_weight)
    input_grad, gains_grad, joint_grad, output_grad, router_grad, expert_grad = pullback(out_cotangent.astype(jnp.float32))
    gains_new = adamw(norm_gains, gains_first, gains_second, gains_grad, 0.6, 0.0)
    joint_new = adamw(joint_weight, joint_first, joint_second, joint_grad, 0.03, 0.1)
    output_new = adamw(output_weight, output_first, output_second, output_grad, 0.25, 0.1)
    router_new = adamw(router_weight, router_first, router_second, router_grad, 0.015, 0.1)
    expert_rate = jnp.array([0.03, 0.03, 0.25], jnp.float32).reshape(1, 1, 3, 1)
    expert_new = adamw(expert_weight, expert_first, expert_second, expert_grad, expert_rate, 0.1)
    return (results.astype(jnp.bfloat16), input_grad, gains_new[0], gains_new[1], gains_new[2], gains_new[3], joint_new[0], joint_new[1], joint_new[2], joint_new[3], output_new[0], output_new[1], output_new[2], output_new[3], router_new[0], router_new[1], router_new[2], router_new[3], expert_new[0], expert_new[1], expert_new[2][:, :, 0:2], expert_new[2][:, :, 2], expert_new[3])
```

```python
import functools
import math

import jax
import jax.numpy as jnp
from jax import lax
from jax.experimental import pallas as pl
from jax.experimental.pallas import tpu as pltpu
from jax.sharding import PartitionSpec as P

QUERY_HEADS = 24
KEY_VALUE_HEADS = 8
HEAD_SIZE = 64
GROUP = QUERY_HEADS // KEY_VALUE_HEADS
E = 16
STEP = 10
SPAN = 256
LANES = 128
BF = jnp.bfloat16
F32 = jnp.float32
NT = (((1,), (1,)), ((), ()))
TN = (((0,), (0,)), ((), ()))
VMEM_LIMIT = 58 * 1024 * 1024


def params(**more):
    return pltpu.CompilerParams(vmem_limit_bytes=VMEM_LIMIT, **more)


def inverse_rms(rows):
    return lax.rsqrt(jnp.mean(rows * rows, axis=-1, keepdims=True) + 1e-06)


def half_turn(x, inverse):
    lane = lax.broadcasted_iota(jnp.int32, x.shape, 1)
    first = (lane % HEAD_SIZE) < HEAD_SIZE // 2
    later = pltpu.roll(x, LANES - HEAD_SIZE // 2, 1)
    sooner = pltpu.roll(x, HEAD_SIZE // 2, 1)
    return jnp.where(first, later, -sooner) if inverse else jnp.where(first, -later, sooner)


def project_kernel(x_ref, gain_ref, w_ref, cos_ref, sin_ref, n_ref, q_ref, k_ref, v_ref):
    x = x_ref[...].astype(F32)
    n = (x * inverse_rms(x) * gain_ref[...]).astype(BF)
    n_ref[...] = n
    c = jnp.dot(n, w_ref[:, LANES:], preferred_element_type=F32)
    cos, sin = cos_ref[...], sin_ref[...]
    a = c[:, :LANES]
    b = c[:, LANES : 2 * LANES]
    a = a * cos + half_turn(a, False) * sin
    b = b * cos + half_turn(b, False) * sin
    scale = 1.0 / math.sqrt(HEAD_SIZE)
    a = a.astype(BF) * jnp.asarray(scale, BF)
    q_ref[0] = a[:, :HEAD_SIZE]
    q_ref[1] = a[:, HEAD_SIZE:]
    b = b.astype(BF)
    q_ref[2] = b[:, :HEAD_SIZE] * jnp.asarray(scale, BF)
    k_ref[...] = b[:, HEAD_SIZE:]
    v_ref[...] = c[:, 2 * LANES :].astype(BF)


def project(x, gain, w, cos, sin):
    rows, width = x.shape
    tile = 512
    row = lambda n: pl.BlockSpec((tile, n), lambda i: (i, 0))
    whole = lambda s: pl.BlockSpec(s, lambda i: (0, 0))
    return pl.pallas_call(
        project_kernel,
        grid=(rows // tile,),
        in_specs=[row(width), whole(gain.shape), whole(w.shape), row(LANES), row(LANES)],
        out_specs=[
            row(width),
            pl.BlockSpec((GROUP, tile, HEAD_SIZE), lambda i: (0, i, 0)),
            row(HEAD_SIZE),
            row(HEAD_SIZE),
        ],
        out_shape=[
            jax.ShapeDtypeStruct((rows, width), BF),
            jax.ShapeDtypeStruct((GROUP, rows, HEAD_SIZE), BF),
            jax.ShapeDtypeStruct((rows, HEAD_SIZE), BF),
            jax.ShapeDtypeStruct((rows, HEAD_SIZE), BF),
        ],
        compiler_params=params(),
        cost_estimate=pl.CostEstimate(
            flops=2 * rows * width * w.shape[1], bytes_accessed=rows * width * 4, transcendentals=0
        ),
    )(x, gain, w, cos, sin)


def to_row(column, eye):
    return jnp.sum(jnp.where(eye, column, 0.0), axis=0, keepdims=True)


def to_column(row, eye):
    return jnp.sum(jnp.where(eye, row, 0.0), axis=1, keepdims=True)


def identity_mask():
    return lax.broadcasted_iota(jnp.int32, (SPAN, SPAN), 0) == lax.broadcasted_iota(
        jnp.int32, (SPAN, SPAN), 1
    )


def attend_kernel(idc_ref, idr_ref, q_ref, k_ref, v_ref, o_ref, lse_ref, s_ref, m_ref, l_ref, a_ref):
    i = pl.program_id(0)
    blocks = pl.num_programs(0)
    q = q_ref[...].reshape(GROUP * SPAN, HEAD_SIZE)
    m_ref[...] = jnp.full(m_ref.shape, -1e30, F32)
    l_ref[...] = jnp.zeros(l_ref.shape, F32)
    a_ref[...] = jnp.zeros(a_ref.shape, F32)

    def place(block):
        return pl.ds(pl.multiple_of(block * SPAN, SPAN), SPAN)

    def score(block, masked):
        at = place(block)
        s = lax.dot_general(k_ref[at, :], q, NT, preferred_element_type=F32)
        if masked:
            seen = (idc_ref[at, :] <= idr_ref[...]).astype(F32)
            s = jnp.where(jnp.concatenate([seen] * GROUP, axis=1) > 0.5, s, -1e30)
        s_ref[at, :] = s
        m_ref[...] = jnp.maximum(m_ref[...], jnp.max(s, axis=0, keepdims=True))

    def weigh(block):
        at = place(block)
        p = jnp.exp(s_ref[at, :] - m_ref[...])
        l_ref[...] += jnp.sum(p, axis=0, keepdims=True)
        a_ref[...] += lax.dot_general(p.astype(BF), v_ref[at, :], TN, preferred_element_type=F32)

    def open_score(block, carried):
        score(block, False)
        return carried

    def open_weigh(block, carried):
        weigh(block)
        return carried

    lax.fori_loop(0, i, open_score, 0)
    score(i, True)

    @pl.when(i + 1 < blocks)
    def _():
        score(i + 1, True)

    lax.fori_loop(0, jnp.minimum(i + 2, blocks), open_weigh, 0)

    total = l_ref[...]
    lse = m_ref[...] + jnp.log(total)
    eye = identity_mask()
    for g in range(GROUP):
        part = slice(g * SPAN, (g + 1) * SPAN)
        out = a_ref[part, :] / to_column(total[:, part], eye)
        o_ref[:, g * HEAD_SIZE : (g + 1) * HEAD_SIZE] = out.astype(BF)
        lse_ref[g] = lse[:, part]


def attend(id_column, id_row, q, k, v):
    rows = k.shape[0]
    whole = lambda s: pl.BlockSpec(s, lambda i: (0,) * len(s))
    return pl.pallas_call(
        attend_kernel,
        grid=(rows // SPAN,),
        in_specs=[
            whole(id_column.shape),
            pl.BlockSpec((1, SPAN), lambda i: (0, i)),
            pl.BlockSpec((GROUP, SPAN, HEAD_SIZE), lambda i: (0, i, 0)),
            whole(k.shape),
            whole(v.shape),
        ],
        out_specs=[
            pl.BlockSpec((SPAN, GROUP * HEAD_SIZE), lambda i: (i, 0)),
            pl.BlockSpec((GROUP, 1, SPAN), lambda i: (0, 0, i)),
        ],
        out_shape=[
            jax.ShapeDtypeStruct((rows, GROUP * HEAD_SIZE), BF),
            jax.ShapeDtypeStruct((GROUP, 1, rows), F32),
        ],
        scratch_shapes=[
            pltpu.VMEM((rows, GROUP * SPAN), F32),
            pltpu.VMEM((1, GROUP * SPAN), F32),
            pltpu.VMEM((1, GROUP * SPAN), F32),
            pltpu.VMEM((GROUP * SPAN, HEAD_SIZE), F32),
        ],
        compiler_params=params(),
        cost_estimate=pl.CostEstimate(
            flops=20 * 1000**3, bytes_accessed=6 * rows * 256, transcendentals=rows * rows
        ),
    )(id_column, id_row, q, k, v)


def attend_back_kernel(
    idc_ref, idr_ref, q_ref, k_ref, v_ref, o_ref, do_ref, lse_ref, dq_ref, dk_ref, dv_ref, a_ref
):
    i = pl.program_id(0)
    blocks = pl.num_programs(0)

    @pl.when(i == 0)
    def _():
        dk_ref[...] = jnp.zeros(dk_ref.shape, F32)
        dv_ref[...] = jnp.zeros(dv_ref.shape, F32)

    q = q_ref[...].reshape(GROUP * SPAN, HEAD_SIZE)
    eye = identity_mask()
    grads, deltas = [], []
    for g in range(GROUP):
        lanes = slice(g * HEAD_SIZE, (g + 1) * HEAD_SIZE)
        part = do_ref[:, lanes]
        grads.append(part)
        product = part.astype(F32) * o_ref[:, lanes].astype(F32)
        deltas.append(to_row(jnp.sum(product, axis=1, keepdims=True), eye))
    do = jnp.concatenate(grads, axis=0)
    delta = jnp.concatenate(deltas, axis=1)
    lse = jnp.concatenate([lse_ref[g] for g in range(GROUP)], axis=1)
    a_ref[...] = jnp.zeros(a_ref.shape, F32)

    def step(block, masked):
        at = pl.ds(pl.multiple_of(block * SPAN, SPAN), SPAN)
        k = k_ref[at, :]
        s = lax.dot_general(k, q, NT, preferred_element_type=F32)
        p = jnp.exp(s - lse)
        if masked:
            seen = idc_ref[at, :] <= idr_ref[...]
            p = jnp.where(jnp.concatenate([seen.astype(F32)] * GROUP, axis=1) > 0.5, p, 0.0)
        dp = lax.dot_general(v_ref[at, :], do, NT, preferred_element_type=F32)
        ds = (p * (dp - delta)).astype(BF)
        dv_ref[at, :] += jnp.dot(p.astype(BF), do, preferred_element_type=F32)
        dk_ref[at, :] += jnp.dot(ds, q, preferred_element_type=F32)
        a_ref[...] += lax.dot_general(ds, k, TN, preferred_element_type=F32)

    def open_step(block, carried):
        step(block, False)
        return carried

    lax.fori_loop(0, i, open_step, 0)
    step(i, True)

    @pl.when(i + 1 < blocks)
    def _():
        step(i + 1, True)

    dq_ref[...] = a_ref[...].reshape(GROUP, SPAN, HEAD_SIZE) * (1.0 / math.sqrt(HEAD_SIZE))


def attend_back(id_column, id_row, q, k, v, o, do, lse):
    rows = k.shape[0]
    whole = lambda s: pl.BlockSpec(s, lambda i: (0,) * len(s))
    heads = pl.BlockSpec((GROUP, SPAN, HEAD_SIZE), lambda i: (0, i, 0))
    flat = pl.BlockSpec((SPAN, GROUP * HEAD_SIZE), lambda i: (i, 0))
    return pl.pallas_call(
        attend_back_kernel,
        grid=(rows // SPAN,),
        in_specs=[
            whole(id_column.shape),
            pl.BlockSpec((1, SPAN), lambda i: (0, i)),
            heads,
            whole(k.shape),
            whole(v.shape),
            flat,
            flat,
            pl.BlockSpec((GROUP, 1, SPAN), lambda i: (0, 0, i)),
        ],
        out_specs=[heads, whole(k.shape), whole(v.shape)],
        out_shape=[
            jax.ShapeDtypeStruct((GROUP, rows, HEAD_SIZE), F32),
            jax.ShapeDtypeStruct(k.shape, F32),
            jax.ShapeDtypeStruct(v.shape, F32),
        ],
        scratch_shapes=[pltpu.VMEM((GROUP * SPAN, HEAD_SIZE), F32)],
        compiler_params=params(),
        cost_estimate=pl.CostEstimate(
            flops=40 * 1000**3, bytes_accessed=12 * rows * 256, transcendentals=rows * rows
        ),
    )(id_column, id_row, q, k, v, o, do, lse)


def turn_back_kernel(dq_ref, dk_ref, dv_ref, cos_ref, sin_ref, out_ref):
    cos, sin = cos_ref[...], sin_ref[...]
    a = jnp.concatenate([dq_ref[0], dq_ref[1]], axis=1)
    b = jnp.concatenate([dq_ref[2], dk_ref[...]], axis=1)
    out_ref[:, :LANES] = (a * cos + half_turn(a, True) * sin).astype(BF)
    out_ref[:, LANES : 2 * LANES] = (b * cos + half_turn(b, True) * sin).astype(BF)
    out_ref[:, 2 * LANES :] = dv_ref[...].astype(BF)


def turn_back(dq, dk, dv, cos, sin):
    rows = dk.shape[0]
    tile = 512
    row = lambda n: pl.BlockSpec((tile, n), lambda i: (i, 0))
    columns = (GROUP + 2) * HEAD_SIZE
    return pl.pallas_call(
        turn_back_kernel,
        grid=(rows // tile,),
        in_specs=[
            pl.BlockSpec((GROUP, tile, HEAD_SIZE), lambda i: (0, i, 0)),
            row(HEAD_SIZE),
            row(HEAD_SIZE),
            row(LANES),
            row(LANES),
        ],
        out_specs=row(columns),
        out_shape=jax.ShapeDtypeStruct((rows, columns), BF),
        compiler_params=params(),
    )(dq, dk, dv, cos, sin)


def expert_kernel(count, at_ref, x_ref, c_ref, r_ref, w_ref, pre_ref, wh_ref, out_ref, grad_ref):
    width = x_ref.shape[1]
    hidden_columns = wh_ref.shape[1]
    units = hidden_columns // count
    x = x_ref[...]
    cot = c_ref[:, :width]
    named = c_ref[:, width:].astype(F32) > 0.5
    logits = jnp.where(named, jnp.dot(x, r_ref[...], preferred_element_type=F32), -1e30)
    top = jnp.max(logits, axis=1, keepdims=True)
    exponent = jnp.where(named, jnp.exp(logits - top), 0.0)
    gates = exponent / jnp.sum(exponent, axis=1, keepdims=True)
    lane = lax.broadcasted_iota(jnp.int32, gates.shape, 1)
    first = at_ref[0]
    found = jnp.zeros(gates.shape, F32)
    for e in range(count):
        cols = slice(e * units, (e + 1) * units)
        up_cols = slice(hidden_columns + e * units, hidden_columns + (e + 1) * units)
        down_cols = slice(2 * hidden_columns + e * units, 2 * hidden_columns + (e + 1) * units)
        mine = lane == first + e
        gate_here = jnp.sum(jnp.where(mine, gates, 0.0), axis=1, keepdims=True)
        g = jnp.dot(x, w_ref[:, cols], preferred_element_type=F32)
        u = jnp.dot(x, w_ref[:, up_cols], preferred_element_type=F32)
        hg = jnp.dot(cot, w_ref[:, down_cols], preferred_element_type=F32)
        s = 1.0 / (1.0 + jnp.exp(-g))
        gs = g * s
        h = (gs * u).astype(BF).astype(F32)
        found = found + jnp.where(mine, jnp.sum(h * hg, axis=1, keepdims=True), 0.0)
        wh_ref[:, cols] = (h * gate_here).astype(BF)
        hg = hg * gate_here
        pre_ref[:, cols] = (hg * u * s * (1.0 + g * (1.0 - s))).astype(BF)
        pre_ref[:, up_cols] = (hg * gs).astype(BF)
    grad_ref[:, width:] = found.astype(BF)
    grad_ref[:, :width] = lax.dot_general(
        pre_ref[...], w_ref[:, : 2 * hidden_columns], NT, preferred_element_type=F32
    ).astype(BF)
    out_ref[...] = lax.dot_general(
        wh_ref[...], w_ref[:, 2 * hidden_columns :], NT, preferred_element_type=F32
    ).astype(BF)


def experts(first, x, c, router, w, count):
    rows, width = x.shape
    tile = 256
    hidden_columns = w.shape[1] // 3
    row = lambda n: pl.BlockSpec((tile, n), lambda i: (i, 0))
    whole = lambda s: pl.BlockSpec(s, lambda i: (0, 0), pipeline_mode=pl.Buffered(1))
    return pl.pallas_call(
        functools.partial(expert_kernel, count),
        grid=(rows // tile,),
        in_specs=[
            pl.BlockSpec(memory_space=pltpu.SMEM),
            row(width),
            row(c.shape[1]),
            whole(router.shape),
            whole(w.shape),
        ],
        out_specs=[row(2 * hidden_columns), row(hidden_columns), row(width), row(c.shape[1])],
        out_shape=[
            jax.ShapeDtypeStruct((rows, 2 * hidden_columns), BF),
            jax.ShapeDtypeStruct((rows, hidden_columns), BF),
            jax.ShapeDtypeStruct((rows, width), BF),
            jax.ShapeDtypeStruct((rows, c.shape[1]), BF),
        ],
        compiler_params=params(),
        cost_estimate=pl.CostEstimate(
            flops=4 * rows * width * w.shape[1],
            bytes_accessed=2 * w.size + rows * 20000,
            transcendentals=rows * hidden_columns,
        ),
    )(first, x, c, router, w)


def adamw(master, first_moment, second_moment, gradient, rate, decay):
    moment_new = 0.9 * first_moment + 0.1 * gradient
    square_new = 0.95 * second_moment + 0.05 * gradient * gradient
    corrected = moment_new / (1.0 - 0.9**STEP) / (jnp.sqrt(square_new / (1.0 - 0.95**STEP)) + 1e-08)
    master_new = master - rate * (corrected + decay * master)
    return (master_new, moment_new, square_new, master_new.astype(BF))


def expert_adamw_kernel(rate, parts, chained, joined, *refs):
    p_ref, f_ref, s_ref, g_ref = refs[:4]
    master_ref, moment_ref, rounded_ref, square_ref = refs[-4:]
    each = E // parts
    pack = max(1, 8 // each)
    for at in range(0, parts, pack):
        rows = slice(at * each, (at + pack) * each)
        grad = jnp.concatenate([g_ref[k].astype(F32) for k in range(at, at + pack)], axis=1)
        new = adamw(p_ref[:, 0, rows], f_ref[:, 0, rows], s_ref[:, 0, rows], grad, rate, 0.1)
        master_ref[:, 0, rows] = new[0]
        moment_ref[:, 0, rows] = new[1]
        rounded_ref[:, 0, rows] = new[3]
        if joined:
            square_ref[:, rows, 0] = refs[4][:, rows]
            square_ref[:, rows, 1] = new[2]
        else:
            square_ref[:, rows] = new[2]


def expert_adamw(slot, rate, weight, first, second, gradient, earlier, joined=None):
    rows, _, count, units = weight.shape
    parts = gradient.shape[0]
    tile = next(t for t in (32, 16, 8) if rows % t == 0)
    here = pl.BlockSpec((tile, 1, count, units), lambda i: (i, slot, 0, 0))
    plain = pl.BlockSpec((tile, count, units), lambda i: (i, 0, 0))
    pair = pl.BlockSpec((tile, count, 2, units), lambda i: (i, 0, 0, 0))
    shape = jax.ShapeDtypeStruct(weight.shape, F32)
    chained = len(earlier)
    more = [] if joined is None else [joined]
    square = (rows, count, units) if joined is None else (rows, count, 2, units)
    return pl.pallas_call(
        functools.partial(expert_adamw_kernel, rate, parts, chained, joined is not None),
        grid=(rows // tile,),
        in_specs=[here, here, here]
        + [pl.BlockSpec((parts, tile, count // parts, units), lambda i: (0, i, 0, 0))]
        + [plain] * len(more)
        + [pl.BlockSpec(memory_space=pl.ANY)] * chained,
        out_specs=[here, here, here, plain if joined is None else pair],
        out_shape=[
            shape,
            shape,
            jax.ShapeDtypeStruct(weight.shape, BF),
            jax.ShapeDtypeStruct(square, F32),
        ],
        input_output_aliases={4 + len(more) + k: k for k in range(chained)},
        compiler_params=params(),
        cost_estimate=pl.CostEstimate(
            flops=20 * rows * count * units,
            bytes_accessed=28 * rows * count * units,
            transcendentals=rows * count * units,
        ),
    )(weight, first, second, gradient, *more, *earlier)


def local(
    sizes,
    block_input,
    out_cotangent,
    block_ids,
    expert_routes,
    norm_gains,
    gains_first,
    gains_second,
    joint_weight,
    joint_first,
    joint_second,
    output_weight,
    output_first,
    output_second,
    router_weight,
    router_first,
    router_second,
    expert_weight,
    expert_first,
    expert_second,
):
    n_fsdp, n_ctx, n_tp = sizes
    z = lax.axis_index("ctx")
    t = lax.axis_index("tp")
    f = lax.axis_index("fsdp")
    tokens_low = block_input[0]
    cot_low = out_cotangent[0]
    count, width = tokens_low.shape
    half = count // n_tp
    length = n_ctx * count
    tokens = tokens_low.astype(F32)
    cotangent = cot_low.astype(F32)
    own_rows = width // n_fsdp
    each = E // n_ctx

    barrier = lax.optimization_barrier

    def beyond(x, m):
        return lax.ppermute(x, "ctx", [(i, i ^ m) for i in range(n_ctx)])

    def swap(x):
        return lax.ppermute(x, "tp", [(0, 1), (1, 0)])

    def across(x, m):
        return lax.ppermute(x, "fsdp", [(i, i ^ m) for i in range(n_fsdp)])

    def mine(x):
        return lax.dynamic_slice_in_dim(x, t * half, half, 0)

    def other(x):
        return lax.dynamic_slice_in_dim(x, (1 - t) * half, half, 0)

    def in_order(a, b):
        return jnp.where(t == 0, jnp.concatenate([a, b], 0), jnp.concatenate([b, a], 0))

    def put(buffer, x, row):
        return lax.dynamic_update_slice_in_dim(buffer, x, row, 0)

    def take(x, row, rows):
        return lax.dynamic_slice_in_dim(x, row, rows, 0)

    def gather_fsdp(x):
        if n_fsdp != 4:
            full = lax.all_gather(x, "fsdp", axis=0, tiled=True)
            return full, full
        rows = x.shape[0]
        cut = rows // 2
        a, b = across(x, 1), across(x, 2)
        c, d = across(a[:cut], 2), across(b[cut:], 1)
        full = jnp.zeros((n_fsdp * rows, x.shape[1]), x.dtype)
        full = put(full, x, f * rows)
        full = put(full, a, (f ^ 1) * rows)
        full = put(full, b, (f ^ 2) * rows)
        full = put(full, c, (f ^ 3) * rows)
        return put(full, d, (f ^ 3) * rows + cut), c

    def scatter_fsdp(x, axis):
        if n_fsdp != 4:
            return lax.psum_scatter(x, "fsdp", scatter_dimension=axis, tiled=True)
        piece = lambda k: lax.dynamic_slice_in_dim(x, k * own_rows, own_rows, axis)
        total = piece(f).astype(F32)
        for m in (3, 1, 2):
            total = total + across(piece(f ^ m), m).astype(F32)
        return total.astype(BF)

    def spread(x):
        one, two = beyond(x, 1), beyond(x, 2)
        return {1: one, 2: two, 3: beyond(two, 1)}

    joint_columns = joint_weight.shape[1]
    group_columns = (GROUP + 2) * HEAD_SIZE
    joint_low = joint_weight.astype(BF)
    first_pack = jnp.concatenate(
        [
            router_weight.astype(BF),
            norm_gains.T.astype(BF),
            jnp.zeros((own_rows, LANES - E - 2), BF),
            lax.dynamic_slice_in_dim(joint_low, z * group_columns, group_columns, 1),
        ],
        axis=1,
    )
    first_full, first_came = gather_fsdp(first_pack)
    small_full = first_full[:, :LANES]
    router_full = small_full[:, :E]
    router_wide = jnp.where(jnp.arange(LANES)[None, :] < E, small_full, jnp.zeros((), BF))
    gain_first = small_full[:, E].astype(F32)[None, :]
    gain_second = small_full[:, E + 1].astype(F32)[None, :]

    tokens_came = spread(mine(tokens_low))
    sequence = put(jnp.zeros((length, width), BF), tokens_low, z * count)
    for m in (1, 2, 3):
        base = (z ^ m) * count
        sequence = put(sequence, tokens_came[m], base + t * half)
        sequence = put(sequence, swap(tokens_came[m]), base + (1 - t) * half)

    slots_first = jnp.transpose(expert_weight, (0, 2, 1, 3))
    units = expert_weight.shape[3]
    output_low, _ = barrier((output_weight.astype(BF), first_came))
    output_full, output_came = gather_fsdp(output_low)
    expert_part = (
        lax.dynamic_slice_in_dim(slots_first, z * each, each, 2)
        .astype(BF)
        .reshape(own_rows, 3 * each * units)
    )
    expert_part, _ = barrier((expert_part, output_came))
    expert_full = lax.all_gather(expert_part, "fsdp", axis=0, tiled=True)
    joint_late, _ = barrier((joint_low, expert_full))
    joint_full, _ = gather_fsdp(joint_late)
    output_turned = barrier(output_full.T)
    joint_turned = barrier(joint_full.T)

    route_rows = expert_routes[0]
    member = jnp.sum(
        (route_rows[:, :, None] == jnp.arange(LANES, dtype=jnp.int32)[None, None, :]).astype(F32),
        axis=1,
    )
    cot_pack = jnp.concatenate([cot_low, member.astype(BF)], axis=1)
    cot_half, _ = barrier((mine(cot_pack), tokens_came[3]))
    cot_came = spread(cot_half)

    positions = jnp.arange(length, dtype=jnp.int32).astype(F32)
    lanes = jnp.arange(LANES, dtype=jnp.int32) % (HEAD_SIZE // 2)
    frequency = jnp.exp(lanes.astype(F32) * (-2.0 * math.log(10000.0) / HEAD_SIZE))
    angles = positions[:, None] * frequency[None, :]
    cosine, sine = jnp.cos(angles), jnp.sin(angles)
    id_row = block_ids
    id_column = block_ids.reshape(length, 1)
    normed_all, queries, keys, values = project(sequence, gain_first, first_full, cosine, sine)
    attended_all, lse = attend(id_column, id_row, queries, keys, values)
    head_columns = GROUP * HEAD_SIZE

    def to_positions(x):
        parts = [take(x, (z ^ m) * count, count) for m in range(n_ctx)]
        return [parts[0]] + [beyond(parts[m], m) for m in range(1, n_ctx)]

    def by_heads(turned, columns):
        return [take(turned, (z ^ m) * columns, columns) for m in range(n_ctx)]

    output_by = by_heads(output_turned, head_columns)
    attended = to_positions(attended_all)
    attn_part = sum(
        jnp.dot(a, w, preferred_element_type=F32) for a, w in zip(attended, output_by)
    )
    attn_part, cot_came = barrier((attn_part, cot_came))
    residual = tokens + (attn_part + swap(attn_part))
    inv_second = inverse_rms(residual)
    normed_second = (residual * inv_second * gain_second).astype(BF)

    normed_half = mine(normed_second)
    came = spread(normed_half)
    first_expert = jnp.reshape(z * each, (1,)).astype(jnp.int32)
    x_chunks, cot_chunks, pre_chunks, hidden_chunks, outs = {}, {}, {}, {}, {}
    grad_sum = None
    for m in range(n_ctx):
        if m == 0:
            x_chunks[0] = jnp.concatenate([normed_half, other(normed_second)], axis=0)
            cot_chunks[0] = jnp.concatenate([mine(cot_pack), other(cot_pack)], axis=0)
        else:
            got, pre_chunks[m - 1] = barrier((came[m], pre_chunks[m - 1]))
            x_chunks[m] = jnp.concatenate([got, swap(got)], axis=0)
            cot_chunks[m] = jnp.concatenate([cot_came[m], swap(cot_came[m])], axis=0)
        pre_chunks[m], hidden_chunks[m], out_part, grad_part = experts(
            first_expert, x_chunks[m], cot_chunks[m], router_wide, expert_full, each
        )
        grad_here = grad_part[:half].astype(F32) + swap(grad_part[half:]).astype(F32)
        outs[m] = out_part[:half].astype(F32) + swap(out_part[half:]).astype(F32)
        if m == 0:
            grad_sum = grad_here
        else:
            grad_sum = grad_sum + beyond(grad_here.astype(BF), m).astype(F32)
    grad_low = grad_sum.astype(BF)
    grad_rows = in_order(grad_low, swap(grad_low)).astype(F32)
    moe_input = grad_rows[:, :width]
    gate_grads = grad_rows[:, width : width + E]

    x_all = jnp.concatenate([x_chunks[m] for m in range(n_ctx)], axis=0)
    cot_all = jnp.concatenate([cot_chunks[m][:, :width] for m in range(n_ctx)], axis=0)
    pre_all = jnp.concatenate([pre_chunks[m] for m in range(n_ctx)], axis=0)
    hidden_all = jnp.concatenate([hidden_chunks[m] for m in range(n_ctx)], axis=0)
    wide = each * units
    terms = {
        2: lax.dot_general(cot_all, hidden_all, TN, preferred_element_type=F32),
        0: lax.dot_general(x_all, pre_all[:, :wide], TN, preferred_element_type=F32),
        1: lax.dot_general(x_all, pre_all[:, wide:], TN, preferred_element_type=F32),
    }
    expert_sums = {}
    for j in (2, 0, 1):
        owned = scatter_fsdp(terms[j].astype(BF), 0).reshape(own_rows, each, units)
        expert_sums[j] = lax.all_gather(owned, "ctx", axis=0, tiled=False)

    named = member[:, :E]
    logits = jnp.dot(normed_second, router_full, preferred_element_type=F32)
    masked = jnp.where(named > 0.5, logits, -1e30)
    exponent = jnp.where(
        named > 0.5, jnp.exp(masked - jnp.max(masked, axis=1, keepdims=True)), 0.0
    )
    gates = exponent / jnp.sum(exponent, axis=1, keepdims=True)
    logit_grads = (
        gates * (gate_grads - jnp.sum(gates * gate_grads, axis=1, keepdims=True))
    ).astype(BF)
    norm_second_grads = moe_input + lax.dot_general(
        logit_grads, router_full, NT, preferred_element_type=F32
    )
    scaled_second = gain_second * norm_second_grads
    cube_second = inv_second * inv_second * inv_second / width
    residual_grads = (
        cotangent
        + inv_second * scaled_second
        - residual * cube_second * jnp.sum(scaled_second * residual, axis=1, keepdims=True)
    )
    gain_second_grad = jnp.sum(norm_second_grads * residual * inv_second, axis=0, keepdims=True)
    residual_low = residual_grads.astype(BF)

    attended_grads_all = jnp.zeros((length, head_columns), BF)
    for m in range(n_ctx):
        part = lax.dot_general(
            residual_low, output_by[m], NT, preferred_element_type=F32
        ).astype(BF)
        got = part if m == 0 else beyond(part, m)
        attended_grads_all = put(attended_grads_all, got, (z ^ m) * count)
    dq, dk, dv = attend_back(
        id_column, id_row, queries, keys, values, attended_all, attended_grads_all, lse
    )
    joint_grads_all = turn_back(dq, dk, dv, cosine, sine)
    joint_grads = to_positions(joint_grads_all)
    first_part = sum(
        jnp.dot(g, w, preferred_element_type=F32)
        for g, w in zip(joint_grads, by_heads(joint_turned, group_columns))
    ).astype(BF)
    norm_first_grads = first_part.astype(F32) + swap(first_part).astype(F32)
    inv_first = inverse_rms(tokens)
    scaled_first = gain_first * norm_first_grads
    cube_first = inv_first * inv_first * inv_first / width
    input_rows = (
        residual_grads
        + inv_first * scaled_first
        - tokens * cube_first * jnp.sum(scaled_first * tokens, axis=1, keepdims=True)
    )
    gain_first_grad = jnp.sum(norm_first_grads * tokens * inv_first, axis=0, keepdims=True)

    late = [outs[m].astype(BF) for m in range(1, n_ctx)]
    late, attended_grads_all = barrier((late, attended_grads_all))
    moe_two = late[1].astype(F32) + beyond(late[2], 1).astype(F32)
    moe_sum = (
        outs[0] + beyond(late[0], 1).astype(F32) + beyond(moe_two.astype(BF), 2).astype(F32)
    )
    moe_low = moe_sum.astype(BF)
    moe_rows = in_order(moe_low, swap(moe_low)).astype(F32)
    block_output = (residual + moe_rows).astype(BF)[None]

    joint_term = lax.dot_general(joint_grads_all, normed_all, TN, preferred_element_type=F32)
    joint_owned = scatter_fsdp(joint_term.astype(BF), 1)
    joint_sum = jnp.zeros((n_ctx * group_columns, own_rows), BF)
    for m, got in {0: joint_owned, **spread(joint_owned)}.items():
        joint_sum = put(joint_sum, got, (z ^ m) * group_columns)
    joint_sum = joint_sum.T.astype(F32)

    def summed_over_ctx(owned):
        part = owned.shape[0] // n_ctx
        total = take(owned, z * part, part).astype(F32)
        for m in range(1, n_ctx):
            total = total + beyond(take(owned, (z ^ m) * part, part), m).astype(F32)
        total = total.astype(BF)
        full = put(jnp.zeros(owned.shape, BF), total, z * part)
        for m, got in spread(total).items():
            full = put(full, got, (z ^ m) * part)
        return full

    output_columns = output_weight.shape[1]
    rest_term = jnp.zeros((output_columns + 64, width), BF)
    for m in range(n_ctx):
        term = lax.dot_general(attended[m], residual_low, TN, preferred_element_type=F32)
        rest_term = put(rest_term, term.astype(BF), (z ^ m) * head_columns)
    router_term = lax.dot_general(logit_grads, normed_second, TN, preferred_element_type=F32)
    few_rows = jnp.concatenate(
        [router_term, gain_second_grad, jnp.zeros((64 - E - 1, width), F32)], axis=0
    )
    rest_term = put(rest_term, few_rows.astype(BF), output_columns)
    rest_full = summed_over_ctx(scatter_fsdp(rest_term, 1))
    output_sum = rest_full[:output_columns].T.astype(F32)
    router_sum = rest_full[output_columns : output_columns + E].T.astype(F32)
    last_term = jnp.concatenate([gain_first_grad, jnp.zeros((15, width), F32)], axis=0)
    last_owned = scatter_fsdp(last_term.astype(BF), 1)
    last_sum = last_owned.astype(F32)
    for m in range(1, n_ctx):
        last_sum = last_sum + beyond(last_owned, m).astype(F32)
    gains_sum = jnp.concatenate(
        [
            last_sum[:1],
            rest_full[output_columns + E : output_columns + E + 1].astype(F32),
        ],
        axis=0,
    )

    gains_new = adamw(norm_gains, gains_first, gains_second, gains_sum, 0.6, 0.0)
    joint_new = adamw(joint_weight, joint_first, joint_second, joint_sum, 0.03, 0.1)
    output_new = adamw(output_weight, output_first, output_second, output_sum, 0.25, 0.1)
    router_new = adamw(router_weight, router_first, router_second, router_sum, 0.015, 0.1)

    first_view = jnp.transpose(expert_first, (0, 2, 1, 3))
    second_view = jnp.transpose(expert_second, (0, 2, 1, 3))
    made = ()
    squares = {}
    for j in (2, 0, 1):
        *made, squares[j] = expert_adamw(
            j,
            0.25 if j == 2 else 0.03,
            slots_first,
            first_view,
            second_view,
            expert_sums[j],
            tuple(made),
            squares[0] if j == 1 else None,
        )
    back = lambda x: jnp.transpose(x, (0, 2, 1, 3))
    return (
        block_output,
        input_rows[None],
        *gains_new,
        *joint_new,
        *output_new,
        *router_new,
        back(made[0]),
        back(made[1]),
        squares[1],
        squares[2],
        back(made[2]),
    )


def solution(mesh):
    rows = P("fsdp", "ctx", None)
    gains = P(None, "fsdp")
    matrix = P("fsdp", "tp")
    router = P("fsdp", None)
    expert = P("fsdp", None, None, "tp")
    sizes = (mesh.shape["fsdp"], mesh.shape["ctx"], mesh.shape["tp"])
    return jax.shard_map(
        functools.partial(local, sizes),
        mesh=mesh,
        in_specs=(rows, rows, P("fsdp", None), rows)
        + (gains,) * 3
        + (matrix,) * 6
        + (router,) * 3
        + (expert,) * 3,
        out_specs=(rows, rows)
        + (gains,) * 4
        + (matrix,) * 8
        + (router,) * 4
        + (expert, expert, expert, P("fsdp", None, "tp"), expert),
        check_vma=False,
    )
```

```python
import functools
import math

import jax
import jax.numpy as jnp
from jax import lax
from jax.experimental import pallas as pl
from jax.experimental.pallas import tpu as pltpu
from jax.sharding import PartitionSpec as P

QUERY_HEADS = 24
KEY_VALUE_HEADS = 8
HEAD_SIZE = 64
GROUP = QUERY_HEADS // KEY_VALUE_HEADS
E = 16
STEP = 10
SPAN = 256
LANES = 128
BF = jnp.bfloat16
F32 = jnp.float32
NT = (((1,), (1,)), ((), ()))
TN = (((0,), (0,)), ((), ()))
VMEM_LIMIT = 58 * 1024 * 1024
LIGHT = pl.CostEstimate(flops=10**9, bytes_accessed=10**6, transcendentals=0)
MESH = pl.DeviceIdType.MESH


def params(**more):
    return pltpu.CompilerParams(vmem_limit_bytes=VMEM_LIMIT, **more)


def inverse_rms(rows):
    return lax.rsqrt(jnp.mean(rows * rows, axis=-1, keepdims=True) + 1e-06)


def half_turn(x, inverse):
    lane = lax.broadcasted_iota(jnp.int32, x.shape, 1)
    first = (lane % HEAD_SIZE) < HEAD_SIZE // 2
    later = pltpu.roll(x, LANES - HEAD_SIZE // 2, 1)
    sooner = pltpu.roll(x, HEAD_SIZE // 2, 1)
    return jnp.where(first, later, -sooner) if inverse else jnp.where(first, -later, sooner)


def first_gather_kernel(weights, tok_ref, pack_ref, seq_ref, full_ref, local, send, recv):
    z, t, f = lax.axis_index("ctx"), lax.axis_index("tp"), lax.axis_index("fsdp")
    half = tok_ref.shape[0] // 2
    rows = pack_ref.shape[0]
    z1, z2, z3 = z + 1 - 2 * (z % 2), (z + 2) % 4, 3 - z
    near, far, core = {"ctx": z1}, {"ctx": z2}, {"tp": 1 - t}
    partners = [near, far, core]
    if weights:
        f1, f2 = f + 1 - 2 * (f % 2), (f + 2) % 4
        f3 = 3 - f
        partners += [{"fsdp": f1}, {"fsdp": f2}]
    barrier = pltpu.get_barrier_semaphore()
    for partner in partners:
        pl.semaphore_signal(barrier, inc=1, device_id=partner, device_id_type=MESH)
    pl.semaphore_wait(barrier, len(partners))

    def at(chunk, side):
        return seq_ref.at[pl.ds(pl.multiple_of((chunk * 2 + side) * half, half), half)]

    def held(owner, first, size):
        start = pl.multiple_of(owner * rows + first, 8)
        return full_ref.at[pl.ds(start, size)]

    def copy(k, source, target, device):
        made = pltpu.make_async_remote_copy(
            src_ref=source,
            dst_ref=target,
            send_sem=send.at[k],
            recv_sem=recv.at[k],
            device_id=device,
            device_id_type=MESH,
        )
        made.start()
        return made

    own_half = tok_ref.at[pl.ds(pl.multiple_of(t * half, half), half)]
    one = copy(0, own_half, at(z, t), near)
    two = copy(1, own_half, at(z, t), far)
    here = pltpu.make_async_copy(
        tok_ref, seq_ref.at[pl.ds(pl.multiple_of(z * 2 * half, half), 2 * half)], local.at[0]
    )
    here.start()
    sent = [one, two]
    came = []
    if weights:
        cut = rows // 2
        pack_one = copy(6, pack_ref, held(f, 0, rows), {"fsdp": f1})
        pack_two = copy(7, pack_ref, held(f, 0, rows), {"fsdp": f2})
        pack_here = pltpu.make_async_copy(pack_ref, held(f, 0, rows), local.at[1])
        pack_here.start()
        sent += [pack_one, pack_two]
    one.wait_recv()
    swap_one = copy(2, at(z1, t), at(z1, t), core)
    if weights:
        pack_one.wait_recv()
        on_one = copy(8, held(f1, 0, cut), held(f1, 0, cut), {"fsdp": f2})
        pack_two.wait_recv()
        on_two = copy(9, held(f2, cut, rows - cut), held(f2, cut, rows - cut), {"fsdp": f1})
        sent += [on_one, on_two]
        came += [on_one, on_two]
    two.wait_recv()
    three = copy(4, at(z2, t), at(z2, t), near)
    swap_two = copy(3, at(z2, t), at(z2, t), core)
    three.wait_recv()
    swap_three = copy(5, at(z3, t), at(z3, t), core)
    sent += [swap_one, three, swap_two, swap_three]
    for made in came + [swap_one, swap_two, swap_three]:
        made.wait_recv()
    for made in sent:
        made.wait_send()
    here.wait()
    if weights:
        pack_here.wait()


def first_gather(n_ctx, n_fsdp, tokens, pack):
    count, width = tokens.shape
    rows, columns = pack.shape
    weights = n_fsdp == 4
    sequence, full = pl.pallas_call(
        functools.partial(first_gather_kernel, weights),
        in_specs=[pl.BlockSpec(memory_space=pl.ANY)] * 2,
        out_specs=[pl.BlockSpec(memory_space=pl.ANY)] * 2,
        out_shape=[
            jax.ShapeDtypeStruct((n_ctx * count, width), tokens.dtype),
            jax.ShapeDtypeStruct((n_fsdp * rows if weights else rows, columns), pack.dtype),
        ],
        scratch_shapes=[
            pltpu.SemaphoreType.DMA((2,)),
            pltpu.SemaphoreType.DMA((10,)),
            pltpu.SemaphoreType.DMA((10,)),
        ],
        compiler_params=pltpu.CompilerParams(collective_id=0, has_side_effects=True),
        cost_estimate=LIGHT,
    )(tokens, pack)
    if not weights:
        full = lax.all_gather(pack, "fsdp", axis=0, tiled=True)
    return sequence, full


def project_kernel(x_ref, gain_ref, w_ref, cos_ref, sin_ref, n_ref, q_ref, k_ref, v_ref):
    x = x_ref[...].astype(F32)
    n = (x * inverse_rms(x) * gain_ref[...]).astype(BF)
    n_ref[...] = n
    c = jnp.dot(n, w_ref[:, LANES:], preferred_element_type=F32)
    cos, sin = cos_ref[...], sin_ref[...]
    a = c[:, :LANES]
    b = c[:, LANES : 2 * LANES]
    a = a * cos + half_turn(a, False) * sin
    b = b * cos + half_turn(b, False) * sin
    scale = 1.0 / math.sqrt(HEAD_SIZE)
    a = a.astype(BF) * jnp.asarray(scale, BF)
    q_ref[0] = a[:, :HEAD_SIZE]
    q_ref[1] = a[:, HEAD_SIZE:]
    b = b.astype(BF)
    q_ref[2] = b[:, :HEAD_SIZE] * jnp.asarray(scale, BF)
    k_ref[...] = b[:, HEAD_SIZE:]
    v_ref[...] = c[:, 2 * LANES :].astype(BF)


def project(x, gain, w, cos, sin):
    rows, width = x.shape
    tile = 512
    row = lambda n: pl.BlockSpec((tile, n), lambda i: (i, 0))
    whole = lambda s: pl.BlockSpec(s, lambda i: (0, 0))
    return pl.pallas_call(
        project_kernel,
        grid=(rows // tile,),
        in_specs=[row(width), whole(gain.shape), whole(w.shape), row(LANES), row(LANES)],
        out_specs=[
            row(width),
            pl.BlockSpec((GROUP, tile, HEAD_SIZE), lambda i: (0, i, 0)),
            row(HEAD_SIZE),
            row(HEAD_SIZE),
        ],
        out_shape=[
            jax.ShapeDtypeStruct((rows, width), BF),
            jax.ShapeDtypeStruct((GROUP, rows, HEAD_SIZE), BF),
            jax.ShapeDtypeStruct((rows, HEAD_SIZE), BF),
            jax.ShapeDtypeStruct((rows, HEAD_SIZE), BF),
        ],
        compiler_params=params(),
        cost_estimate=LIGHT,
    )(x, gain, w, cos, sin)


def to_row(column, eye):
    return jnp.sum(jnp.where(eye, column, 0.0), axis=0, keepdims=True)


def to_column(row, eye):
    return jnp.sum(jnp.where(eye, row, 0.0), axis=1, keepdims=True)


def identity_mask():
    return lax.broadcasted_iota(jnp.int32, (SPAN, SPAN), 0) == lax.broadcasted_iota(
        jnp.int32, (SPAN, SPAN), 1
    )


def attend_kernel(idc_ref, idr_ref, q_ref, k_ref, v_ref, o_ref, lse_ref, s_ref, m_ref, l_ref, a_ref):
    i = pl.program_id(0)
    blocks = pl.num_programs(0)
    q = q_ref[...].reshape(GROUP * SPAN, HEAD_SIZE)
    m_ref[...] = jnp.full(m_ref.shape, -1e30, F32)
    l_ref[...] = jnp.zeros(l_ref.shape, F32)
    a_ref[...] = jnp.zeros(a_ref.shape, F32)

    def place(block):
        return pl.ds(pl.multiple_of(block * SPAN, SPAN), SPAN)

    def score(block, masked):
        at = place(block)
        s = lax.dot_general(k_ref[at, :], q, NT, preferred_element_type=F32)
        if masked:
            seen = (idc_ref[at, :] <= idr_ref[...]).astype(F32)
            s = jnp.where(jnp.concatenate([seen] * GROUP, axis=1) > 0.5, s, -1e30)
        s_ref[at, :] = s
        m_ref[...] = jnp.maximum(m_ref[...], jnp.max(s, axis=0, keepdims=True))

    def weigh(block):
        at = place(block)
        p = jnp.exp(s_ref[at, :] - m_ref[...])
        l_ref[...] += jnp.sum(p, axis=0, keepdims=True)
        a_ref[...] += lax.dot_general(p.astype(BF), v_ref[at, :], TN, preferred_element_type=F32)

    def open_score(block, carried):
        score(block, False)
        return carried

    def open_weigh(block, carried):
        weigh(block)
        return carried

    lax.fori_loop(0, i, open_score, 0)
    score(i, True)

    @pl.when(i + 1 < blocks)
    def _():
        score(i + 1, True)

    lax.fori_loop(0, jnp.minimum(i + 2, blocks), open_weigh, 0)

    total = l_ref[...]
    lse = m_ref[...] + jnp.log(total)
    eye = identity_mask()
    for g in range(GROUP):
        part = slice(g * SPAN, (g + 1) * SPAN)
        out = a_ref[part, :] / to_column(total[:, part], eye)
        o_ref[:, g * HEAD_SIZE : (g + 1) * HEAD_SIZE] = out.astype(BF)
        lse_ref[g] = lse[:, part]


def attend(id_column, id_row, q, k, v):
    rows = k.shape[0]
    whole = lambda s: pl.BlockSpec(s, lambda i: (0,) * len(s))
    return pl.pallas_call(
        attend_kernel,
        grid=(rows // SPAN,),
        in_specs=[
            whole(id_column.shape),
            pl.BlockSpec((1, SPAN), lambda i: (0, i)),
            pl.BlockSpec((GROUP, SPAN, HEAD_SIZE), lambda i: (0, i, 0)),
            whole(k.shape),
            whole(v.shape),
        ],
        out_specs=[
            pl.BlockSpec((SPAN, GROUP * HEAD_SIZE), lambda i: (i, 0)),
            pl.BlockSpec((GROUP, 1, SPAN), lambda i: (0, 0, i)),
        ],
        out_shape=[
            jax.ShapeDtypeStruct((rows, GROUP * HEAD_SIZE), BF),
            jax.ShapeDtypeStruct((GROUP, 1, rows), F32),
        ],
        scratch_shapes=[
            pltpu.VMEM((rows, GROUP * SPAN), F32),
            pltpu.VMEM((1, GROUP * SPAN), F32),
            pltpu.VMEM((1, GROUP * SPAN), F32),
            pltpu.VMEM((GROUP * SPAN, HEAD_SIZE), F32),
        ],
        compiler_params=params(),
        cost_estimate=LIGHT,
    )(id_column, id_row, q, k, v)


def attend_back_kernel(
    idc_ref, idr_ref, q_ref, k_ref, v_ref, o_ref, do_ref, lse_ref, dq_ref, dk_ref, dv_ref, a_ref
):
    i = pl.program_id(0)
    blocks = pl.num_programs(0)

    @pl.when(i == 0)
    def _():
        dk_ref[...] = jnp.zeros(dk_ref.shape, F32)
        dv_ref[...] = jnp.zeros(dv_ref.shape, F32)

    q = q_ref[...].reshape(GROUP * SPAN, HEAD_SIZE)
    eye = identity_mask()
    grads, deltas = [], []
    for g in range(GROUP):
        lanes = slice(g * HEAD_SIZE, (g + 1) * HEAD_SIZE)
        part = do_ref[:, lanes]
        grads.append(part)
        product = part.astype(F32) * o_ref[:, lanes].astype(F32)
        deltas.append(to_row(jnp.sum(product, axis=1, keepdims=True), eye))
    do = jnp.concatenate(grads, axis=0)
    delta = jnp.concatenate(deltas, axis=1)
    lse = jnp.concatenate([lse_ref[g] for g in range(GROUP)], axis=1)
    a_ref[...] = jnp.zeros(a_ref.shape, F32)

    def step(block, masked):
        at = pl.ds(pl.multiple_of(block * SPAN, SPAN), SPAN)
        k = k_ref[at, :]
        s = lax.dot_general(k, q, NT, preferred_element_type=F32)
        p = jnp.exp(s - lse)
        if masked:
            seen = idc_ref[at, :] <= idr_ref[...]
            p = jnp.where(jnp.concatenate([seen.astype(F32)] * GROUP, axis=1) > 0.5, p, 0.0)
        dp = lax.dot_general(v_ref[at, :], do, NT, preferred_element_type=F32)
        ds = (p * (dp - delta)).astype(BF)
        dv_ref[at, :] += jnp.dot(p.astype(BF), do, preferred_element_type=F32)
        dk_ref[at, :] += jnp.dot(ds, q, preferred_element_type=F32)
        a_ref[...] += lax.dot_general(ds, k, TN, preferred_element_type=F32)

    def open_step(block, carried):
        step(block, False)
        return carried

    lax.fori_loop(0, i, open_step, 0)
    step(i, True)

    @pl.when(i + 1 < blocks)
    def _():
        step(i + 1, True)

    dq_ref[...] = a_ref[...].reshape(GROUP, SPAN, HEAD_SIZE) * (1.0 / math.sqrt(HEAD_SIZE))


def attend_back(id_column, id_row, q, k, v, o, do, lse):
    rows = k.shape[0]
    whole = lambda s: pl.BlockSpec(s, lambda i: (0,) * len(s))
    heads = pl.BlockSpec((GROUP, SPAN, HEAD_SIZE), lambda i: (0, i, 0))
    flat = pl.BlockSpec((SPAN, GROUP * HEAD_SIZE), lambda i: (i, 0))
    return pl.pallas_call(
        attend_back_kernel,
        grid=(rows // SPAN,),
        in_specs=[
            whole(id_column.shape),
            pl.BlockSpec((1, SPAN), lambda i: (0, i)),
            heads,
            whole(k.shape),
            whole(v.shape),
            flat,
            flat,
            pl.BlockSpec((GROUP, 1, SPAN), lambda i: (0, 0, i)),
        ],
        out_specs=[heads, whole(k.shape), whole(v.shape)],
        out_shape=[
            jax.ShapeDtypeStruct((GROUP, rows, HEAD_SIZE), F32),
            jax.ShapeDtypeStruct(k.shape, F32),
            jax.ShapeDtypeStruct(v.shape, F32),
        ],
        scratch_shapes=[pltpu.VMEM((GROUP * SPAN, HEAD_SIZE), F32)],
        compiler_params=params(),
        cost_estimate=LIGHT,
    )(id_column, id_row, q, k, v, o, do, lse)


def turn_back_kernel(dq_ref, dk_ref, dv_ref, cos_ref, sin_ref, out_ref):
    cos, sin = cos_ref[...], sin_ref[...]
    a = jnp.concatenate([dq_ref[0], dq_ref[1]], axis=1)
    b = jnp.concatenate([dq_ref[2], dk_ref[...]], axis=1)
    out_ref[:, :LANES] = (a * cos + half_turn(a, True) * sin).astype(BF)
    out_ref[:, LANES : 2 * LANES] = (b * cos + half_turn(b, True) * sin).astype(BF)
    out_ref[:, 2 * LANES :] = dv_ref[...].astype(BF)


def turn_back(dq, dk, dv, cos, sin):
    rows = dk.shape[0]
    tile = 512
    row = lambda n: pl.BlockSpec((tile, n), lambda i: (i, 0))
    columns = (GROUP + 2) * HEAD_SIZE
    return pl.pallas_call(
        turn_back_kernel,
        grid=(rows // tile,),
        in_specs=[
            pl.BlockSpec((GROUP, tile, HEAD_SIZE), lambda i: (0, i, 0)),
            row(HEAD_SIZE),
            row(HEAD_SIZE),
            row(LANES),
            row(LANES),
        ],
        out_specs=row(columns),
        out_shape=jax.ShapeDtypeStruct((rows, columns), BF),
        compiler_params=params(),
    )(dq, dk, dv, cos, sin)


def expert_kernel(count, pieces, n_ref, cot_ref, one_ref, two_ref, r_ref, w_any, *refs):
    pre_ref, wh_ref, out_ref = refs[:3]
    x_parts, cot_parts = refs[3 : 3 + pieces], refs[3 + pieces : 3 + 2 * pieces]
    grad_any = refs[3 + 2 * pieces]
    x_ref, c_ref, w_ref, part_ref, there_ref, sum_ref, back_ref, full_ref = refs[4 + 2 * pieces : -4]
    local, wrote, send, recv = refs[-4:]
    i = pl.program_id(0)
    z, t, f = lax.axis_index("ctx"), lax.axis_index("tp"), lax.axis_index("fsdp")
    z1, z2, z3 = z + 1 - 2 * (z % 2), (z + 2) % 4, 3 - z
    near, far, third, core = {"ctx": z1}, {"ctx": z2}, {"ctx": z3}, {"tp": 1 - t}
    half, width = x_ref.shape[1:]
    piece = width // pieces
    hidden_columns = wh_ref.shape[1]
    units = hidden_columns // count

    def rows(side):
        return pl.ds(pl.multiple_of(side * half, half), half)

    def remote(k, source, target, device):
        return pltpu.make_async_remote_copy(
            src_ref=source,
            dst_ref=target,
            send_sem=send.at[k],
            recv_sem=recv.at[k],
            device_id=device,
            device_id_type=MESH,
        )

    own = n_ref.at[rows(t)]
    x_one = remote(0, own, x_ref.at[2], near)
    x_two = remote(1, own, x_ref.at[4], far)
    x_three = remote(2, x_ref.at[4], x_ref.at[6], near)
    c_three = remote(3, two_ref, c_ref.at[6], near)
    x_swaps = [None] + [remote(3 + m, x_ref.at[2 * m], x_ref.at[2 * m + 1], core) for m in (1, 2, 3)]
    c_swaps = [
        None,
        remote(7, one_ref, c_ref.at[3], core),
        remote(8, two_ref, c_ref.at[5], core),
        remote(9, c_ref.at[6], c_ref.at[7], core),
    ]
    crossed = [remote(10 + m, part_ref.at[2 * m + 1], there_ref.at[m], core) for m in range(4)]
    returned = [None] + [
        remote(13 + m, sum_ref.at[m], back_ref.at[m], device)
        for m, device in ((1, near), (2, far), (3, third))
    ]
    last = remote(17, full_ref.at[rows(t)], full_ref.at[rows(t)], core)
    loads = [
        pltpu.make_async_copy(source, target, local.at[k])
        for k, (source, target) in enumerate(
            (
                (n_ref.at[rows(t)], x_ref.at[0]),
                (n_ref.at[rows(1 - t)], x_ref.at[1]),
                (cot_ref.at[rows(t)], c_ref.at[0]),
                (cot_ref.at[rows(1 - t)], c_ref.at[1]),
                (w_any, w_ref),
                (one_ref, c_ref.at[2]),
                (two_ref, c_ref.at[4]),
            )
        )
    ]
    store = pltpu.make_async_copy(full_ref, grad_any, local.at[7])

    def keep(step):
        made = []
        at_rows = pl.ds(pl.multiple_of(step * half, half), half)
        for k in range(pieces):
            owner = [f, f + 1 - 2 * (f % 2), (f + 2) % 4, 3 - f][k] if pieces > 1 else 0
            at = pl.ds(pl.multiple_of(owner * piece, piece), piece)
            for n, (source, target) in enumerate(((x_ref, x_parts[k]), (c_ref, cot_parts[k]))):
                made.append(
                    pltpu.make_async_copy(
                        source.at[step, :, at], target.at[at_rows], wrote.at[step, 2 * k + n]
                    )
                )
        return made

    def finish(m):
        crossed[m].wait_recv()
        sum_ref[m] = (part_ref[2 * m].astype(F32) + there_ref[m].astype(F32)).astype(BF)
        if m:
            returned[m].start()

    @pl.when(i == 0)
    def _():
        barrier = pltpu.get_barrier_semaphore()
        for partner in (near, far, third, core):
            pl.semaphore_signal(barrier, inc=1, device_id=partner, device_id_type=MESH)
        pl.semaphore_wait(barrier, 4)
        for made in [x_one, x_two] + loads + [c_swaps[1], c_swaps[2], c_three]:
            made.start()
        for made in (loads[0], loads[2], loads[4]):
            made.wait()

    @pl.when(i == 1)
    def _():
        loads[1].wait()
        loads[3].wait()

    @pl.when(i == 2)
    def _():
        x_one.wait_recv()
        x_swaps[1].start()
        loads[5].wait()

    @pl.when(i == 3)
    def _():
        x_swaps[1].wait_recv()
        c_swaps[1].wait_recv()

    @pl.when(i == 4)
    def _():
        x_two.wait_recv()
        x_three.start()
        x_swaps[2].start()
        loads[6].wait()

    @pl.when(i == 5)
    def _():
        x_swaps[2].wait_recv()
        c_swaps[2].wait_recv()

    @pl.when(i == 6)
    def _():
        c_three.wait_recv()
        c_swaps[3].start()
        x_three.wait_recv()
        x_swaps[3].start()

    @pl.when(i == 7)
    def _():
        x_swaps[3].wait_recv()
        c_swaps[3].wait_recv()

    for made in keep(i):
        made.start()

    def columns(j, e):
        return slice(j * hidden_columns + e * units, j * hidden_columns + (e + 1) * units)

    x = x_ref[i]
    both = c_ref[i]
    cot = both[:, :width]
    named = both[:, width:].astype(F32) > 0.5
    logits = jnp.where(named, jnp.dot(x, r_ref[...], preferred_element_type=F32), -1e30)
    top = jnp.max(logits, axis=1, keepdims=True)
    exponent = jnp.where(named, jnp.exp(logits - top), 0.0)
    gates = exponent / jnp.sum(exponent, axis=1, keepdims=True)
    lane = lax.broadcasted_iota(jnp.int32, gates.shape, 1)
    found = jnp.zeros(gates.shape, F32)
    for e in range(count):
        mine = lane == z * count + e
        gate_here = jnp.sum(jnp.where(mine, gates, 0.0), axis=1, keepdims=True)
        g = jnp.dot(x, w_ref[:, columns(0, e)], preferred_element_type=F32)
        u = jnp.dot(x, w_ref[:, columns(1, e)], preferred_element_type=F32)
        hg = jnp.dot(cot, w_ref[:, columns(2, e)], preferred_element_type=F32)
        s = 1.0 / (1.0 + jnp.exp(-g))
        gs = g * s
        h = (gs * u).astype(BF).astype(F32)
        found = found + jnp.where(mine, jnp.sum(h * hg, axis=1, keepdims=True), 0.0)
        wh_ref[:, columns(0, e)] = (h * gate_here).astype(BF)
        hg = hg * gate_here
        pre_ref[:, columns(0, e)] = (hg * u * s * (1.0 + g * (1.0 - s))).astype(BF)
        pre_ref[:, columns(1, e)] = (hg * gs).astype(BF)
    part_ref[i, :, width:] = found.astype(BF)
    part_ref[i, :, :width] = lax.dot_general(
        pre_ref[...], w_ref[:, : 2 * hidden_columns], NT, preferred_element_type=F32
    ).astype(BF)
    for m in range(4):

        @pl.when(i == 2 * m + 1)
        def _():
            crossed[m].start()

    out_ref[...] = lax.dot_general(
        wh_ref[...], w_ref[:, 2 * hidden_columns :], NT, preferred_element_type=F32
    ).astype(BF)
    for m in range(3):

        @pl.when(i == 2 * m + 2)
        def _():
            finish(m)

    @pl.when(i == 7)
    def _():
        finish(3)
        total = sum_ref[0].astype(F32)
        for m in (1, 2, 3):
            returned[m].wait_recv()
            total = total + back_ref[m].astype(F32)
        full_ref[rows(t), :] = total.astype(BF)
        last.start()
        for made in [x_one, x_two, x_three, c_three] + x_swaps[1:] + c_swaps[1:] + crossed:
            made.wait_send()
        for made in returned[1:]:
            made.wait_send()
        last.wait_send()
        last.wait_recv()
        store.start()

        def settle(step, carried):
            for made in keep(step):
                made.wait()
            return carried

        lax.fori_loop(0, 8, settle, 0)
        store.wait()


def experts(pieces, normed, cot, one, two, router, w, count):
    rows, width = normed.shape
    half = rows // 2
    packed = cot.shape[1]
    hidden_columns = w.shape[1] // 3
    slot = lambda n: pl.BlockSpec((half, n), lambda i: (i, 0))
    anywhere = pl.BlockSpec(memory_space=pl.ANY)
    blocks = [2 * hidden_columns, hidden_columns, width]
    return pl.pallas_call(
        functools.partial(expert_kernel, count, pieces),
        grid=(8,),
        in_specs=[anywhere] * 4 + [pl.BlockSpec(router.shape, lambda i: (0, 0)), anywhere],
        out_specs=[slot(n) for n in blocks] + [anywhere] * (2 * pieces + 1),
        out_shape=[
            jax.ShapeDtypeStruct((8 * half, n), BF) for n in blocks + [width // pieces] * (2 * pieces)
        ]
        + [jax.ShapeDtypeStruct((rows, packed), BF)],
        scratch_shapes=[
            pltpu.VMEM((8, half, width), BF),
            pltpu.VMEM((8, half, packed), BF),
            pltpu.VMEM(w.shape, BF),
            pltpu.VMEM((8, half, packed), BF),
            pltpu.VMEM((4, half, packed), BF),
            pltpu.VMEM((4, half, packed), BF),
            pltpu.VMEM((4, half, packed), BF),
            pltpu.VMEM((rows, packed), BF),
            pltpu.SemaphoreType.DMA((8,)),
            pltpu.SemaphoreType.DMA((8, 2 * pieces)),
            pltpu.SemaphoreType.DMA((18,)),
            pltpu.SemaphoreType.DMA((18,)),
        ],
        compiler_params=params(collective_id=1, has_side_effects=True),
        cost_estimate=LIGHT,
    )(normed, cot, one, two, router, w)


def adamw(master, first_moment, second_moment, gradient, rate, decay):
    moment_new = 0.9 * first_moment + 0.1 * gradient
    square_new = 0.95 * second_moment + 0.05 * gradient * gradient
    corrected = moment_new / (1.0 - 0.9**STEP) / (jnp.sqrt(square_new / (1.0 - 0.95**STEP)) + 1e-08)
    master_new = master - rate * (corrected + decay * master)
    return (master_new, moment_new, square_new, master_new.astype(BF))


def expert_adamw_kernel(rate, joined, *refs):
    p_ref, f_ref, s_ref, g_ref = refs[:4]
    master_ref, moment_ref, rounded_ref, square_ref, grad_ref = refs[-5:]
    parts, _, columns = g_ref.shape
    units = p_ref.shape[3]
    each = columns // units
    for k in range(parts):
        for e in range(each):
            grad_ref[:, k * each + e, :] = g_ref[k, :, e * units : (e + 1) * units].astype(F32)
    for at in range(0, parts * each, 8):
        rows = slice(at, at + 8)
        new = adamw(
            p_ref[:, 0, rows], f_ref[:, 0, rows], s_ref[:, 0, rows], grad_ref[:, rows], rate, 0.1
        )
        master_ref[:, 0, rows] = new[0]
        moment_ref[:, 0, rows] = new[1]
        rounded_ref[:, 0, rows] = new[3]
        if joined:
            square_ref[:, rows, 0] = refs[4][:, rows]
            square_ref[:, rows, 1] = new[2]
        else:
            square_ref[:, rows] = new[2]


def expert_adamw(slot, rate, weight, first, second, gradient, earlier, joined=None):
    rows, _, count, units = weight.shape
    parts = gradient.shape[0]
    tile = next(t for t in (32, 16, 8) if rows % t == 0)
    here = pl.BlockSpec((tile, 1, count, units), lambda i: (i, slot, 0, 0))
    plain = pl.BlockSpec((tile, count, units), lambda i: (i, 0, 0))
    pair = pl.BlockSpec((tile, count, 2, units), lambda i: (i, 0, 0, 0))
    shape = jax.ShapeDtypeStruct(weight.shape, F32)
    chained = len(earlier)
    more = [] if joined is None else [joined]
    square = (rows, count, units) if joined is None else (rows, count, 2, units)
    return pl.pallas_call(
        functools.partial(expert_adamw_kernel, rate, joined is not None),
        grid=(rows // tile,),
        in_specs=[here, here, here]
        + [pl.BlockSpec((parts, tile, gradient.shape[2]), lambda i: (0, i, 0))]
        + [plain] * len(more)
        + [pl.BlockSpec(memory_space=pl.ANY)] * chained,
        out_specs=[here, here, here, plain if joined is None else pair],
        out_shape=[
            shape,
            shape,
            jax.ShapeDtypeStruct(weight.shape, BF),
            jax.ShapeDtypeStruct(square, F32),
        ],
        scratch_shapes=[pltpu.VMEM((tile, count, units), F32)],
        input_output_aliases={4 + len(more) + k: k for k in range(chained)},
        compiler_params=params(),
        cost_estimate=pl.CostEstimate(
            flops=20 * rows * count * units,
            bytes_accessed=45 * rows * count * units,
            transcendentals=rows * count * units,
        ),
    )(weight, first, second, gradient, *more, *earlier)


def matrix_adamw_kernel(rate, p_ref, f_ref, s_ref, g_ref, *outs):
    grad = g_ref[...].astype(F32).T
    new = adamw(p_ref[...], f_ref[...], s_ref[...], grad, rate, 0.1)
    for ref, value in zip(outs, new):
        ref[...] = value


def matrix_adamw(rate, weight, first, second, turned):
    rows, columns = weight.shape
    if rows % LANES:
        return adamw(weight, first, second, turned[:columns].T.astype(F32), rate, 0.1)
    tile = 256
    here = pl.BlockSpec((rows, tile), lambda i: (0, i))
    shape = jax.ShapeDtypeStruct(weight.shape, F32)
    return pl.pallas_call(
        functools.partial(matrix_adamw_kernel, rate),
        grid=(columns // tile,),
        in_specs=[here, here, here, pl.BlockSpec((tile, rows), lambda i: (i, 0))],
        out_specs=[here] * 4,
        out_shape=[shape, shape, shape, jax.ShapeDtypeStruct(weight.shape, BF)],
        compiler_params=params(),
        cost_estimate=pl.CostEstimate(
            flops=20 * rows * columns, bytes_accessed=28 * rows * columns, transcendentals=0
        ),
    )(weight, first, second, turned)


def local(
    sizes,
    block_input,
    out_cotangent,
    block_ids,
    expert_routes,
    norm_gains,
    gains_first,
    gains_second,
    joint_weight,
    joint_first,
    joint_second,
    output_weight,
    output_first,
    output_second,
    router_weight,
    router_first,
    router_second,
    expert_weight,
    expert_first,
    expert_second,
):
    n_fsdp, n_ctx, n_tp = sizes
    z = lax.axis_index("ctx")
    t = lax.axis_index("tp")
    f = lax.axis_index("fsdp")
    tokens_low = block_input[0]
    cot_low = out_cotangent[0]
    count, width = tokens_low.shape
    half = count // n_tp
    length = n_ctx * count
    tokens = tokens_low.astype(F32)
    cotangent = cot_low.astype(F32)
    own_rows = width // n_fsdp
    each = E // n_ctx

    barrier = lax.optimization_barrier

    def beyond(x, m):
        return lax.ppermute(x, "ctx", [(i, i ^ m) for i in range(n_ctx)])

    def swap(x):
        return lax.ppermute(x, "tp", [(0, 1), (1, 0)])

    def across(x, m):
        return lax.ppermute(x, "fsdp", [(i, i ^ m) for i in range(n_fsdp)])

    def mine(x):
        return lax.dynamic_slice_in_dim(x, t * half, half, 0)

    def other(x):
        return lax.dynamic_slice_in_dim(x, (1 - t) * half, half, 0)

    def in_order(a, b):
        return jnp.where(t == 0, jnp.concatenate([a, b], 0), jnp.concatenate([b, a], 0))

    def put(buffer, x, place):
        return lax.dynamic_update_slice_in_dim(buffer, x[None], place, 0)

    def take(x, place, places):
        return lax.dynamic_index_in_dim(
            x.reshape(places, x.shape[0] // places, x.shape[1]), place, 0, keepdims=False
        )

    def scatter_fsdp(x, axis):
        if n_fsdp != 4:
            return lax.psum_scatter(x, "fsdp", scatter_dimension=axis, tiled=True)
        if axis:
            piece = lambda k: lax.dynamic_slice_in_dim(x, k * own_rows, own_rows, 1)
        else:
            piece = lambda k: take(x, k, n_fsdp)
        total = piece(f).astype(F32)
        for m in (3, 1, 2):
            total = total + across(piece(f ^ m), m).astype(F32)
        return total.astype(BF)

    def spread(x):
        one, two = beyond(x, 1), beyond(x, 2)
        return {1: one, 2: two, 3: beyond(two, 1)}

    slots_first = jnp.transpose(expert_weight, (0, 2, 1, 3))
    units = expert_weight.shape[3]
    expert_part = (
        lax.dynamic_slice_in_dim(slots_first, z * each, each, 2)
        .astype(BF)
        .reshape(own_rows, 3 * each * units)
    )
    expert_full = lax.all_gather(expert_part, "fsdp", axis=0, tiled=True)

    group_columns = (GROUP + 2) * HEAD_SIZE
    head_columns = GROUP * HEAD_SIZE
    joint_low = joint_weight.astype(BF)
    output_columns = output_weight.shape[1]
    first_pack = jnp.concatenate(
        [
            router_weight.astype(BF),
            norm_gains.T.astype(BF),
            jnp.zeros((own_rows, LANES - E - 2), BF),
            lax.dynamic_slice_in_dim(joint_low, z * group_columns, group_columns, 1),
        ],
        axis=1,
    )
    first_pack, _ = barrier((first_pack, expert_part))
    sequence, first_full = first_gather(n_ctx, n_fsdp, tokens_low, first_pack)
    small_full = first_full[:, :LANES]
    router_full = small_full[:, :E]
    router_wide = jnp.where(jnp.arange(LANES)[None, :] < E, small_full, jnp.zeros((), BF))
    gain_first = small_full[:, E].astype(F32)[None, :]
    gain_second = small_full[:, E + 1].astype(F32)[None, :]
    output_late, _ = barrier((output_weight.astype(BF), (expert_full, sequence)))
    output_full = lax.all_gather(output_late, "fsdp", axis=0, tiled=True)
    joint_late, _ = barrier((joint_low, output_full))
    joint_full = lax.all_gather(joint_late, "fsdp", axis=0, tiled=True)
    output_turned = barrier(output_full.T)
    joint_turned = barrier(joint_full.T)

    route_rows = expert_routes[0]
    lane_row = jnp.arange(LANES, dtype=jnp.int32)[None, :]
    member = sum((route_rows[:, k : k + 1] == lane_row).astype(F32) for k in range(route_rows.shape[1]))
    cot_pack = jnp.concatenate([cot_low, member.astype(BF)], axis=1)
    cot_half, sequence = barrier((mine(cot_pack), sequence))
    cot_came = [beyond(cot_half, 1), beyond(cot_half, 2)]

    lanes = jnp.arange(LANES, dtype=jnp.int32) % (HEAD_SIZE // 2)
    frequency = jnp.exp(lanes.astype(F32) * (-2.0 * math.log(10000.0) / HEAD_SIZE))
    fine = 64
    small_angles = jnp.arange(fine, dtype=jnp.int32).astype(F32)[:, None] * frequency
    large_angles = (fine * jnp.arange(length // fine, dtype=jnp.int32)).astype(F32)[:, None] * frequency
    cos_a, sin_a = jnp.cos(large_angles)[:, None], jnp.sin(large_angles)[:, None]
    cos_b, sin_b = jnp.cos(small_angles)[None], jnp.sin(small_angles)[None]
    cosine = (cos_a * cos_b - sin_a * sin_b).reshape(length, LANES)
    sine = (sin_a * cos_b + cos_a * sin_b).reshape(length, LANES)
    cosine, sine, tokens_low = barrier((cosine, sine, tokens_low))
    id_row = block_ids
    id_column = block_ids.reshape(length, 1)
    normed_all, queries, keys, values = project(sequence, gain_first, first_full, cosine, sine)
    attended_all, lse = attend(id_column, id_row, queries, keys, values)
    def to_positions(x):
        parts = [take(x, z ^ m, n_ctx) for m in range(n_ctx)]
        return [parts[0]] + [beyond(parts[m], m) for m in range(1, n_ctx)]

    def by_heads(turned):
        return [take(turned, z ^ m, n_ctx) for m in range(n_ctx)]

    output_by = by_heads(output_turned)
    attended = to_positions(attended_all)
    attn_part = sum(
        jnp.dot(a, w, preferred_element_type=F32) for a, w in zip(attended, output_by)
    )
    residual = tokens + (attn_part + swap(attn_part))
    inv_second = inverse_rms(residual)
    normed_second = (residual * inv_second * gain_second).astype(BF)

    pieces = n_fsdp if n_fsdp == 4 else 1
    pre_all, hidden_all, out_all, *kept, grad_rows = experts(
        pieces, normed_second, cot_pack, *cot_came, router_wide, expert_full, each
    )
    x_parts, cot_parts = kept[:pieces], kept[pieces:]

    wide = each * units

    def expert_terms(j):
        left = cot_parts if j == 2 else x_parts
        right = hidden_all if j == 2 else pre_all[:, j * wide : (j + 1) * wide]
        return [
            lax.dot_general(left[k], right, TN, preferred_element_type=F32).astype(BF)
            for k in range(pieces)
        ]

    terms = {j: expert_terms(j) for j in (2, 0, 1)}
    pieces_came = {}
    for j in (2, 0, 1):
        if pieces > 1:
            pieces_came[j] = [terms[j][0]] + [across(terms[j][k], k) for k in range(1, pieces)]
        else:
            pieces_came[j] = lax.psum_scatter(terms[j][0], "fsdp", scatter_dimension=0, tiled=True)

    def gathered(came):
        if pieces > 1:
            came = sum(x.astype(F32) for x in came).astype(BF)
        return lax.all_gather(came, "ctx", axis=0, tiled=False)

    grad_rows, terms[2] = barrier((grad_rows, terms[2]))
    grad_rows = grad_rows.astype(F32)
    moe_input = grad_rows[:, :width]
    gate_grads = grad_rows[:, width : width + E]

    named = member[:, :E]
    logits = jnp.dot(normed_second, router_full, preferred_element_type=F32)
    masked = jnp.where(named > 0.5, logits, -1e30)
    exponent = jnp.where(
        named > 0.5, jnp.exp(masked - jnp.max(masked, axis=1, keepdims=True)), 0.0
    )
    gates = exponent / jnp.sum(exponent, axis=1, keepdims=True)
    logit_grads = (
        gates * (gate_grads - jnp.sum(gates * gate_grads, axis=1, keepdims=True))
    ).astype(BF)
    norm_second_grads = moe_input + lax.dot_general(
        logit_grads, router_full, NT, preferred_element_type=F32
    )
    scaled_second = gain_second * norm_second_grads
    cube_second = inv_second * inv_second * inv_second / width
    residual_grads = (
        cotangent
        + inv_second * scaled_second
        - residual * cube_second * jnp.sum(scaled_second * residual, axis=1, keepdims=True)
    )
    gain_second_grad = jnp.sum(norm_second_grads * residual * inv_second, axis=0, keepdims=True)
    residual_low = residual_grads.astype(BF)

    attended_grads_all = jnp.zeros((n_ctx, count, head_columns), BF)
    for m in range(n_ctx):
        part = lax.dot_general(
            residual_low, output_by[m], NT, preferred_element_type=F32
        ).astype(BF)
        got = part if m == 0 else beyond(part, m)
        attended_grads_all = put(attended_grads_all, got, z ^ m)
    attended_grads_all = attended_grads_all.reshape(length, head_columns)
    attended_grads_all, pieces_came[2], *_ = barrier(
        (attended_grads_all, pieces_came[2], terms[0], terms[1])
    )
    down_sum = gathered(pieces_came[2])
    dq, dk, dv = attend_back(
        id_column, id_row, queries, keys, values, attended_all, attended_grads_all, lse
    )
    joint_grads_all = turn_back(dq, dk, dv, cosine, sine)
    joint_grads = to_positions(joint_grads_all)
    expert_sums = {2: down_sum}
    for j in (0, 1):
        expert_sums[j] = gathered(pieces_came[j])
    first_view = jnp.transpose(expert_first, (0, 2, 1, 3))
    second_view = jnp.transpose(expert_second, (0, 2, 1, 3))
    made = []
    squares = {}

    def expert_step(j, joined=None):
        rate = 0.25 if j == 2 else 0.03
        *made[:], squares[j] = expert_adamw(
            j, rate, slots_first, first_view, second_view, expert_sums[j], tuple(made), joined
        )

    expert_step(2)
    joint_grads, made[:], squares[2] = barrier((joint_grads, made, squares[2]))
    first_part = sum(
        jnp.dot(g, w, preferred_element_type=F32)
        for g, w in zip(joint_grads, by_heads(joint_turned))
    ).astype(BF)
    norm_first_grads = first_part.astype(F32) + swap(first_part).astype(F32)
    inv_first = inverse_rms(tokens)
    scaled_first = gain_first * norm_first_grads
    cube_first = inv_first * inv_first * inv_first / width
    input_rows = (
        residual_grads
        + inv_first * scaled_first
        - tokens * cube_first * jnp.sum(scaled_first * tokens, axis=1, keepdims=True)
    )
    gain_first_grad = jnp.sum(norm_first_grads * tokens * inv_first, axis=0, keepdims=True)

    out_all, attended_grads_all = barrier((out_all, attended_grads_all))
    outs = out_all.reshape(n_ctx, 2, half, width)
    halves = {
        m: outs[m, 0].astype(F32) + swap(outs[m, 1]).astype(F32) for m in range(n_ctx)
    }
    moe_two = halves[2] + beyond(halves[3].astype(BF), 1).astype(F32)
    moe_sum = (
        halves[0]
        + beyond(halves[1].astype(BF), 1).astype(F32)
        + beyond(moe_two.astype(BF), 2).astype(F32)
    )
    moe_low = moe_sum.astype(BF)
    moe_rows = in_order(moe_low, swap(moe_low)).astype(F32)
    block_output = (residual + moe_rows).astype(BF)[None]

    joint_term = lax.dot_general(joint_grads_all, normed_all, TN, preferred_element_type=F32)
    joint_owned = scatter_fsdp(joint_term.astype(BF), 1)
    joint_sum = jnp.zeros((n_ctx, group_columns, own_rows), BF)
    for m, got in {0: joint_owned, **spread(joint_owned)}.items():
        joint_sum = put(joint_sum, got, z ^ m)
    joint_sum = joint_sum.reshape(n_ctx * group_columns, own_rows)

    def summed_over_ctx(owned):
        total = take(owned, z, n_ctx).astype(F32)
        for m in range(1, n_ctx):
            total = total + beyond(take(owned, z ^ m, n_ctx), m).astype(F32)
        total = total.astype(BF)
        full = put(jnp.zeros((n_ctx, *total.shape), BF), total, z)
        for m, got in spread(total).items():
            full = put(full, got, z ^ m)
        return full.reshape(owned.shape)

    step = 64
    blocks = head_columns // step
    rest_term = jnp.zeros((output_columns // step + 1, step, width), BF)
    for m in range(n_ctx):
        term = lax.dot_general(attended[m], residual_low, TN, preferred_element_type=F32)
        rest_term = lax.dynamic_update_slice_in_dim(
            rest_term, term.astype(BF).reshape(blocks, step, width), (z ^ m) * blocks, 0
        )
    router_term = lax.dot_general(logit_grads, normed_second, TN, preferred_element_type=F32)
    few_rows = jnp.concatenate(
        [router_term, gain_second_grad, jnp.zeros((step - E - 1, width), F32)], axis=0
    )
    rest_term = put(rest_term, few_rows.astype(BF), output_columns // step)
    rest_term = rest_term.reshape(output_columns + step, width)
    rest_full = summed_over_ctx(scatter_fsdp(rest_term, 1))
    router_sum = rest_full[output_columns : output_columns + E].T.astype(F32)
    last_term = jnp.concatenate([gain_first_grad, jnp.zeros((15, width), F32)], axis=0)
    last_owned = scatter_fsdp(last_term.astype(BF), 1)
    last_came = [last_owned] + [beyond(last_owned, m) for m in range(1, n_ctx)]
    expert_step(0)
    last_came, made[:], squares[0] = barrier((last_came, made, squares[0]))
    last_sum = sum(x.astype(F32) for x in last_came)
    gains_sum = jnp.concatenate(
        [
            last_sum[:1],
            rest_full[output_columns + E : output_columns + E + 1].astype(F32),
        ],
        axis=0,
    )

    gains_new = adamw(norm_gains, gains_first, gains_second, gains_sum, 0.6, 0.0)
    joint_new = matrix_adamw(0.03, joint_weight, joint_first, joint_second, joint_sum)
    output_new = matrix_adamw(0.25, output_weight, output_first, output_second, rest_full)
    router_new = adamw(router_weight, router_first, router_second, router_sum, 0.015, 0.1)

    expert_step(1, squares[0])
    back = lambda x: jnp.transpose(x, (0, 2, 1, 3))
    return (
        block_output,
        input_rows[None],
        *gains_new,
        *joint_new,
        *output_new,
        *router_new,
        back(made[0]),
        back(made[1]),
        squares[1],
        squares[2],
        back(made[2]),
    )


def solution(mesh):
    rows = P("fsdp", "ctx", None)
    gains = P(None, "fsdp")
    matrix = P("fsdp", "tp")
    router = P("fsdp", None)
    expert = P("fsdp", None, None, "tp")
    sizes = (mesh.shape["fsdp"], mesh.shape["ctx"], mesh.shape["tp"])
    return jax.shard_map(
        functools.partial(local, sizes),
        mesh=mesh,
        in_specs=(rows, rows, P("fsdp", None), rows)
        + (gains,) * 3
        + (matrix,) * 6
        + (router,) * 3
        + (expert,) * 3,
        out_specs=(rows, rows)
        + (gains,) * 4
        + (matrix,) * 8
        + (router,) * 4
        + (expert, expert, expert, P("fsdp", None, "tp"), expert),
        check_vma=False,
    )
```

```python
import functools
import math

import jax
import jax.numpy as jnp
from jax import lax
from jax.experimental import pallas as pl
from jax.experimental.pallas import tpu as pltpu
from jax.sharding import PartitionSpec as P

QUERY_HEADS = 24
KEY_VALUE_HEADS = 8
HEAD_SIZE = 64
GROUP = QUERY_HEADS // KEY_VALUE_HEADS
E = 16
STEP = 10
SPAN = 256
LANES = 128
BF = jnp.bfloat16
F32 = jnp.float32
NT = (((1,), (1,)), ((), ()))
TN = (((0,), (0,)), ((), ()))
VMEM_LIMIT = 58 * 1024 * 1024
LIGHT = pl.CostEstimate(flops=10**9, bytes_accessed=10**6, transcendentals=0)
MESH = pl.DeviceIdType.MESH


def params(**more):
    return pltpu.CompilerParams(vmem_limit_bytes=VMEM_LIMIT, **more)


def inverse_rms(rows):
    return lax.rsqrt(jnp.mean(rows * rows, axis=-1, keepdims=True) + 1e-06)


def half_turn(x, inverse):
    lane = lax.broadcasted_iota(jnp.int32, x.shape, 1)
    first = (lane % HEAD_SIZE) < HEAD_SIZE // 2
    later = pltpu.roll(x, LANES - HEAD_SIZE // 2, 1)
    sooner = pltpu.roll(x, HEAD_SIZE // 2, 1)
    return jnp.where(first, later, -sooner) if inverse else jnp.where(first, -later, sooner)


def first_gather_kernel(weights, tok_ref, pack_ref, seq_ref, full_ref, local, send, recv):
    z, t, f = lax.axis_index("ctx"), lax.axis_index("tp"), lax.axis_index("fsdp")
    half = tok_ref.shape[0] // 2
    rows = pack_ref.shape[0]
    z1, z2, z3 = z + 1 - 2 * (z % 2), (z + 2) % 4, 3 - z
    near, far, core = {"ctx": z1}, {"ctx": z2}, {"tp": 1 - t}
    partners = [near, far, core]
    if weights:
        f1, f2 = f + 1 - 2 * (f % 2), (f + 2) % 4
        f3 = 3 - f
        partners += [{"fsdp": f1}, {"fsdp": f2}]
    barrier = pltpu.get_barrier_semaphore()
    for partner in partners:
        pl.semaphore_signal(barrier, inc=1, device_id=partner, device_id_type=MESH)
    pl.semaphore_wait(barrier, len(partners))

    def at(chunk, side):
        return seq_ref.at[pl.ds(pl.multiple_of((chunk * 2 + side) * half, half), half)]

    def held(owner, first, size):
        start = pl.multiple_of(owner * rows + first, 8)
        return full_ref.at[pl.ds(start, size)]

    def copy(k, source, target, device):
        made = pltpu.make_async_remote_copy(
            src_ref=source,
            dst_ref=target,
            send_sem=send.at[k],
            recv_sem=recv.at[k],
            device_id=device,
            device_id_type=MESH,
        )
        made.start()
        return made

    own_half = tok_ref.at[pl.ds(pl.multiple_of(t * half, half), half)]
    one = copy(0, own_half, at(z, t), near)
    two = copy(1, own_half, at(z, t), far)
    here = pltpu.make_async_copy(
        tok_ref, seq_ref.at[pl.ds(pl.multiple_of(z * 2 * half, half), 2 * half)], local.at[0]
    )
    here.start()
    sent = [one, two]
    came = []
    if weights:
        cut = rows // 2
        pack_one = copy(6, pack_ref, held(f, 0, rows), {"fsdp": f1})
        pack_two = copy(7, pack_ref, held(f, 0, rows), {"fsdp": f2})
        pack_here = pltpu.make_async_copy(pack_ref, held(f, 0, rows), local.at[1])
        pack_here.start()
        sent += [pack_one, pack_two]
    one.wait_recv()
    swap_one = copy(2, at(z1, t), at(z1, t), core)
    if weights:
        pack_one.wait_recv()
        on_one = copy(8, held(f1, 0, cut), held(f1, 0, cut), {"fsdp": f2})
        pack_two.wait_recv()
        on_two = copy(9, held(f2, cut, rows - cut), held(f2, cut, rows - cut), {"fsdp": f1})
        sent += [on_one, on_two]
        came += [on_one, on_two]
    two.wait_recv()
    three = copy(4, at(z2, t), at(z2, t), near)
    swap_two = copy(3, at(z2, t), at(z2, t), core)
    three.wait_recv()
    swap_three = copy(5, at(z3, t), at(z3, t), core)
    sent += [swap_one, three, swap_two, swap_three]
    for made in came + [swap_one, swap_two, swap_three]:
        made.wait_recv()
    for made in sent:
        made.wait_send()
    here.wait()
    if weights:
        pack_here.wait()


def first_gather(n_ctx, n_fsdp, tokens, pack):
    count, width = tokens.shape
    rows, columns = pack.shape
    weights = n_fsdp == 4
    sequence, full = pl.pallas_call(
        functools.partial(first_gather_kernel, weights),
        in_specs=[pl.BlockSpec(memory_space=pl.ANY)] * 2,
        out_specs=[pl.BlockSpec(memory_space=pl.ANY)] * 2,
        out_shape=[
            jax.ShapeDtypeStruct((n_ctx * count, width), tokens.dtype),
            jax.ShapeDtypeStruct((n_fsdp * rows if weights else rows, columns), pack.dtype),
        ],
        scratch_shapes=[
            pltpu.SemaphoreType.DMA((2,)),
            pltpu.SemaphoreType.DMA((10,)),
            pltpu.SemaphoreType.DMA((10,)),
        ],
        compiler_params=pltpu.CompilerParams(collective_id=0, has_side_effects=True),
        cost_estimate=LIGHT,
    )(tokens, pack)
    if not weights:
        full = lax.all_gather(pack, "fsdp", axis=0, tiled=True)
    return sequence, full


def project_kernel(x_ref, gain_ref, w_ref, cos_ref, sin_ref, n_ref, q_ref, k_ref, v_ref):
    x = x_ref[...].astype(F32)
    n = (x * inverse_rms(x) * gain_ref[...]).astype(BF)
    n_ref[...] = n
    c = jnp.dot(n, w_ref[:, LANES:], preferred_element_type=F32)
    cos, sin = cos_ref[...], sin_ref[...]
    a = c[:, :LANES]
    b = c[:, LANES : 2 * LANES]
    a = a * cos + half_turn(a, False) * sin
    b = b * cos + half_turn(b, False) * sin
    scale = 1.0 / math.sqrt(HEAD_SIZE)
    a = a.astype(BF) * jnp.asarray(scale, BF)
    q_ref[0] = a[:, :HEAD_SIZE]
    q_ref[1] = a[:, HEAD_SIZE:]
    b = b.astype(BF)
    q_ref[2] = b[:, :HEAD_SIZE] * jnp.asarray(scale, BF)
    k_ref[...] = b[:, HEAD_SIZE:]
    v_ref[...] = c[:, 2 * LANES :].astype(BF)


def project(x, gain, w, cos, sin):
    rows, width = x.shape
    tile = 512
    row = lambda n: pl.BlockSpec((tile, n), lambda i: (i, 0))
    whole = lambda s: pl.BlockSpec(s, lambda i: (0, 0))
    return pl.pallas_call(
        project_kernel,
        grid=(rows // tile,),
        in_specs=[row(width), whole(gain.shape), whole(w.shape), row(LANES), row(LANES)],
        out_specs=[
            row(width),
            pl.BlockSpec((GROUP, tile, HEAD_SIZE), lambda i: (0, i, 0)),
            row(HEAD_SIZE),
            row(HEAD_SIZE),
        ],
        out_shape=[
            jax.ShapeDtypeStruct((rows, width), BF),
            jax.ShapeDtypeStruct((GROUP, rows, HEAD_SIZE), BF),
            jax.ShapeDtypeStruct((rows, HEAD_SIZE), BF),
            jax.ShapeDtypeStruct((rows, HEAD_SIZE), BF),
        ],
        compiler_params=params(),
        cost_estimate=LIGHT,
    )(x, gain, w, cos, sin)


def to_row(column, eye):
    return jnp.sum(jnp.where(eye, column, 0.0), axis=0, keepdims=True)


def to_column(row, eye):
    return jnp.sum(jnp.where(eye, row, 0.0), axis=1, keepdims=True)


def identity_mask():
    return lax.broadcasted_iota(jnp.int32, (SPAN, SPAN), 0) == lax.broadcasted_iota(
        jnp.int32, (SPAN, SPAN), 1
    )


def attend_kernel(weights, *refs):
    idc_ref, idr_ref, q_ref, k_ref, v_ref, shard_ref, o_ref, lse_ref, att_ref, full_ref = refs[:10]
    s_ref, m_ref, l_ref, a_ref, oall_ref, local, send, recv = refs[10:]
    i = pl.program_id(0)
    blocks = pl.num_programs(0)
    z, f = lax.axis_index("ctx"), lax.axis_index("fsdp")
    rows = shard_ref.shape[0]
    cut = rows // 2
    f1, f2 = f + 1 - 2 * (f % 2), (f + 2) % 4
    f3 = 3 - f

    def remote(k, source, target, device):
        return pltpu.make_async_remote_copy(
            src_ref=source,
            dst_ref=target,
            send_sem=send.at[k],
            recv_sem=recv.at[k],
            device_id=device,
            device_id_type=MESH,
        )

    def held(owner, first, size):
        return full_ref.at[pl.ds(pl.multiple_of(owner * rows + first, 8), size)]

    own_weights = pltpu.make_async_copy(shard_ref, held(f, 0, rows), local.at[1])
    if weights:
        one = remote(4, shard_ref, held(f, 0, rows), {"fsdp": f1})
        two = remote(5, shard_ref, held(f, 0, rows), {"fsdp": f2})
        on_one = remote(6, held(f1, 0, cut), held(f1, 0, cut), {"fsdp": f2})
        on_two = remote(7, held(f2, cut, rows - cut), held(f2, cut, rows - cut), {"fsdp": f1})

    def to(c):
        return pltpu.make_async_remote_copy(
            src_ref=oall_ref.at[pl.ds(2 * c, 2)],
            dst_ref=att_ref.at[pl.ds(2 * z, 2)],
            send_sem=send.at[c],
            recv_sem=recv.at[z],
            device_id={"ctx": c},
            device_id_type=MESH,
        )

    def back_from(c):
        return pltpu.make_async_remote_copy(
            src_ref=oall_ref.at[pl.ds(2 * c, 2)],
            dst_ref=att_ref.at[pl.ds(2 * c, 2)],
            send_sem=send.at[c],
            recv_sem=recv.at[c],
            device_id={"ctx": c},
            device_id_type=MESH,
        )

    own_rows = pltpu.make_async_copy(
        oall_ref.at[pl.ds(2 * z, 2)], att_ref.at[pl.ds(2 * z, 2)], local.at[0]
    )

    @pl.when(i == 0)
    def _():
        barrier = pltpu.get_barrier_semaphore()
        partners = [{"ctx": (z + k) % 4} for k in (1, 2, 3)]
        if weights:
            partners += [{"fsdp": f1}, {"fsdp": f2}]
        for partner in partners:
            pl.semaphore_signal(barrier, inc=1, device_id=partner, device_id_type=MESH)
        pl.semaphore_wait(barrier, len(partners))
        if weights:
            one.start()
            two.start()
            own_weights.start()

    if weights:

        @pl.when(i == 6)
        def _():
            one.wait_recv()
            on_one.start()
            two.wait_recv()
            on_two.start()

    q = q_ref[...].reshape(GROUP * SPAN, HEAD_SIZE)
    m_ref[...] = jnp.full(m_ref.shape, -1e30, F32)
    l_ref[...] = jnp.zeros(l_ref.shape, F32)
    a_ref[...] = jnp.zeros(a_ref.shape, F32)

    def place(block):
        return pl.ds(pl.multiple_of(block * SPAN, SPAN), SPAN)

    def score(block, masked):
        at = place(block)
        s = lax.dot_general(k_ref[at, :], q, NT, preferred_element_type=F32)
        if masked:
            seen = (idc_ref[at, :] <= idr_ref[...]).astype(F32)
            s = jnp.where(jnp.concatenate([seen] * GROUP, axis=1) > 0.5, s, -1e30)
        s_ref[at, :] = s
        m_ref[...] = jnp.maximum(m_ref[...], jnp.max(s, axis=0, keepdims=True))

    def weigh(block):
        at = place(block)
        p = jnp.exp(s_ref[at, :] - m_ref[...])
        l_ref[...] += jnp.sum(p, axis=0, keepdims=True)
        a_ref[...] += lax.dot_general(p.astype(BF), v_ref[at, :], TN, preferred_element_type=F32)

    def open_score(block, carried):
        score(block, False)
        return carried

    def open_weigh(block, carried):
        weigh(block)
        return carried

    lax.fori_loop(0, i, open_score, 0)
    score(i, True)

    @pl.when(i + 1 < blocks)
    def _():
        score(i + 1, True)

    lax.fori_loop(0, jnp.minimum(i + 2, blocks), open_weigh, 0)

    total = l_ref[...]
    lse = m_ref[...] + jnp.log(total)
    eye = identity_mask()
    for g in range(GROUP):
        part = slice(g * SPAN, (g + 1) * SPAN)
        out = a_ref[part, :] / to_column(total[:, part], eye)
        o_ref[:, g * HEAD_SIZE : (g + 1) * HEAD_SIZE] = out.astype(BF)
        oall_ref[i, :, g * HEAD_SIZE : (g + 1) * HEAD_SIZE] = out.astype(BF)
        lse_ref[g] = lse[:, part]
    for c in range(4):

        @pl.when(jnp.logical_and(i == 2 * c + 1, z != c))
        def _():
            to(c).start()

    @pl.when(i == 7)
    def _():
        own_rows.start()
        own_rows.wait()
        if weights:
            on_one.wait_recv()
            on_two.wait_recv()
            for made in (one, two, on_one, on_two):
                made.wait_send()
            own_weights.wait()

    for c in range(4):

        @pl.when(jnp.logical_and(i == 7, z != c))
        def _():
            to(c).wait_send()
            back_from(c).wait_recv()


def attend(n_fsdp, id_column, id_row, q, k, v, shard):
    rows = k.shape[0]
    weights = n_fsdp == 4
    anywhere = pl.BlockSpec(memory_space=pl.ANY)
    full_rows = shard.shape[0] * (n_fsdp if weights else 1)
    whole = lambda s: pl.BlockSpec(s, lambda i: (0,) * len(s))
    return pl.pallas_call(
        functools.partial(attend_kernel, weights),
        grid=(rows // SPAN,),
        in_specs=[
            whole(id_column.shape),
            pl.BlockSpec((1, SPAN), lambda i: (0, i)),
            pl.BlockSpec((GROUP, SPAN, HEAD_SIZE), lambda i: (0, i, 0)),
            whole(k.shape),
            whole(v.shape),
            anywhere,
        ],
        out_specs=[
            pl.BlockSpec((SPAN, GROUP * HEAD_SIZE), lambda i: (i, 0)),
            pl.BlockSpec((GROUP, 1, SPAN), lambda i: (0, 0, i)),
            anywhere,
            anywhere,
        ],
        out_shape=[
            jax.ShapeDtypeStruct((rows, GROUP * HEAD_SIZE), BF),
            jax.ShapeDtypeStruct((GROUP, 1, rows), F32),
            jax.ShapeDtypeStruct((8, SPAN, GROUP * HEAD_SIZE), BF),
            jax.ShapeDtypeStruct((full_rows, shard.shape[1]), BF),
        ],
        scratch_shapes=[
            pltpu.VMEM((rows, GROUP * SPAN), F32),
            pltpu.VMEM((1, GROUP * SPAN), F32),
            pltpu.VMEM((1, GROUP * SPAN), F32),
            pltpu.VMEM((GROUP * SPAN, HEAD_SIZE), F32),
            pltpu.VMEM((8, SPAN, GROUP * HEAD_SIZE), BF),
            pltpu.SemaphoreType.DMA((2,)),
            pltpu.SemaphoreType.DMA((8,)),
            pltpu.SemaphoreType.DMA((8,)),
        ],
        compiler_params=params(collective_id=2, has_side_effects=True),
        cost_estimate=LIGHT,
    )(id_column, id_row, q, k, v, shard)


def attend_back_kernel(
    idc_ref, idr_ref, q_ref, k_ref, v_ref, o_ref, do_ref, lse_ref, dq_ref, dk_ref, dv_ref, a_ref
):
    i = pl.program_id(0)
    blocks = pl.num_programs(0)

    @pl.when(i == 0)
    def _():
        dk_ref[...] = jnp.zeros(dk_ref.shape, F32)
        dv_ref[...] = jnp.zeros(dv_ref.shape, F32)

    q = q_ref[...].reshape(GROUP * SPAN, HEAD_SIZE)
    eye = identity_mask()
    grads, deltas = [], []
    for g in range(GROUP):
        lanes = slice(g * HEAD_SIZE, (g + 1) * HEAD_SIZE)
        part = do_ref[:, lanes]
        grads.append(part)
        product = part.astype(F32) * o_ref[:, lanes].astype(F32)
        deltas.append(to_row(jnp.sum(product, axis=1, keepdims=True), eye))
    do = jnp.concatenate(grads, axis=0)
    delta = jnp.concatenate(deltas, axis=1)
    lse = jnp.concatenate([lse_ref[g] for g in range(GROUP)], axis=1)
    a_ref[...] = jnp.zeros(a_ref.shape, F32)

    def step(block, masked):
        at = pl.ds(pl.multiple_of(block * SPAN, SPAN), SPAN)
        k = k_ref[at, :]
        s = lax.dot_general(k, q, NT, preferred_element_type=F32)
        p = jnp.exp(s - lse)
        if masked:
            seen = idc_ref[at, :] <= idr_ref[...]
            p = jnp.where(jnp.concatenate([seen.astype(F32)] * GROUP, axis=1) > 0.5, p, 0.0)
        dp = lax.dot_general(v_ref[at, :], do, NT, preferred_element_type=F32)
        ds = (p * (dp - delta)).astype(BF)
        dv_ref[at, :] += jnp.dot(p.astype(BF), do, preferred_element_type=F32)
        dk_ref[at, :] += jnp.dot(ds, q, preferred_element_type=F32)
        a_ref[...] += lax.dot_general(ds, k, TN, preferred_element_type=F32)

    def open_step(block, carried):
        step(block, False)
        return carried

    lax.fori_loop(0, i, open_step, 0)
    step(i, True)

    @pl.when(i + 1 < blocks)
    def _():
        step(i + 1, True)

    dq_ref[...] = a_ref[...].reshape(GROUP, SPAN, HEAD_SIZE) * (1.0 / math.sqrt(HEAD_SIZE))


def attend_back(id_column, id_row, q, k, v, o, do, lse):
    rows = k.shape[0]
    whole = lambda s: pl.BlockSpec(s, lambda i: (0,) * len(s))
    heads = pl.BlockSpec((GROUP, SPAN, HEAD_SIZE), lambda i: (0, i, 0))
    flat = pl.BlockSpec((SPAN, GROUP * HEAD_SIZE), lambda i: (i, 0))
    return pl.pallas_call(
        attend_back_kernel,
        grid=(rows // SPAN,),
        in_specs=[
            whole(id_column.shape),
            pl.BlockSpec((1, SPAN), lambda i: (0, i)),
            heads,
            whole(k.shape),
            whole(v.shape),
            flat,
            flat,
            pl.BlockSpec((GROUP, 1, SPAN), lambda i: (0, 0, i)),
        ],
        out_specs=[heads, whole(k.shape), whole(v.shape)],
        out_shape=[
            jax.ShapeDtypeStruct((GROUP, rows, HEAD_SIZE), F32),
            jax.ShapeDtypeStruct(k.shape, F32),
            jax.ShapeDtypeStruct(v.shape, F32),
        ],
        scratch_shapes=[pltpu.VMEM((GROUP * SPAN, HEAD_SIZE), F32)],
        compiler_params=params(),
        cost_estimate=LIGHT,
    )(id_column, id_row, q, k, v, o, do, lse)


def project_out_kernel(att_ref, w_ref, tok_ref, gain_ref, res_ref, n_ref, a_ref, p_ref, o_ref, send, recv):
    t = lax.axis_index("tp")
    core = {"tp": 1 - t}
    barrier = pltpu.get_barrier_semaphore()
    pl.semaphore_signal(barrier, inc=1, device_id=core, device_id_type=MESH)
    pl.semaphore_wait(barrier, 1)
    columns = att_ref.shape[2]
    sent = []
    for side in (0, 1):
        rows = slice(side * SPAN, (side + 1) * SPAN)
        for c in range(4):
            a_ref[rows, c * columns : (c + 1) * columns] = att_ref[2 * c + side]
        p_ref[side] = lax.dot_general(a_ref[rows, :], w_ref[...], NT, preferred_element_type=F32)
        made = pltpu.make_async_remote_copy(
            src_ref=p_ref.at[side],
            dst_ref=o_ref.at[side],
            send_sem=send.at[side],
            recv_sem=recv.at[side],
            device_id=core,
            device_id_type=MESH,
        )
        made.start()
        sent.append(made)
    for side in (0, 1):
        rows = slice(side * SPAN, (side + 1) * SPAN)
        sent[side].wait_recv()
        residual = tok_ref[rows, :].astype(F32) + (p_ref[side] + o_ref[side])
        res_ref[rows, :] = residual
        n_ref[rows, :] = (residual * inverse_rms(residual) * gain_ref[...]).astype(BF)
    for made in sent:
        made.wait_send()


def project_out(att, w, tokens, gain):
    rows, width = tokens.shape
    columns = w.shape[1]
    return pl.pallas_call(
        project_out_kernel,
        in_specs=[pl.BlockSpec(memory_space=pltpu.VMEM)] * 4,
        out_specs=[pl.BlockSpec(memory_space=pltpu.VMEM)] * 3,
        out_shape=[
            jax.ShapeDtypeStruct((rows, width), F32),
            jax.ShapeDtypeStruct((rows, width), BF),
            jax.ShapeDtypeStruct((rows, columns), BF),
        ],
        scratch_shapes=[
            pltpu.VMEM((2, SPAN, width), F32),
            pltpu.VMEM((2, SPAN, width), F32),
            pltpu.SemaphoreType.DMA((2,)),
            pltpu.SemaphoreType.DMA((2,)),
        ],
        compiler_params=params(collective_id=3, has_side_effects=True),
        cost_estimate=LIGHT,
    )(att, w, tokens, gain)


def residual_back_kernel(
    g_ref, res_ref, n_ref, c_ref, r_ref, gain_ref, w_ref, rg_ref, low_ref, lg_ref, gg_ref, all_ref, p_ref, local, send, recv
):
    z = lax.axis_index("ctx")
    width = res_ref.shape[1]
    barrier = pltpu.get_barrier_semaphore()
    for k in (1, 2, 3):
        pl.semaphore_signal(barrier, inc=1, device_id={"ctx": (z + k) % 4}, device_id_type=MESH)
    pl.semaphore_wait(barrier, 3)
    gain = gain_ref[...]
    gain_grad = jnp.zeros(gain.shape, F32)
    columns = p_ref.shape[3]

    def to(c, side):
        return pltpu.make_async_remote_copy(
            src_ref=p_ref.at[side, c],
            dst_ref=all_ref.at[2 * z + side],
            send_sem=send.at[side, c],
            recv_sem=recv.at[side, z],
            device_id={"ctx": c},
            device_id_type=MESH,
        )

    def back_from(c, side):
        return pltpu.make_async_remote_copy(
            src_ref=p_ref.at[side, c],
            dst_ref=all_ref.at[2 * c + side],
            send_sem=send.at[side, c],
            recv_sem=recv.at[side, c],
            device_id={"ctx": c},
            device_id_type=MESH,
        )

    own = [
        pltpu.make_async_copy(p_ref.at[side, z], all_ref.at[2 * z + side], local.at[side])
        for side in (0, 1)
    ]
    for side in (0, 1):
        rows = slice(side * SPAN, (side + 1) * SPAN)
        named = c_ref[rows, width:].astype(F32) > 0.5
        logits = jnp.dot(n_ref[rows, :], r_ref[...], preferred_element_type=F32)
        logits = jnp.where(named, logits, -1e30)
        exponent = jnp.where(
            named, jnp.exp(logits - jnp.max(logits, axis=1, keepdims=True)), 0.0
        )
        gates = exponent / jnp.sum(exponent, axis=1, keepdims=True)
        found = g_ref[rows, width:].astype(F32)
        logit_grads = (gates * (found - jnp.sum(gates * found, axis=1, keepdims=True))).astype(BF)
        lg_ref[rows, :] = logit_grads
        grads = g_ref[rows, :width].astype(F32) + lax.dot_general(
            logit_grads, r_ref[...], NT, preferred_element_type=F32
        )
        residual = res_ref[rows, :]
        inverse = inverse_rms(residual)
        gain_grad = gain_grad + jnp.sum(grads * residual * inverse, axis=0, keepdims=True)
        scaled = gain * grads
        cube = inverse * inverse * inverse / width
        total = (
            c_ref[rows, :width].astype(F32)
            + inverse * scaled
            - residual * cube * jnp.sum(scaled * residual, axis=1, keepdims=True)
        )
        rg_ref[rows, :] = total
        low = total.astype(BF)
        low_ref[rows, :] = low
        attended = jnp.dot(low, w_ref[...], preferred_element_type=F32).astype(BF)
        for c in range(4):
            p_ref[side, c] = attended[:, c * columns : (c + 1) * columns]
        for c in range(4):

            @pl.when(z != c)
            def _():
                to(c, side).start()

        own[side].start()
    gg_ref[...] = gain_grad
    for side in (0, 1):
        own[side].wait()
        for c in range(4):

            @pl.when(z != c)
            def _():
                to(c, side).wait_send()
                back_from(c, side).wait_recv()


def residual_back(grad, residual, normed, cot, router, gain, w):
    rows, width = residual.shape
    columns = w.shape[1] // 4
    vmem = pl.BlockSpec(memory_space=pltpu.VMEM)
    return pl.pallas_call(
        residual_back_kernel,
        in_specs=[vmem] * 7,
        out_specs=[vmem] * 4 + [pl.BlockSpec(memory_space=pl.ANY)],
        out_shape=[
            jax.ShapeDtypeStruct((rows, width), F32),
            jax.ShapeDtypeStruct((rows, width), BF),
            jax.ShapeDtypeStruct((rows, LANES), BF),
            jax.ShapeDtypeStruct((1, width), F32),
            jax.ShapeDtypeStruct((8, SPAN, columns), BF),
        ],
        scratch_shapes=[
            pltpu.VMEM((2, 4, SPAN, columns), BF),
            pltpu.SemaphoreType.DMA((2,)),
            pltpu.SemaphoreType.DMA((2, 4)),
            pltpu.SemaphoreType.DMA((2, 4)),
        ],
        compiler_params=params(collective_id=4, has_side_effects=True),
        cost_estimate=LIGHT,
    )(grad, residual, normed, cot, router, gain, w)


def joint_back_kernel(
    dq_ref, dk_ref, dv_ref, cos_ref, sin_ref, w_ref, tok_ref, gain_ref, rg_ref,
    jg_ref, in_ref, gg_ref, land_ref, a_ref, p_ref, o_ref, send, recv, core_send, core_recv,
):
    z, t = lax.axis_index("ctx"), lax.axis_index("tp")
    core = {"tp": 1 - t}
    barrier = pltpu.get_barrier_semaphore()
    for partner in [{"ctx": (z + k) % 4} for k in (1, 2, 3)] + [core]:
        pl.semaphore_signal(barrier, inc=1, device_id=partner, device_id_type=MESH)
    pl.semaphore_wait(barrier, 4)
    columns = jg_ref.shape[2]
    rows_here = jg_ref.shape[1]

    def to(c):
        return pltpu.make_async_remote_copy(
            src_ref=jg_ref.at[c],
            dst_ref=land_ref.at[z],
            send_sem=send.at[c],
            recv_sem=recv.at[z],
            device_id={"ctx": c},
            device_id_type=MESH,
        )

    def back_from(c):
        return pltpu.make_async_remote_copy(
            src_ref=jg_ref.at[c],
            dst_ref=land_ref.at[c],
            send_sem=send.at[c],
            recv_sem=recv.at[c],
            device_id={"ctx": c},
            device_id_type=MESH,
        )

    for c in range(4):
        rows = slice(c * rows_here, (c + 1) * rows_here)
        cos, sin = cos_ref[rows, :], sin_ref[rows, :]
        a = jnp.concatenate([dq_ref[0, rows, :], dq_ref[1, rows, :]], axis=1)
        b = jnp.concatenate([dq_ref[2, rows, :], dk_ref[rows, :]], axis=1)
        jg_ref[c, :, :LANES] = (a * cos + half_turn(a, True) * sin).astype(BF)
        jg_ref[c, :, LANES : 2 * LANES] = (b * cos + half_turn(b, True) * sin).astype(BF)
        jg_ref[c, :, 2 * LANES :] = dv_ref[rows, :].astype(BF)

        @pl.when(z != c)
        def _():
            to(c).start()

    for c in range(4):
        place = slice(c * columns, (c + 1) * columns)

        @pl.when(z == c)
        def _():
            a_ref[:, place] = jg_ref[c]

        @pl.when(z != c)
        def _():
            back_from(c).wait_recv()
            a_ref[:, place] = land_ref[c]

    sent = []
    for side in (0, 1):
        rows = slice(side * SPAN, (side + 1) * SPAN)
        p_ref[side] = lax.dot_general(
            a_ref[rows, :], w_ref[...], NT, preferred_element_type=F32
        ).astype(BF)
        made = pltpu.make_async_remote_copy(
            src_ref=p_ref.at[side],
            dst_ref=o_ref.at[side],
            send_sem=core_send.at[side],
            recv_sem=core_recv.at[side],
            device_id=core,
            device_id_type=MESH,
        )
        made.start()
        sent.append(made)
    gain = gain_ref[...]
    width = gain.shape[1]
    gain_grad = jnp.zeros(gain.shape, F32)
    for side in (0, 1):
        rows = slice(side * SPAN, (side + 1) * SPAN)
        sent[side].wait_recv()
        grads = p_ref[side].astype(F32) + o_ref[side].astype(F32)
        tokens = tok_ref[rows, :].astype(F32)
        inverse = inverse_rms(tokens)
        gain_grad = gain_grad + jnp.sum(grads * tokens * inverse, axis=0, keepdims=True)
        scaled = gain * grads
        cube = inverse * inverse * inverse / width
        in_ref[rows, :] = (
            rg_ref[rows, :]
            + inverse * scaled
            - tokens * cube * jnp.sum(scaled * tokens, axis=1, keepdims=True)
        )
    gg_ref[...] = gain_grad
    for made in sent:
        made.wait_send()
    for c in range(4):

        @pl.when(z != c)
        def _():
            to(c).wait_send()


def joint_back(dq, dk, dv, cos, sin, w, tokens, gain, grads):
    rows, width = tokens.shape
    columns = (GROUP + 2) * HEAD_SIZE
    vmem = pl.BlockSpec(memory_space=pltpu.VMEM)
    return pl.pallas_call(
        joint_back_kernel,
        in_specs=[vmem] * 9,
        out_specs=[vmem] * 3,
        out_shape=[
            jax.ShapeDtypeStruct((4, rows, columns), BF),
            jax.ShapeDtypeStruct((rows, width), F32),
            jax.ShapeDtypeStruct((1, width), F32),
        ],
        scratch_shapes=[
            pltpu.VMEM((4, rows, columns), BF),
            pltpu.VMEM((rows, 4 * columns), BF),
            pltpu.VMEM((2, SPAN, width), BF),
            pltpu.VMEM((2, SPAN, width), BF),
            pltpu.SemaphoreType.DMA((4,)),
            pltpu.SemaphoreType.DMA((4,)),
            pltpu.SemaphoreType.DMA((2,)),
            pltpu.SemaphoreType.DMA((2,)),
        ],
        compiler_params=params(collective_id=5, has_side_effects=True),
        cost_estimate=LIGHT,
    )(dq, dk, dv, cos, sin, w, tokens, gain, grads)


def owner_of(f, k):
    return [f, f + 1 - 2 * (f % 2), (f + 2) % 4, 3 - f][k]


def expert_kernel(count, pieces, n_ref, cot_ref, one_ref, two_ref, r_ref, w_any, shard_ref, *refs):
    pre_ref, wh_ref, out_ref = refs[:3]
    x_parts, cot_parts = refs[3 : 3 + pieces], refs[3 + pieces : 3 + 2 * pieces]
    grad_any, joint_ref = refs[3 + 2 * pieces : 5 + 2 * pieces]
    x_ref, c_ref, w_ref, part_ref, there_ref, sum_ref, back_ref, full_ref = refs[5 + 2 * pieces : -4]
    local, wrote, send, recv = refs[-4:]
    i = pl.program_id(0)
    z, t, f = lax.axis_index("ctx"), lax.axis_index("tp"), lax.axis_index("fsdp")
    z1, z2, z3 = z + 1 - 2 * (z % 2), (z + 2) % 4, 3 - z
    near, far, third, core = {"ctx": z1}, {"ctx": z2}, {"ctx": z3}, {"tp": 1 - t}
    half, width = x_ref.shape[1:]
    piece = width // pieces
    hidden_columns = wh_ref.shape[1]
    units = hidden_columns // count

    def rows(side):
        return pl.ds(pl.multiple_of(side * half, half), half)

    def remote(k, source, target, device):
        return pltpu.make_async_remote_copy(
            src_ref=source,
            dst_ref=target,
            send_sem=send.at[k],
            recv_sem=recv.at[k],
            device_id=device,
            device_id_type=MESH,
        )

    own = n_ref.at[rows(t)]
    x_one = remote(0, own, x_ref.at[2], near)
    x_two = remote(1, own, x_ref.at[4], far)
    x_three = remote(2, x_ref.at[4], x_ref.at[6], near)
    c_three = remote(3, two_ref, c_ref.at[6], near)
    x_swaps = [None] + [remote(3 + m, x_ref.at[2 * m], x_ref.at[2 * m + 1], core) for m in (1, 2, 3)]
    c_swaps = [
        None,
        remote(7, one_ref, c_ref.at[3], core),
        remote(8, two_ref, c_ref.at[5], core),
        remote(9, c_ref.at[6], c_ref.at[7], core),
    ]
    crossed = [remote(10 + m, part_ref.at[2 * m + 1], there_ref.at[m], core) for m in range(4)]
    returned = [None] + [
        remote(13 + m, sum_ref.at[m], back_ref.at[m], device)
        for m, device in ((1, near), (2, far), (3, third))
    ]
    last = remote(17, full_ref.at[rows(t)], full_ref.at[rows(t)], core)
    loads = [
        pltpu.make_async_copy(source, target, local.at[k])
        for k, (source, target) in enumerate(
            (
                (n_ref.at[rows(t)], x_ref.at[0]),
                (n_ref.at[rows(1 - t)], x_ref.at[1]),
                (cot_ref.at[rows(t)], c_ref.at[0]),
                (cot_ref.at[rows(1 - t)], c_ref.at[1]),
                (w_any, w_ref),
                (one_ref, c_ref.at[2]),
                (two_ref, c_ref.at[4]),
            )
        )
    ]
    store = pltpu.make_async_copy(full_ref, grad_any, local.at[7])
    carried = []
    if pieces > 1:
        shard_rows = shard_ref.shape[0]
        cut = shard_rows // 2
        f1, f2 = owner_of(f, 1), owner_of(f, 2)

        def held(place, first, size):
            return joint_ref.at[pl.ds(pl.multiple_of(place * shard_rows + first, 8), size)]

        own_shard = pltpu.make_async_copy(shard_ref, held(f, 0, shard_rows), local.at[8])
        joint_one = remote(18, shard_ref, held(f, 0, shard_rows), {"fsdp": f1})
        joint_two = remote(19, shard_ref, held(f, 0, shard_rows), {"fsdp": f2})
        later = shard_rows - cut
        on_one = remote(20, held(f1, 0, cut), held(f1, 0, cut), {"fsdp": f2})
        on_two = remote(21, held(f2, cut, later), held(f2, cut, later), {"fsdp": f1})
        carried = [joint_one, joint_two, on_one, on_two]

    def keep(step):
        made = []
        at_rows = pl.ds(pl.multiple_of(step * half, half), half)
        for k in range(pieces):
            owner = [f, f + 1 - 2 * (f % 2), (f + 2) % 4, 3 - f][k] if pieces > 1 else 0
            at = pl.ds(pl.multiple_of(owner * piece, piece), piece)
            for n, (source, target) in enumerate(((x_ref, x_parts[k]), (c_ref, cot_parts[k]))):
                made.append(
                    pltpu.make_async_copy(
                        source.at[step, :, at], target.at[at_rows], wrote.at[step, 2 * k + n]
                    )
                )
        return made

    def finish(m):
        crossed[m].wait_recv()
        sum_ref[m] = (part_ref[2 * m].astype(F32) + there_ref[m].astype(F32)).astype(BF)
        if m:
            returned[m].start()

    @pl.when(i == 0)
    def _():
        partners = [near, far, third, core]
        if carried:
            partners += [{"fsdp": f1}, {"fsdp": f2}]
        barrier = pltpu.get_barrier_semaphore()
        for partner in partners:
            pl.semaphore_signal(barrier, inc=1, device_id=partner, device_id_type=MESH)
        pl.semaphore_wait(barrier, len(partners))
        if carried:
            joint_one.start()
            joint_two.start()
            own_shard.start()
        for made in [x_one, x_two] + loads + [c_swaps[1], c_swaps[2], c_three]:
            made.start()
        for made in (loads[0], loads[2], loads[4]):
            made.wait()

    @pl.when(i == 1)
    def _():
        loads[1].wait()
        loads[3].wait()

    @pl.when(i == 2)
    def _():
        x_one.wait_recv()
        x_swaps[1].start()
        loads[5].wait()

    @pl.when(i == 3)
    def _():
        x_swaps[1].wait_recv()
        c_swaps[1].wait_recv()

    @pl.when(i == 4)
    def _():
        x_two.wait_recv()
        x_three.start()
        x_swaps[2].start()
        loads[6].wait()

    @pl.when(i == 5)
    def _():
        x_swaps[2].wait_recv()
        c_swaps[2].wait_recv()

    @pl.when(i == 6)
    def _():
        finish(2)
        x_three.wait_recv()
        x_swaps[3].start()
        c_three.wait_recv()
        c_swaps[3].start()

        if carried:
            joint_one.wait_recv()
            on_one.start()
            joint_two.wait_recv()
            on_two.start()

    @pl.when(i == 7)
    def _():
        x_swaps[3].wait_recv()
        c_swaps[3].wait_recv()

    for made in keep(i):
        made.start()

    def columns(j, e):
        return slice(j * hidden_columns + e * units, j * hidden_columns + (e + 1) * units)

    x = x_ref[i]
    both = c_ref[i]
    cot = both[:, :width]
    named = both[:, width:].astype(F32) > 0.5
    logits = jnp.where(named, jnp.dot(x, r_ref[...], preferred_element_type=F32), -1e30)
    top = jnp.max(logits, axis=1, keepdims=True)
    exponent = jnp.where(named, jnp.exp(logits - top), 0.0)
    gates = exponent / jnp.sum(exponent, axis=1, keepdims=True)
    lane = lax.broadcasted_iota(jnp.int32, gates.shape, 1)
    found = jnp.zeros(gates.shape, F32)
    for e in range(count):
        mine = lane == z * count + e
        gate_here = jnp.sum(jnp.where(mine, gates, 0.0), axis=1, keepdims=True)
        g = jnp.dot(x, w_ref[:, columns(0, e)], preferred_element_type=F32)
        u = jnp.dot(x, w_ref[:, columns(1, e)], preferred_element_type=F32)
        hg = jnp.dot(cot, w_ref[:, columns(2, e)], preferred_element_type=F32)
        s = 1.0 / (1.0 + jnp.exp(-g))
        gs = g * s
        h = (gs * u).astype(BF).astype(F32)
        found = found + jnp.where(mine, jnp.sum(h * hg, axis=1, keepdims=True), 0.0)
        wh_ref[:, columns(0, e)] = (h * gate_here).astype(BF)
        hg = hg * gate_here
        pre_ref[:, columns(0, e)] = (hg * u * s * (1.0 + g * (1.0 - s))).astype(BF)
        pre_ref[:, columns(1, e)] = (hg * gs).astype(BF)
    part_ref[i, :, width:] = found.astype(BF)
    part_ref[i, :, :width] = lax.dot_general(
        pre_ref[...], w_ref[:, : 2 * hidden_columns], NT, preferred_element_type=F32
    ).astype(BF)
    for m in range(4):

        @pl.when(i == 2 * m + 1)
        def _():
            crossed[m].start()

    out_ref[...] = lax.dot_general(
        wh_ref[...], w_ref[:, 2 * hidden_columns :], NT, preferred_element_type=F32
    ).astype(BF)
    for m in range(2):

        @pl.when(i == 2 * m + 2)
        def _():
            finish(m)

    @pl.when(i == 7)
    def _():
        finish(3)
        total = sum_ref[0].astype(F32)
        for m in (1, 2, 3):
            returned[m].wait_recv()
            total = total + back_ref[m].astype(F32)
        full_ref[rows(t), :] = total.astype(BF)
        last.start()
        for made in [x_one, x_two, x_three, c_three] + x_swaps[1:] + c_swaps[1:] + crossed:
            made.wait_send()
        for made in returned[1:]:
            made.wait_send()
        last.wait_send()
        last.wait_recv()
        store.start()
        if carried:
            on_one.wait_recv()
            on_two.wait_recv()
            for made in carried:
                made.wait_send()
            own_shard.wait()

        def settle(step, carried):
            for made in keep(step):
                made.wait()
            return carried

        lax.fori_loop(0, 8, settle, 0)
        store.wait()


def experts(pieces, normed, cot, one, two, router, w, shard, count):
    rows, width = normed.shape
    half = rows // 2
    packed = cot.shape[1]
    hidden_columns = w.shape[1] // 3
    slot = lambda n: pl.BlockSpec((half, n), lambda i: (i, 0))
    anywhere = pl.BlockSpec(memory_space=pl.ANY)
    blocks = [2 * hidden_columns, hidden_columns, width]
    return pl.pallas_call(
        functools.partial(expert_kernel, count, pieces),
        grid=(8,),
        in_specs=[anywhere] * 4 + [pl.BlockSpec(router.shape, lambda i: (0, 0)), anywhere, anywhere],
        out_specs=[slot(n) for n in blocks] + [anywhere] * (2 * pieces + 2),
        out_shape=[
            jax.ShapeDtypeStruct((8 * half, n), BF) for n in blocks + [width // pieces] * (2 * pieces)
        ]
        + [
            jax.ShapeDtypeStruct((rows, packed), BF),
            jax.ShapeDtypeStruct((pieces * shard.shape[0], shard.shape[1]), BF),
        ],
        scratch_shapes=[
            pltpu.VMEM((8, half, width), BF),
            pltpu.VMEM((8, half, packed), BF),
            pltpu.VMEM(w.shape, BF),
            pltpu.VMEM((8, half, packed), BF),
            pltpu.VMEM((4, half, packed), BF),
            pltpu.VMEM((4, half, packed), BF),
            pltpu.VMEM((4, half, packed), BF),
            pltpu.VMEM((rows, packed), BF),
            pltpu.SemaphoreType.DMA((9,)),
            pltpu.SemaphoreType.DMA((8, 2 * pieces)),
            pltpu.SemaphoreType.DMA((22,)),
            pltpu.SemaphoreType.DMA((22,)),
        ],
        compiler_params=params(collective_id=1, has_side_effects=True),
        cost_estimate=LIGHT,
    )(normed, cot, one, two, router, w, shard)


def adamw(master, first_moment, second_moment, gradient, rate, decay):
    moment_new = 0.9 * first_moment + 0.1 * gradient
    square_new = 0.95 * second_moment + 0.05 * gradient * gradient
    corrected = moment_new / (1.0 - 0.9**STEP) / (jnp.sqrt(square_new / (1.0 - 0.95**STEP)) + 1e-08)
    master_new = master - rate * (corrected + decay * master)
    return (master_new, moment_new, square_new, master_new.astype(BF))


def expert_adamw_kernel(rate, joined, *refs):
    p_ref, f_ref, s_ref, g_ref = refs[:4]
    master_ref, moment_ref, rounded_ref, square_ref, grad_ref = refs[-5:]
    parts, _, columns = g_ref.shape
    units = p_ref.shape[3]
    each = columns // units
    for k in range(parts):
        for e in range(each):
            grad_ref[:, k * each + e, :] = g_ref[k, :, e * units : (e + 1) * units].astype(F32)
    for at in range(0, parts * each, 8):
        rows = slice(at, at + 8)
        new = adamw(
            p_ref[:, 0, rows], f_ref[:, 0, rows], s_ref[:, 0, rows], grad_ref[:, rows], rate, 0.1
        )
        master_ref[:, 0, rows] = new[0]
        moment_ref[:, 0, rows] = new[1]
        rounded_ref[:, 0, rows] = new[3]
        if joined:
            square_ref[:, rows, 0] = refs[4][:, rows]
            square_ref[:, rows, 1] = new[2]
        else:
            square_ref[:, rows] = new[2]


def expert_adamw(slot, rate, weight, first, second, gradient, earlier, joined=None):
    rows, _, count, units = weight.shape
    parts = gradient.shape[0]
    tile = next(t for t in (32, 16, 8) if rows % t == 0)
    here = pl.BlockSpec((tile, 1, count, units), lambda i: (i, slot, 0, 0))
    plain = pl.BlockSpec((tile, count, units), lambda i: (i, 0, 0))
    pair = pl.BlockSpec((tile, count, 2, units), lambda i: (i, 0, 0, 0))
    shape = jax.ShapeDtypeStruct(weight.shape, F32)
    chained = len(earlier)
    more = [] if joined is None else [joined]
    square = (rows, count, units) if joined is None else (rows, count, 2, units)
    return pl.pallas_call(
        functools.partial(expert_adamw_kernel, rate, joined is not None),
        grid=(rows // tile,),
        in_specs=[here, here, here]
        + [pl.BlockSpec((parts, tile, gradient.shape[2]), lambda i: (0, i, 0))]
        + [plain] * len(more)
        + [pl.BlockSpec(memory_space=pl.ANY)] * chained,
        out_specs=[here, here, here, plain if joined is None else pair],
        out_shape=[
            shape,
            shape,
            jax.ShapeDtypeStruct(weight.shape, BF),
            jax.ShapeDtypeStruct(square, F32),
        ],
        scratch_shapes=[pltpu.VMEM((tile, count, units), F32)],
        input_output_aliases={4 + len(more) + k: k for k in range(chained)},
        compiler_params=params(),
        cost_estimate=pl.CostEstimate(
            flops=20 * rows * count * units,
            bytes_accessed=45 * rows * count * units,
            transcendentals=rows * count * units,
        ),
    )(weight, first, second, gradient, *more, *earlier)


def matrix_adamw_kernel(rate, p_ref, f_ref, s_ref, g_ref, *outs):
    grad = g_ref[...].astype(F32).T
    new = adamw(p_ref[...], f_ref[...], s_ref[...], grad, rate, 0.1)
    for ref, value in zip(outs, new):
        ref[...] = value


def matrix_adamw(rate, weight, first, second, turned):
    rows, columns = weight.shape
    if rows % LANES:
        return adamw(weight, first, second, turned[:columns].T.astype(F32), rate, 0.1)
    tile = 256
    here = pl.BlockSpec((rows, tile), lambda i: (0, i))
    shape = jax.ShapeDtypeStruct(weight.shape, F32)
    return pl.pallas_call(
        functools.partial(matrix_adamw_kernel, rate),
        grid=(columns // tile,),
        in_specs=[here, here, here, pl.BlockSpec((tile, rows), lambda i: (i, 0))],
        out_specs=[here] * 4,
        out_shape=[shape, shape, shape, jax.ShapeDtypeStruct(weight.shape, BF)],
        compiler_params=params(),
        cost_estimate=pl.CostEstimate(
            flops=20 * rows * columns, bytes_accessed=28 * rows * columns, transcendentals=0
        ),
    )(weight, first, second, turned)


def local(
    sizes,
    block_input,
    out_cotangent,
    block_ids,
    expert_routes,
    norm_gains,
    gains_first,
    gains_second,
    joint_weight,
    joint_first,
    joint_second,
    output_weight,
    output_first,
    output_second,
    router_weight,
    router_first,
    router_second,
    expert_weight,
    expert_first,
    expert_second,
):
    n_fsdp, n_ctx, n_tp = sizes
    z = lax.axis_index("ctx")
    t = lax.axis_index("tp")
    f = lax.axis_index("fsdp")
    tokens_low = block_input[0]
    cot_low = out_cotangent[0]
    count, width = tokens_low.shape
    half = count // n_tp
    length = n_ctx * count
    own_rows = width // n_fsdp
    each = E // n_ctx

    barrier = lax.optimization_barrier

    def beyond(x, m):
        return lax.ppermute(x, "ctx", [(i, i ^ m) for i in range(n_ctx)])

    def swap(x):
        return lax.ppermute(x, "tp", [(0, 1), (1, 0)])

    def across(x, m):
        return lax.ppermute(x, "fsdp", [(i, i ^ m) for i in range(n_fsdp)])

    def mine(x):
        return lax.dynamic_slice_in_dim(x, t * half, half, 0)

    def other(x):
        return lax.dynamic_slice_in_dim(x, (1 - t) * half, half, 0)

    def in_order(a, b):
        return jnp.where(t == 0, jnp.concatenate([a, b], 0), jnp.concatenate([b, a], 0))

    def put(buffer, x, place):
        return lax.dynamic_update_slice_in_dim(buffer, x[None], place, 0)

    def put_row(x, row, place):
        return lax.dynamic_update_slice(x, row[None], (place, 0))

    def take(x, place, places):
        return lax.dynamic_index_in_dim(
            x.reshape(places, x.shape[0] // places, x.shape[1]), place, 0, keepdims=False
        )

    def sent_to_owners(x):
        if n_fsdp != 4:
            return [lax.psum_scatter(x, "fsdp", scatter_dimension=1, tiled=True)]
        part = lambda k: lax.dynamic_slice_in_dim(x, (f ^ k) * own_rows, own_rows, 1)
        return [part(0)] + [across(part(k), k) for k in (1, 2, 3)]

    def added(came):
        return came[0] if len(came) == 1 else sum(x.astype(F32) for x in came).astype(BF)

    def spread(x):
        one, two = beyond(x, 1), beyond(x, 2)
        return {1: one, 2: two, 3: beyond(two, 1)}

    slots_first = jnp.transpose(expert_weight, (0, 2, 1, 3))
    units = expert_weight.shape[3]
    expert_part = (
        lax.dynamic_slice_in_dim(slots_first, z * each, each, 2)
        .astype(BF)
        .reshape(own_rows, 3 * each * units)
    )
    expert_full = lax.all_gather(expert_part, "fsdp", axis=0, tiled=True)

    group_columns = (GROUP + 2) * HEAD_SIZE
    head_columns = GROUP * HEAD_SIZE
    joint_low = joint_weight.astype(BF)
    output_columns = output_weight.shape[1]
    first_pack = jnp.concatenate(
        [
            router_weight.astype(BF),
            norm_gains.T.astype(BF),
            jnp.zeros((own_rows, LANES - E - 2), BF),
            lax.dynamic_slice_in_dim(joint_low, z * group_columns, group_columns, 1),
        ],
        axis=1,
    )
    first_pack, _ = barrier((first_pack, expert_part))
    sequence, first_full = first_gather(n_ctx, n_fsdp, tokens_low, first_pack)
    small_full = first_full[:, :LANES]
    router_full = small_full[:, :E]
    router_wide = jnp.where(jnp.arange(LANES)[None, :] < E, small_full, jnp.zeros((), BF))
    gain_first = small_full[:, E].astype(F32)[None, :]
    gain_second = small_full[:, E + 1].astype(F32)[None, :]

    route_rows = expert_routes[0]
    lane_row = jnp.arange(LANES, dtype=jnp.int32)[None, :]
    member = sum((route_rows[:, k : k + 1] == lane_row).astype(F32) for k in range(route_rows.shape[1]))
    cot_pack = jnp.concatenate([cot_low, member.astype(BF)], axis=1)
    cot_half, sequence = barrier((mine(cot_pack), sequence))
    cot_came = [beyond(cot_half, 1), beyond(cot_half, 2)]

    lanes = jnp.arange(LANES, dtype=jnp.int32) % (HEAD_SIZE // 2)
    frequency = jnp.exp(lanes.astype(F32) * (-2.0 * math.log(10000.0) / HEAD_SIZE))
    fine = 64
    small_angles = jnp.arange(fine, dtype=jnp.int32).astype(F32)[:, None] * frequency
    large_angles = (fine * jnp.arange(length // fine, dtype=jnp.int32)).astype(F32)[:, None] * frequency
    cos_a, sin_a = jnp.cos(large_angles)[:, None], jnp.sin(large_angles)[:, None]
    cos_b, sin_b = jnp.cos(small_angles)[None], jnp.sin(small_angles)[None]
    cosine = (cos_a * cos_b - sin_a * sin_b).reshape(length, LANES)
    sine = (sin_a * cos_b + cos_a * sin_b).reshape(length, LANES)
    cosine, sine, tokens_low = barrier((cosine, sine, tokens_low))
    id_row = block_ids
    id_column = block_ids.reshape(length, 1)
    normed_all, queries, keys, values = project(sequence, gain_first, first_full, cosine, sine)
    output_low = output_weight.astype(BF)
    attended_all, lse, attended_here, output_full = attend(
        n_fsdp, id_column, id_row, queries, keys, values, output_low
    )
    if n_fsdp != 4:
        output_full = lax.all_gather(output_low, "fsdp", axis=0, tiled=True)
    residual, normed_second, attended = project_out(
        attended_here, output_full, tokens_low, gain_second
    )

    pieces = n_fsdp if n_fsdp == 4 else 1
    pre_all, hidden_all, out_all, *kept, grad_rows, joint_full = experts(
        pieces, normed_second, cot_pack, *cot_came, router_wide, expert_full, joint_low, each
    )
    if pieces == 1:
        joint_full = lax.all_gather(joint_low, "fsdp", axis=0, tiled=True)
    x_parts, cot_parts = kept[:pieces], kept[pieces:]
    outs = out_all.reshape(n_ctx, 2, half, width)
    outs = [
        (outs[m, 0].astype(F32) + swap(outs[m, 1]).astype(F32)).astype(BF) for m in range(n_ctx)
    ]
    outs, x_parts, cot_parts = barrier((outs, x_parts, cot_parts))
    out_near = [beyond(outs[1], 1), beyond(outs[3], 1)]

    wide = each * units

    def expert_terms(j):
        left = cot_parts if j == 2 else x_parts
        right = hidden_all if j == 2 else pre_all[:, j * wide : (j + 1) * wide]
        return [
            lax.dot_general(left[k], right, TN, preferred_element_type=F32).astype(BF)
            for k in range(pieces)
        ]

    terms = {j: expert_terms(j) for j in (2, 0, 1)}
    pieces_came = {}
    for j in (2, 0, 1):
        if pieces > 1:
            pieces_came[j] = [terms[j][0]] + [across(terms[j][k], k) for k in range(1, pieces)]
        else:
            pieces_came[j] = [
                lax.psum_scatter(terms[j][0], "fsdp", scatter_dimension=0, tiled=True)
            ]

    def gathered(came):
        return lax.all_gather(added(came), "ctx", axis=0, tiled=False)

    grad_rows, joint_full, terms[2], out_near = barrier(
        (grad_rows, joint_full, terms[2], out_near)
    )
    out_far = beyond((outs[2].astype(F32) + out_near[1].astype(F32)).astype(BF), 2)
    residual_grads, residual_low, logit_grads, gain_second_grad, attended_grads_all = residual_back(
        grad_rows, residual, normed_second, cot_pack, router_wide, gain_second, output_full
    )
    attended_grads_all, pieces_came[2], out_far, *_ = barrier(
        (attended_grads_all, pieces_came[2], out_far, terms[0], terms[1])
    )
    expert_sums = {2: gathered(pieces_came[2])}
    step = 64
    few_rows = jnp.concatenate([logit_grads[:, :E], jnp.zeros((count, step - E), BF)], axis=1)
    rest_term = jnp.concatenate(
        [
            lax.dot_general(attended, residual_low, TN, preferred_element_type=F32).astype(BF),
            lax.dot_general(few_rows, normed_second, TN, preferred_element_type=F32).astype(BF),
        ],
        axis=0,
    )
    rest_term = lax.dynamic_update_slice(
        rest_term, gain_second_grad.astype(BF), (output_columns + E, 0)
    )
    rest_term, attended_grads_all = barrier((rest_term, attended_grads_all))
    dq, dk, dv = attend_back(
        id_column,
        id_row,
        queries,
        keys,
        values,
        attended_all,
        attended_grads_all.reshape(length, head_columns),
        lse,
    )
    dq, pieces_came[0] = barrier((dq, pieces_came[0]))
    expert_sums[0] = gathered(pieces_came[0])
    joint_grads, input_rows, gain_first_grad = joint_back(
        dq, dk, dv, cosine, sine, joint_full, tokens_low, gain_first, residual_grads
    )
    joint_grads, pieces_came[1], rest_term = barrier((joint_grads, pieces_came[1], rest_term))
    expert_sums[1] = gathered(pieces_came[1])
    joint_grads_all = joint_grads.reshape(length, group_columns)

    first_view = jnp.transpose(expert_first, (0, 2, 1, 3))
    second_view = jnp.transpose(expert_second, (0, 2, 1, 3))
    made = []
    squares = {}

    def expert_step(j, joined=None):
        rate = 0.25 if j == 2 else 0.03
        *made[:], squares[j] = expert_adamw(
            j, rate, slots_first, first_view, second_view, expert_sums[j], tuple(made), joined
        )

    joint_term = lax.dot_general(joint_grads_all, normed_all, TN, preferred_element_type=F32)
    joint_term = jnp.concatenate(
        [
            joint_term.astype(BF),
            jnp.where(jnp.arange(16)[:, None] == 0, gain_first_grad, 0.0).astype(BF),
            rest_term,
        ],
        axis=0,
    )
    joint_came = sent_to_owners(joint_term)

    expert_step(2)
    joint_came, made[:], squares[2] = barrier((joint_came, made, squares[2]))
    joint_owned = added(joint_came)
    rest_owned = put_row(
        joint_owned[group_columns + 16 :], joint_owned[group_columns], output_columns + E + 1
    )
    joint_owned = joint_owned[:group_columns]
    rest_parts = [take(rest_owned, z, n_ctx)]
    rest_parts += [beyond(take(rest_owned, z ^ m, n_ctx), m) for m in range(1, n_ctx)]
    expert_step(0)
    rest_parts, made[:], squares[0] = barrier((rest_parts, made, squares[0]))
    rest_low = sum(x.astype(F32) for x in rest_parts).astype(BF)
    both = jnp.concatenate([joint_owned, rest_low], axis=0)
    both_all = {0: both, **spread(both)}
    full = jnp.zeros((n_ctx, *both.shape), BF)
    for m, got in both_all.items():
        full = put(full, got, z ^ m)
    joint_sum = full[:, :group_columns].reshape(n_ctx * group_columns, own_rows)
    rest_full = full[:, group_columns:].reshape(output_columns + step, own_rows)
    moe_low = (
        outs[0].astype(F32) + out_near[0].astype(F32) + out_far.astype(F32)
    ).astype(BF)
    moe_rows = in_order(moe_low, swap(moe_low)).astype(F32)
    block_output = (residual + moe_rows).astype(BF)[None]
    router_sum = rest_full[output_columns : output_columns + E].T.astype(F32)
    gains_sum = jnp.stack(
        [rest_full[output_columns + E + 1], rest_full[output_columns + E]]
    ).astype(F32)

    gains_new = adamw(norm_gains, gains_first, gains_second, gains_sum, 0.6, 0.0)
    joint_new = matrix_adamw(0.03, joint_weight, joint_first, joint_second, joint_sum)
    output_new = matrix_adamw(0.25, output_weight, output_first, output_second, rest_full)
    router_new = adamw(router_weight, router_first, router_second, router_sum, 0.015, 0.1)

    expert_sums[1], block_output, joint_new, output_new = barrier(
        (expert_sums[1], block_output, joint_new, output_new)
    )
    expert_step(1, squares[0])
    back = lambda x: jnp.transpose(x, (0, 2, 1, 3))
    return (
        block_output,
        input_rows[None],
        *gains_new,
        *joint_new,
        *output_new,
        *router_new,
        back(made[0]),
        back(made[1]),
        squares[1],
        squares[2],
        back(made[2]),
    )


def solution(mesh):
    rows = P("fsdp", "ctx", None)
    gains = P(None, "fsdp")
    matrix = P("fsdp", "tp")
    router = P("fsdp", None)
    expert = P("fsdp", None, None, "tp")
    sizes = (mesh.shape["fsdp"], mesh.shape["ctx"], mesh.shape["tp"])
    return jax.shard_map(
        functools.partial(local, sizes),
        mesh=mesh,
        in_specs=(rows, rows, P("fsdp", None), rows)
        + (gains,) * 3
        + (matrix,) * 6
        + (router,) * 3
        + (expert,) * 3,
        out_specs=(rows, rows)
        + (gains,) * 4
        + (matrix,) * 8
        + (router,) * 4
        + (expert, expert, expert, P("fsdp", None, "tp"), expert),
        check_vma=False,
    )
```

```python
import functools
import math

import jax
import jax.numpy as jnp
from jax import lax
from jax.experimental import pallas as pl
from jax.experimental.pallas import tpu as pltpu
from jax.sharding import PartitionSpec as P

QUERY_HEADS = 24
KEY_VALUE_HEADS = 8
HEAD_SIZE = 64
GROUP = QUERY_HEADS // KEY_VALUE_HEADS
E = 16
STEP = 10
SPAN = 256
LANES = 128
BF = jnp.bfloat16
F32 = jnp.float32
NT = (((1,), (1,)), ((), ()))
TN = (((0,), (0,)), ((), ()))
VMEM_LIMIT = 58 * 1024 * 1024
LIGHT = pl.CostEstimate(flops=10**9, bytes_accessed=10**6, transcendentals=0)
MESH = pl.DeviceIdType.MESH


def params(**more):
    return pltpu.CompilerParams(vmem_limit_bytes=VMEM_LIMIT, **more)


def inverse_rms(rows):
    return lax.rsqrt(jnp.mean(rows * rows, axis=-1, keepdims=True) + 1e-06)


def half_turn(x, inverse):
    lane = lax.broadcasted_iota(jnp.int32, x.shape, 1)
    first = (lane % HEAD_SIZE) < HEAD_SIZE // 2
    later = pltpu.roll(x, LANES - HEAD_SIZE // 2, 1)
    sooner = pltpu.roll(x, HEAD_SIZE // 2, 1)
    return jnp.where(first, later, -sooner) if inverse else jnp.where(first, -later, sooner)


def first_gather_kernel(weights, tok_ref, pack_ref, seq_ref, full_ref, local, send, recv):
    z, t, f = lax.axis_index("ctx"), lax.axis_index("tp"), lax.axis_index("fsdp")
    half = tok_ref.shape[0] // 2
    rows = pack_ref.shape[0]
    z1, z2, z3 = z + 1 - 2 * (z % 2), (z + 2) % 4, 3 - z
    near, far, core = {"ctx": z1}, {"ctx": z2}, {"tp": 1 - t}
    partners = [near, far, core]
    if weights:
        f1, f2 = f + 1 - 2 * (f % 2), (f + 2) % 4
        f3 = 3 - f
        partners += [{"fsdp": f1}, {"fsdp": f2}]
    barrier = pltpu.get_barrier_semaphore()
    for partner in partners:
        pl.semaphore_signal(barrier, inc=1, device_id=partner, device_id_type=MESH)
    pl.semaphore_wait(barrier, len(partners))

    def at(chunk, side):
        return seq_ref.at[pl.ds(pl.multiple_of((chunk * 2 + side) * half, half), half)]

    def held(owner, first, size):
        start = pl.multiple_of(owner * rows + first, 8)
        return full_ref.at[pl.ds(start, size)]

    def copy(k, source, target, device):
        made = pltpu.make_async_remote_copy(
            src_ref=source,
            dst_ref=target,
            send_sem=send.at[k],
            recv_sem=recv.at[k],
            device_id=device,
            device_id_type=MESH,
        )
        made.start()
        return made

    own_half = tok_ref.at[pl.ds(pl.multiple_of(t * half, half), half)]
    one = copy(0, own_half, at(z, t), near)
    two = copy(1, own_half, at(z, t), far)
    here = pltpu.make_async_copy(
        tok_ref, seq_ref.at[pl.ds(pl.multiple_of(z * 2 * half, half), 2 * half)], local.at[0]
    )
    here.start()
    sent = [one, two]
    came = []
    if weights:
        cut = rows // 2
        pack_one = copy(6, pack_ref, held(f, 0, rows), {"fsdp": f1})
        pack_two = copy(7, pack_ref, held(f, 0, rows), {"fsdp": f2})
        pack_here = pltpu.make_async_copy(pack_ref, held(f, 0, rows), local.at[1])
        pack_here.start()
        sent += [pack_one, pack_two]
    one.wait_recv()
    swap_one = copy(2, at(z1, t), at(z1, t), core)
    if weights:
        pack_one.wait_recv()
        on_one = copy(8, held(f1, 0, cut), held(f1, 0, cut), {"fsdp": f2})
        pack_two.wait_recv()
        on_two = copy(9, held(f2, cut, rows - cut), held(f2, cut, rows - cut), {"fsdp": f1})
        sent += [on_one, on_two]
        came += [on_one, on_two]
    two.wait_recv()
    three = copy(4, at(z2, t), at(z2, t), near)
    swap_two = copy(3, at(z2, t), at(z2, t), core)
    three.wait_recv()
    swap_three = copy(5, at(z3, t), at(z3, t), core)
    sent += [swap_one, three, swap_two, swap_three]
    for made in came + [swap_one, swap_two, swap_three]:
        made.wait_recv()
    for made in sent:
        made.wait_send()
    here.wait()
    if weights:
        pack_here.wait()


def first_gather(n_ctx, n_fsdp, tokens, pack):
    count, width = tokens.shape
    rows, columns = pack.shape
    weights = n_fsdp == 4
    sequence, full = pl.pallas_call(
        functools.partial(first_gather_kernel, weights),
        in_specs=[pl.BlockSpec(memory_space=pl.ANY)] * 2,
        out_specs=[pl.BlockSpec(memory_space=pl.ANY)] * 2,
        out_shape=[
            jax.ShapeDtypeStruct((n_ctx * count, width), tokens.dtype),
            jax.ShapeDtypeStruct((n_fsdp * rows if weights else rows, columns), pack.dtype),
        ],
        scratch_shapes=[
            pltpu.SemaphoreType.DMA((2,)),
            pltpu.SemaphoreType.DMA((10,)),
            pltpu.SemaphoreType.DMA((10,)),
        ],
        compiler_params=pltpu.CompilerParams(collective_id=0, has_side_effects=True),
        cost_estimate=LIGHT,
    )(tokens, pack)
    if not weights:
        full = lax.all_gather(pack, "fsdp", axis=0, tiled=True)
    return sequence, full


def project_kernel(x_ref, gain_ref, w_ref, cos_ref, sin_ref, n_ref, q_ref, k_ref, v_ref):
    x = x_ref[...].astype(F32)
    n = (x * inverse_rms(x) * gain_ref[...]).astype(BF)
    n_ref[...] = n
    c = jnp.dot(n, w_ref[:, LANES:], preferred_element_type=F32)
    cos, sin = cos_ref[...], sin_ref[...]
    a = c[:, :LANES]
    b = c[:, LANES : 2 * LANES]
    a = a * cos + half_turn(a, False) * sin
    b = b * cos + half_turn(b, False) * sin
    scale = 1.0 / math.sqrt(HEAD_SIZE)
    a = a.astype(BF) * jnp.asarray(scale, BF)
    q_ref[0] = a[:, :HEAD_SIZE]
    q_ref[1] = a[:, HEAD_SIZE:]
    b = b.astype(BF)
    q_ref[2] = b[:, :HEAD_SIZE] * jnp.asarray(scale, BF)
    k_ref[...] = b[:, HEAD_SIZE:]
    v_ref[...] = c[:, 2 * LANES :].astype(BF)


def project(x, gain, w, cos, sin):
    rows, width = x.shape
    tile = 512
    row = lambda n: pl.BlockSpec((tile, n), lambda i: (i, 0))
    whole = lambda s: pl.BlockSpec(s, lambda i: (0, 0))
    return pl.pallas_call(
        project_kernel,
        grid=(rows // tile,),
        in_specs=[row(width), whole(gain.shape), whole(w.shape), row(LANES), row(LANES)],
        out_specs=[
            row(width),
            pl.BlockSpec((GROUP, tile, HEAD_SIZE), lambda i: (0, i, 0)),
            row(HEAD_SIZE),
            row(HEAD_SIZE),
        ],
        out_shape=[
            jax.ShapeDtypeStruct((rows, width), BF),
            jax.ShapeDtypeStruct((GROUP, rows, HEAD_SIZE), BF),
            jax.ShapeDtypeStruct((rows, HEAD_SIZE), BF),
            jax.ShapeDtypeStruct((rows, HEAD_SIZE), BF),
        ],
        compiler_params=params(),
        cost_estimate=LIGHT,
    )(x, gain, w, cos, sin)


def to_row(column, eye):
    return jnp.sum(jnp.where(eye, column, 0.0), axis=0, keepdims=True)


def to_column(row, eye):
    return jnp.sum(jnp.where(eye, row, 0.0), axis=1, keepdims=True)


def identity_mask():
    return lax.broadcasted_iota(jnp.int32, (SPAN, SPAN), 0) == lax.broadcasted_iota(
        jnp.int32, (SPAN, SPAN), 1
    )


def attend_kernel(weights, *refs):
    idc_ref, idr_ref, q_ref, k_ref, v_ref, shard_ref, o_ref, lse_ref, att_ref, full_ref = refs[:10]
    s_ref, m_ref, l_ref, a_ref, oall_ref, local, send, recv = refs[10:]
    i = pl.program_id(0)
    blocks = pl.num_programs(0)
    z, f = lax.axis_index("ctx"), lax.axis_index("fsdp")
    rows = shard_ref.shape[0]
    cut = rows // 2
    f1, f2 = f + 1 - 2 * (f % 2), (f + 2) % 4
    f3 = 3 - f

    def remote(k, source, target, device):
        return pltpu.make_async_remote_copy(
            src_ref=source,
            dst_ref=target,
            send_sem=send.at[k],
            recv_sem=recv.at[k],
            device_id=device,
            device_id_type=MESH,
        )

    def held(owner, first, size):
        return full_ref.at[pl.ds(pl.multiple_of(owner * rows + first, 8), size)]

    own_weights = pltpu.make_async_copy(shard_ref, held(f, 0, rows), local.at[1])
    if weights:
        one = remote(4, shard_ref, held(f, 0, rows), {"fsdp": f1})
        two = remote(5, shard_ref, held(f, 0, rows), {"fsdp": f2})
        on_one = remote(6, held(f1, 0, cut), held(f1, 0, cut), {"fsdp": f2})
        on_two = remote(7, held(f2, cut, rows - cut), held(f2, cut, rows - cut), {"fsdp": f1})

    def to(c):
        return pltpu.make_async_remote_copy(
            src_ref=oall_ref.at[pl.ds(2 * c, 2)],
            dst_ref=att_ref.at[pl.ds(2 * z, 2)],
            send_sem=send.at[c],
            recv_sem=recv.at[z],
            device_id={"ctx": c},
            device_id_type=MESH,
        )

    def back_from(c):
        return pltpu.make_async_remote_copy(
            src_ref=oall_ref.at[pl.ds(2 * c, 2)],
            dst_ref=att_ref.at[pl.ds(2 * c, 2)],
            send_sem=send.at[c],
            recv_sem=recv.at[c],
            device_id={"ctx": c},
            device_id_type=MESH,
        )

    own_rows = pltpu.make_async_copy(
        oall_ref.at[pl.ds(2 * z, 2)], att_ref.at[pl.ds(2 * z, 2)], local.at[0]
    )

    @pl.when(i == 0)
    def _():
        barrier = pltpu.get_barrier_semaphore()
        partners = [{"ctx": (z + k) % 4} for k in (1, 2, 3)]
        if weights:
            partners += [{"fsdp": f1}, {"fsdp": f2}]
        for partner in partners:
            pl.semaphore_signal(barrier, inc=1, device_id=partner, device_id_type=MESH)
        pl.semaphore_wait(barrier, len(partners))
        if weights:
            one.start()
            two.start()
            own_weights.start()

    if weights:

        @pl.when(i == 6)
        def _():
            one.wait_recv()
            on_one.start()
            two.wait_recv()
            on_two.start()

    q = q_ref[...].reshape(GROUP * SPAN, HEAD_SIZE)
    m_ref[...] = jnp.full(m_ref.shape, -1e30, F32)
    l_ref[...] = jnp.zeros(l_ref.shape, F32)
    a_ref[...] = jnp.zeros(a_ref.shape, F32)

    def place(block):
        return pl.ds(pl.multiple_of(block * SPAN, SPAN), SPAN)

    def score(block, masked):
        at = place(block)
        s = lax.dot_general(k_ref[at, :], q, NT, preferred_element_type=F32)
        if masked:
            seen = (idc_ref[at, :] <= idr_ref[...]).astype(F32)
            s = jnp.where(jnp.concatenate([seen] * GROUP, axis=1) > 0.5, s, -1e30)
        s_ref[at, :] = s
        m_ref[...] = jnp.maximum(m_ref[...], jnp.max(s, axis=0, keepdims=True))

    def weigh(block):
        at = place(block)
        p = jnp.exp(s_ref[at, :] - m_ref[...])
        l_ref[...] += jnp.sum(p, axis=0, keepdims=True)
        a_ref[...] += lax.dot_general(p.astype(BF), v_ref[at, :], TN, preferred_element_type=F32)

    def open_score(block, carried):
        score(block, False)
        return carried

    def open_weigh(block, carried):
        weigh(block)
        return carried

    lax.fori_loop(0, i, open_score, 0)
    score(i, True)

    @pl.when(i + 1 < blocks)
    def _():
        score(i + 1, True)

    lax.fori_loop(0, jnp.minimum(i + 2, blocks), open_weigh, 0)

    total = l_ref[...]
    lse = m_ref[...] + jnp.log(total)
    eye = identity_mask()
    for g in range(GROUP):
        part = slice(g * SPAN, (g + 1) * SPAN)
        out = a_ref[part, :] / to_column(total[:, part], eye)
        o_ref[:, g * HEAD_SIZE : (g + 1) * HEAD_SIZE] = out.astype(BF)
        oall_ref[i, :, g * HEAD_SIZE : (g + 1) * HEAD_SIZE] = out.astype(BF)
        lse_ref[g] = lse[:, part]
    for c in range(4):

        @pl.when(jnp.logical_and(i == 2 * c + 1, z != c))
        def _():
            to(c).start()

    @pl.when(i == 7)
    def _():
        own_rows.start()
        own_rows.wait()
        if weights:
            on_one.wait_recv()
            on_two.wait_recv()
            for made in (one, two, on_one, on_two):
                made.wait_send()
            own_weights.wait()

    for c in range(4):

        @pl.when(jnp.logical_and(i == 7, z != c))
        def _():
            to(c).wait_send()
            back_from(c).wait_recv()


def attend(n_fsdp, id_column, id_row, q, k, v, shard):
    rows = k.shape[0]
    weights = n_fsdp == 4
    anywhere = pl.BlockSpec(memory_space=pl.ANY)
    full_rows = shard.shape[0] * (n_fsdp if weights else 1)
    whole = lambda s: pl.BlockSpec(s, lambda i: (0,) * len(s))
    return pl.pallas_call(
        functools.partial(attend_kernel, weights),
        grid=(rows // SPAN,),
        in_specs=[
            whole(id_column.shape),
            pl.BlockSpec((1, SPAN), lambda i: (0, i)),
            pl.BlockSpec((GROUP, SPAN, HEAD_SIZE), lambda i: (0, i, 0)),
            whole(k.shape),
            whole(v.shape),
            anywhere,
        ],
        out_specs=[
            pl.BlockSpec((SPAN, GROUP * HEAD_SIZE), lambda i: (i, 0)),
            pl.BlockSpec((GROUP, 1, SPAN), lambda i: (0, 0, i)),
            anywhere,
            anywhere,
        ],
        out_shape=[
            jax.ShapeDtypeStruct((rows, GROUP * HEAD_SIZE), BF),
            jax.ShapeDtypeStruct((GROUP, 1, rows), F32),
            jax.ShapeDtypeStruct((8, SPAN, GROUP * HEAD_SIZE), BF),
            jax.ShapeDtypeStruct((full_rows, shard.shape[1]), BF),
        ],
        scratch_shapes=[
            pltpu.VMEM((rows, GROUP * SPAN), F32),
            pltpu.VMEM((1, GROUP * SPAN), F32),
            pltpu.VMEM((1, GROUP * SPAN), F32),
            pltpu.VMEM((GROUP * SPAN, HEAD_SIZE), F32),
            pltpu.VMEM((8, SPAN, GROUP * HEAD_SIZE), BF),
            pltpu.SemaphoreType.DMA((2,)),
            pltpu.SemaphoreType.DMA((8,)),
            pltpu.SemaphoreType.DMA((8,)),
        ],
        compiler_params=params(collective_id=2, has_side_effects=True),
        cost_estimate=LIGHT,
    )(id_column, id_row, q, k, v, shard)


def attend_back_kernel(
    idc_ref, idr_ref, q_ref, k_ref, v_ref, o_ref, do_ref, lse_ref, dq_ref, dk_ref, dv_ref, a_ref
):
    i = pl.program_id(0)
    blocks = pl.num_programs(0)

    @pl.when(i == 0)
    def _():
        dk_ref[...] = jnp.zeros(dk_ref.shape, F32)
        dv_ref[...] = jnp.zeros(dv_ref.shape, F32)

    q = q_ref[...].reshape(GROUP * SPAN, HEAD_SIZE)
    eye = identity_mask()
    grads, deltas = [], []
    for g in range(GROUP):
        lanes = slice(g * HEAD_SIZE, (g + 1) * HEAD_SIZE)
        part = do_ref[:, lanes]
        grads.append(part)
        product = part.astype(F32) * o_ref[:, lanes].astype(F32)
        deltas.append(to_row(jnp.sum(product, axis=1, keepdims=True), eye))
    do = jnp.concatenate(grads, axis=0)
    delta = jnp.concatenate(deltas, axis=1)
    lse = jnp.concatenate([lse_ref[g] for g in range(GROUP)], axis=1)
    a_ref[...] = jnp.zeros(a_ref.shape, F32)

    def step(block, masked):
        at = pl.ds(pl.multiple_of(block * SPAN, SPAN), SPAN)
        k = k_ref[at, :]
        s = lax.dot_general(k, q, NT, preferred_element_type=F32)
        p = jnp.exp(s - lse)
        if masked:
            seen = idc_ref[at, :] <= idr_ref[...]
            p = jnp.where(jnp.concatenate([seen.astype(F32)] * GROUP, axis=1) > 0.5, p, 0.0)
        dp = lax.dot_general(v_ref[at, :], do, NT, preferred_element_type=F32)
        ds = (p * (dp - delta)).astype(BF)
        dv_ref[at, :] += jnp.dot(p.astype(BF), do, preferred_element_type=F32)
        dk_ref[at, :] += jnp.dot(ds, q, preferred_element_type=F32)
        a_ref[...] += lax.dot_general(ds, k, TN, preferred_element_type=F32)

    def open_step(block, carried):
        step(block, False)
        return carried

    lax.fori_loop(0, i, open_step, 0)
    step(i, True)

    @pl.when(i + 1 < blocks)
    def _():
        step(i + 1, True)

    dq_ref[...] = a_ref[...].reshape(GROUP, SPAN, HEAD_SIZE) * (1.0 / math.sqrt(HEAD_SIZE))


def attend_back(id_column, id_row, q, k, v, o, do, lse):
    rows = k.shape[0]
    whole = lambda s: pl.BlockSpec(s, lambda i: (0,) * len(s))
    heads = pl.BlockSpec((GROUP, SPAN, HEAD_SIZE), lambda i: (0, i, 0))
    flat = pl.BlockSpec((SPAN, GROUP * HEAD_SIZE), lambda i: (i, 0))
    return pl.pallas_call(
        attend_back_kernel,
        grid=(rows // SPAN,),
        in_specs=[
            whole(id_column.shape),
            pl.BlockSpec((1, SPAN), lambda i: (0, i)),
            heads,
            whole(k.shape),
            whole(v.shape),
            flat,
            flat,
            pl.BlockSpec((GROUP, 1, SPAN), lambda i: (0, 0, i)),
        ],
        out_specs=[heads, whole(k.shape), whole(v.shape)],
        out_shape=[
            jax.ShapeDtypeStruct((GROUP, rows, HEAD_SIZE), F32),
            jax.ShapeDtypeStruct(k.shape, F32),
            jax.ShapeDtypeStruct(v.shape, F32),
        ],
        scratch_shapes=[pltpu.VMEM((GROUP * SPAN, HEAD_SIZE), F32)],
        compiler_params=params(),
        cost_estimate=LIGHT,
    )(id_column, id_row, q, k, v, o, do, lse)


def project_out_kernel(att_ref, w_ref, tok_ref, gain_ref, res_ref, n_ref, a_ref, p_ref, o_ref, send, recv):
    t = lax.axis_index("tp")
    core = {"tp": 1 - t}
    barrier = pltpu.get_barrier_semaphore()
    pl.semaphore_signal(barrier, inc=1, device_id=core, device_id_type=MESH)
    pl.semaphore_wait(barrier, 1)
    columns = att_ref.shape[2]
    sent = []
    for side in (0, 1):
        rows = slice(side * SPAN, (side + 1) * SPAN)
        for c in range(4):
            a_ref[rows, c * columns : (c + 1) * columns] = att_ref[2 * c + side]
        p_ref[side] = lax.dot_general(a_ref[rows, :], w_ref[...], NT, preferred_element_type=F32)
        made = pltpu.make_async_remote_copy(
            src_ref=p_ref.at[side],
            dst_ref=o_ref.at[side],
            send_sem=send.at[side],
            recv_sem=recv.at[side],
            device_id=core,
            device_id_type=MESH,
        )
        made.start()
        sent.append(made)
    for side in (0, 1):
        rows = slice(side * SPAN, (side + 1) * SPAN)
        sent[side].wait_recv()
        residual = tok_ref[rows, :].astype(F32) + (p_ref[side] + o_ref[side])
        res_ref[rows, :] = residual
        n_ref[rows, :] = (residual * inverse_rms(residual) * gain_ref[...]).astype(BF)
    for made in sent:
        made.wait_send()


def project_out(att, w, tokens, gain):
    rows, width = tokens.shape
    columns = w.shape[1]
    return pl.pallas_call(
        project_out_kernel,
        in_specs=[pl.BlockSpec(memory_space=pltpu.VMEM)] * 4,
        out_specs=[pl.BlockSpec(memory_space=pltpu.VMEM)] * 3,
        out_shape=[
            jax.ShapeDtypeStruct((rows, width), F32),
            jax.ShapeDtypeStruct((rows, width), BF),
            jax.ShapeDtypeStruct((rows, columns), BF),
        ],
        scratch_shapes=[
            pltpu.VMEM((2, SPAN, width), F32),
            pltpu.VMEM((2, SPAN, width), F32),
            pltpu.SemaphoreType.DMA((2,)),
            pltpu.SemaphoreType.DMA((2,)),
        ],
        compiler_params=params(collective_id=3, has_side_effects=True),
        cost_estimate=LIGHT,
    )(att, w, tokens, gain)


def residual_back_kernel(
    g_ref, res_ref, n_ref, c_ref, r_ref, gain_ref, w_ref, rg_ref, low_ref, lg_ref, gg_ref, all_ref, p_ref, local, send, recv
):
    z = lax.axis_index("ctx")
    width = res_ref.shape[1]
    barrier = pltpu.get_barrier_semaphore()
    for k in (1, 2, 3):
        pl.semaphore_signal(barrier, inc=1, device_id={"ctx": (z + k) % 4}, device_id_type=MESH)
    pl.semaphore_wait(barrier, 3)
    gain = gain_ref[...]
    gain_grad = jnp.zeros(gain.shape, F32)
    columns = p_ref.shape[3]

    def to(c, side):
        return pltpu.make_async_remote_copy(
            src_ref=p_ref.at[side, c],
            dst_ref=all_ref.at[2 * z + side],
            send_sem=send.at[side, c],
            recv_sem=recv.at[side, z],
            device_id={"ctx": c},
            device_id_type=MESH,
        )

    def back_from(c, side):
        return pltpu.make_async_remote_copy(
            src_ref=p_ref.at[side, c],
            dst_ref=all_ref.at[2 * c + side],
            send_sem=send.at[side, c],
            recv_sem=recv.at[side, c],
            device_id={"ctx": c},
            device_id_type=MESH,
        )

    own = [
        pltpu.make_async_copy(p_ref.at[side, z], all_ref.at[2 * z + side], local.at[side])
        for side in (0, 1)
    ]
    for side in (0, 1):
        rows = slice(side * SPAN, (side + 1) * SPAN)
        named = c_ref[rows, width:].astype(F32) > 0.5
        logits = jnp.dot(n_ref[rows, :], r_ref[...], preferred_element_type=F32)
        logits = jnp.where(named, logits, -1e30)
        exponent = jnp.where(
            named, jnp.exp(logits - jnp.max(logits, axis=1, keepdims=True)), 0.0
        )
        gates = exponent / jnp.sum(exponent, axis=1, keepdims=True)
        found = g_ref[rows, width:].astype(F32)
        logit_grads = (gates * (found - jnp.sum(gates * found, axis=1, keepdims=True))).astype(BF)
        lg_ref[rows, :] = logit_grads
        grads = g_ref[rows, :width].astype(F32) + lax.dot_general(
            logit_grads, r_ref[...], NT, preferred_element_type=F32
        )
        residual = res_ref[rows, :]
        inverse = inverse_rms(residual)
        gain_grad = gain_grad + jnp.sum(grads * residual * inverse, axis=0, keepdims=True)
        scaled = gain * grads
        cube = inverse * inverse * inverse / width
        total = (
            c_ref[rows, :width].astype(F32)
            + inverse * scaled
            - residual * cube * jnp.sum(scaled * residual, axis=1, keepdims=True)
        )
        rg_ref[rows, :] = total
        low = total.astype(BF)
        low_ref[rows, :] = low
        attended = jnp.dot(low, w_ref[...], preferred_element_type=F32).astype(BF)
        for c in range(4):
            p_ref[side, c] = attended[:, c * columns : (c + 1) * columns]
        for c in range(4):

            @pl.when(z != c)
            def _():
                to(c, side).start()

        own[side].start()
    gg_ref[...] = gain_grad
    for side in (0, 1):
        own[side].wait()
        for c in range(4):

            @pl.when(z != c)
            def _():
                to(c, side).wait_send()
                back_from(c, side).wait_recv()


def residual_back(grad, residual, normed, cot, router, gain, w):
    rows, width = residual.shape
    columns = w.shape[1] // 4
    vmem = pl.BlockSpec(memory_space=pltpu.VMEM)
    return pl.pallas_call(
        residual_back_kernel,
        in_specs=[vmem] * 7,
        out_specs=[vmem] * 4 + [pl.BlockSpec(memory_space=pl.ANY)],
        out_shape=[
            jax.ShapeDtypeStruct((rows, width), F32),
            jax.ShapeDtypeStruct((rows, width), BF),
            jax.ShapeDtypeStruct((rows, LANES), BF),
            jax.ShapeDtypeStruct((1, width), F32),
            jax.ShapeDtypeStruct((8, SPAN, columns), BF),
        ],
        scratch_shapes=[
            pltpu.VMEM((2, 4, SPAN, columns), BF),
            pltpu.SemaphoreType.DMA((2,)),
            pltpu.SemaphoreType.DMA((2, 4)),
            pltpu.SemaphoreType.DMA((2, 4)),
        ],
        compiler_params=params(collective_id=4, has_side_effects=True),
        cost_estimate=LIGHT,
    )(grad, residual, normed, cot, router, gain, w)


def joint_back_kernel(
    dq_ref, dk_ref, dv_ref, cos_ref, sin_ref, w_ref, tok_ref, gain_ref, rg_ref,
    jg_ref, in_ref, gg_ref, land_ref, a_ref, p_ref, o_ref, send, recv, core_send, core_recv,
):
    z, t = lax.axis_index("ctx"), lax.axis_index("tp")
    core = {"tp": 1 - t}
    barrier = pltpu.get_barrier_semaphore()
    for partner in [{"ctx": (z + k) % 4} for k in (1, 2, 3)] + [core]:
        pl.semaphore_signal(barrier, inc=1, device_id=partner, device_id_type=MESH)
    pl.semaphore_wait(barrier, 4)
    columns = jg_ref.shape[2]
    rows_here = jg_ref.shape[1]

    def to(c):
        return pltpu.make_async_remote_copy(
            src_ref=jg_ref.at[c],
            dst_ref=land_ref.at[z],
            send_sem=send.at[c],
            recv_sem=recv.at[z],
            device_id={"ctx": c},
            device_id_type=MESH,
        )

    def back_from(c):
        return pltpu.make_async_remote_copy(
            src_ref=jg_ref.at[c],
            dst_ref=land_ref.at[c],
            send_sem=send.at[c],
            recv_sem=recv.at[c],
            device_id={"ctx": c},
            device_id_type=MESH,
        )

    for c in range(4):
        rows = slice(c * rows_here, (c + 1) * rows_here)
        cos, sin = cos_ref[rows, :], sin_ref[rows, :]
        a = jnp.concatenate([dq_ref[0, rows, :], dq_ref[1, rows, :]], axis=1)
        b = jnp.concatenate([dq_ref[2, rows, :], dk_ref[rows, :]], axis=1)
        jg_ref[c, :, :LANES] = (a * cos + half_turn(a, True) * sin).astype(BF)
        jg_ref[c, :, LANES : 2 * LANES] = (b * cos + half_turn(b, True) * sin).astype(BF)
        jg_ref[c, :, 2 * LANES :] = dv_ref[rows, :].astype(BF)

        @pl.when(z != c)
        def _():
            to(c).start()

    for c in range(4):
        place = slice(c * columns, (c + 1) * columns)

        @pl.when(z == c)
        def _():
            a_ref[:, place] = jg_ref[c]

        @pl.when(z != c)
        def _():
            back_from(c).wait_recv()
            a_ref[:, place] = land_ref[c]

    sent = []
    for side in (0, 1):
        rows = slice(side * SPAN, (side + 1) * SPAN)
        p_ref[side] = lax.dot_general(
            a_ref[rows, :], w_ref[...], NT, preferred_element_type=F32
        ).astype(BF)
        made = pltpu.make_async_remote_copy(
            src_ref=p_ref.at[side],
            dst_ref=o_ref.at[side],
            send_sem=core_send.at[side],
            recv_sem=core_recv.at[side],
            device_id=core,
            device_id_type=MESH,
        )
        made.start()
        sent.append(made)
    gain = gain_ref[...]
    width = gain.shape[1]
    gain_grad = jnp.zeros(gain.shape, F32)
    for side in (0, 1):
        rows = slice(side * SPAN, (side + 1) * SPAN)
        sent[side].wait_recv()
        grads = p_ref[side].astype(F32) + o_ref[side].astype(F32)
        tokens = tok_ref[rows, :].astype(F32)
        inverse = inverse_rms(tokens)
        gain_grad = gain_grad + jnp.sum(grads * tokens * inverse, axis=0, keepdims=True)
        scaled = gain * grads
        cube = inverse * inverse * inverse / width
        in_ref[rows, :] = (
            rg_ref[rows, :]
            + inverse * scaled
            - tokens * cube * jnp.sum(scaled * tokens, axis=1, keepdims=True)
        )
    gg_ref[...] = gain_grad
    for made in sent:
        made.wait_send()
    for c in range(4):

        @pl.when(z != c)
        def _():
            to(c).wait_send()


def joint_back(dq, dk, dv, cos, sin, w, tokens, gain, grads):
    rows, width = tokens.shape
    columns = (GROUP + 2) * HEAD_SIZE
    vmem = pl.BlockSpec(memory_space=pltpu.VMEM)
    return pl.pallas_call(
        joint_back_kernel,
        in_specs=[vmem] * 9,
        out_specs=[vmem] * 3,
        out_shape=[
            jax.ShapeDtypeStruct((4, rows, columns), BF),
            jax.ShapeDtypeStruct((rows, width), F32),
            jax.ShapeDtypeStruct((1, width), F32),
        ],
        scratch_shapes=[
            pltpu.VMEM((4, rows, columns), BF),
            pltpu.VMEM((rows, 4 * columns), BF),
            pltpu.VMEM((2, SPAN, width), BF),
            pltpu.VMEM((2, SPAN, width), BF),
            pltpu.SemaphoreType.DMA((4,)),
            pltpu.SemaphoreType.DMA((4,)),
            pltpu.SemaphoreType.DMA((2,)),
            pltpu.SemaphoreType.DMA((2,)),
        ],
        compiler_params=params(collective_id=5, has_side_effects=True),
        cost_estimate=LIGHT,
    )(dq, dk, dv, cos, sin, w, tokens, gain, grads)


def owner_of(f, k):
    return [f, f + 1 - 2 * (f % 2), (f + 2) % 4, 3 - f][k]


def expert_kernel(count, pieces, n_ref, cot_ref, one_ref, two_ref, r_ref, w_any, shard_ref, *refs):
    pre_ref, wh_ref = refs[:2]
    x_parts, cot_parts = refs[2 : 2 + pieces], refs[2 + pieces : 2 + 2 * pieces]
    grad_any, joint_ref, out_any, far_any = refs[2 + 2 * pieces : 6 + 2 * pieces]
    x_ref, c_ref, w_ref, part_ref, there_ref, back_ref, full_ref = refs[6 + 2 * pieces : -7]
    out_ref, out_there, out_near = refs[-7:-4]
    local, wrote, send, recv = refs[-4:]
    i = pl.program_id(0)
    z, t, f = lax.axis_index("ctx"), lax.axis_index("tp"), lax.axis_index("fsdp")
    z1, z2, z3 = z + 1 - 2 * (z % 2), (z + 2) % 4, 3 - z
    near, far, third, core = {"ctx": z1}, {"ctx": z2}, {"ctx": z3}, {"tp": 1 - t}
    half, width = x_ref.shape[1:]
    piece = width // pieces
    hidden_columns = wh_ref.shape[1]
    units = hidden_columns // count

    def rows(side):
        return pl.ds(pl.multiple_of(side * half, half), half)

    def remote(k, source, target, device):
        return pltpu.make_async_remote_copy(
            src_ref=source,
            dst_ref=target,
            send_sem=send.at[k],
            recv_sem=recv.at[k],
            device_id=device,
            device_id_type=MESH,
        )

    own = n_ref.at[rows(t)]
    x_one = remote(0, own, x_ref.at[2], near)
    x_two = remote(1, own, x_ref.at[4], far)
    x_three = remote(2, x_ref.at[4], x_ref.at[6], near)
    c_three = remote(3, two_ref, c_ref.at[6], near)
    x_swaps = [None] + [remote(3 + m, x_ref.at[2 * m], x_ref.at[2 * m + 1], core) for m in (1, 2, 3)]
    c_swaps = [
        None,
        remote(7, one_ref, c_ref.at[3], core),
        remote(8, two_ref, c_ref.at[5], core),
        remote(9, c_ref.at[6], c_ref.at[7], core),
    ]
    crossed = [remote(10 + m, part_ref.at[2 * m + 1], there_ref.at[m], core) for m in range(4)]
    returned = [None] + [
        remote(13 + m, part_ref.at[2 * m], back_ref.at[m], device)
        for m, device in ((1, near), (2, far), (3, third))
    ]
    out_crossed = [
        remote(22 + m, out_ref.at[2 * m + 1], out_there.at[m], core) for m in range(4)
    ]
    out_sent = [remote(26 + n, out_ref.at[4 * n + 2], out_near.at[n], near) for n in (0, 1)]
    out_stores = [
        pltpu.make_async_copy(out_ref.at[0], out_any, local.at[9]),
        pltpu.make_async_copy(out_ref.at[4], far_any, local.at[10]),
    ]
    last = remote(17, full_ref.at[rows(t)], full_ref.at[rows(t)], core)
    loads = [
        pltpu.make_async_copy(source, target, local.at[k])
        for k, (source, target) in enumerate(
            (
                (n_ref.at[rows(t)], x_ref.at[0]),
                (n_ref.at[rows(1 - t)], x_ref.at[1]),
                (cot_ref.at[rows(t)], c_ref.at[0]),
                (cot_ref.at[rows(1 - t)], c_ref.at[1]),
                (w_any, w_ref),
                (one_ref, c_ref.at[2]),
                (two_ref, c_ref.at[4]),
            )
        )
    ]
    store = pltpu.make_async_copy(full_ref, grad_any, local.at[7])
    carried = []
    if pieces > 1:
        shard_rows = shard_ref.shape[0]
        cut = shard_rows // 2
        f1, f2 = owner_of(f, 1), owner_of(f, 2)

        def held(place, first, size):
            return joint_ref.at[pl.ds(pl.multiple_of(place * shard_rows + first, 8), size)]

        own_shard = pltpu.make_async_copy(shard_ref, held(f, 0, shard_rows), local.at[8])
        joint_one = remote(18, shard_ref, held(f, 0, shard_rows), {"fsdp": f1})
        joint_two = remote(19, shard_ref, held(f, 0, shard_rows), {"fsdp": f2})
        later = shard_rows - cut
        on_one = remote(20, held(f1, 0, cut), held(f1, 0, cut), {"fsdp": f2})
        on_two = remote(21, held(f2, cut, later), held(f2, cut, later), {"fsdp": f1})
        carried = [joint_one, joint_two, on_one, on_two]

    def keep(step):
        made = []
        at_rows = pl.ds(pl.multiple_of(step * half, half), half)
        for k in range(pieces):
            owner = [f, f + 1 - 2 * (f % 2), (f + 2) % 4, 3 - f][k] if pieces > 1 else 0
            at = pl.ds(pl.multiple_of(owner * piece, piece), piece)
            for n, (source, target) in enumerate(((x_ref, x_parts[k]), (c_ref, cot_parts[k]))):
                made.append(
                    pltpu.make_async_copy(
                        source.at[step, :, at], target.at[at_rows], wrote.at[step, 2 * k + n]
                    )
                )
        return made

    def finish(m):
        crossed[m].wait_recv()
        part_ref[2 * m] = (part_ref[2 * m].astype(F32) + there_ref[m].astype(F32)).astype(BF)
        if m:
            returned[m].start()

    def finish_out(m):
        out_crossed[m].wait_recv()
        out_ref[2 * m] = (out_ref[2 * m].astype(F32) + out_there[m].astype(F32)).astype(BF)
        if m % 2:
            out_sent[m // 2].start()

    @pl.when(i == 0)
    def _():
        partners = [near, far, third, core]
        if carried:
            partners += [{"fsdp": f1}, {"fsdp": f2}]
        barrier = pltpu.get_barrier_semaphore()
        for partner in partners:
            pl.semaphore_signal(barrier, inc=1, device_id=partner, device_id_type=MESH)
        pl.semaphore_wait(barrier, len(partners))
        if carried:
            joint_one.start()
            joint_two.start()
            own_shard.start()
        for made in [x_one, x_two] + loads + [c_swaps[1], c_swaps[2], c_three]:
            made.start()
        for made in (loads[0], loads[2], loads[4]):
            made.wait()

    @pl.when(i == 1)
    def _():
        loads[1].wait()
        loads[3].wait()

    @pl.when(i == 2)
    def _():
        x_one.wait_recv()
        x_swaps[1].start()
        loads[5].wait()

    @pl.when(i == 3)
    def _():
        x_swaps[1].wait_recv()
        c_swaps[1].wait_recv()

    @pl.when(i == 4)
    def _():
        x_two.wait_recv()
        x_three.start()
        x_swaps[2].start()
        loads[6].wait()

    @pl.when(i == 5)
    def _():
        x_swaps[2].wait_recv()
        c_swaps[2].wait_recv()

    @pl.when(i == 6)
    def _():
        finish(2)
        x_three.wait_recv()
        x_swaps[3].start()
        c_three.wait_recv()
        c_swaps[3].start()

        if carried:
            joint_one.wait_recv()
            on_one.start()
            joint_two.wait_recv()
            on_two.start()

    @pl.when(i == 7)
    def _():
        x_swaps[3].wait_recv()
        c_swaps[3].wait_recv()

    for made in keep(i):
        made.start()

    def columns(j, e):
        return slice(j * hidden_columns + e * units, j * hidden_columns + (e + 1) * units)

    x = x_ref[i]
    both = c_ref[i]
    cot = both[:, :width]
    named = both[:, width:].astype(F32) > 0.5
    logits = jnp.where(named, jnp.dot(x, r_ref[...], preferred_element_type=F32), -1e30)
    top = jnp.max(logits, axis=1, keepdims=True)
    exponent = jnp.where(named, jnp.exp(logits - top), 0.0)
    gates = exponent / jnp.sum(exponent, axis=1, keepdims=True)
    lane = lax.broadcasted_iota(jnp.int32, gates.shape, 1)
    found = jnp.zeros(gates.shape, F32)
    for e in range(count):
        mine = lane == z * count + e
        gate_here = jnp.sum(jnp.where(mine, gates, 0.0), axis=1, keepdims=True)
        g = jnp.dot(x, w_ref[:, columns(0, e)], preferred_element_type=F32)
        u = jnp.dot(x, w_ref[:, columns(1, e)], preferred_element_type=F32)
        hg = jnp.dot(cot, w_ref[:, columns(2, e)], preferred_element_type=F32)
        s = 1.0 / (1.0 + jnp.exp(-g))
        gs = g * s
        h = (gs * u).astype(BF).astype(F32)
        found = found + jnp.where(mine, jnp.sum(h * hg, axis=1, keepdims=True), 0.0)
        wh_ref[:, columns(0, e)] = (h * gate_here).astype(BF)
        hg = hg * gate_here
        pre_ref[:, columns(0, e)] = (hg * u * s * (1.0 + g * (1.0 - s))).astype(BF)
        pre_ref[:, columns(1, e)] = (hg * gs).astype(BF)
    part_ref[i, :, width:] = found.astype(BF)
    part_ref[i, :, :width] = lax.dot_general(
        pre_ref[...], w_ref[:, : 2 * hidden_columns], NT, preferred_element_type=F32
    ).astype(BF)
    for m in range(4):

        @pl.when(i == 2 * m + 1)
        def _():
            crossed[m].start()

    out_ref[i] = lax.dot_general(
        wh_ref[...], w_ref[:, 2 * hidden_columns :], NT, preferred_element_type=F32
    ).astype(BF)
    for m in range(4):

        @pl.when(i == 2 * m + 1)
        def _():
            out_crossed[m].start()

    for m in range(2):

        @pl.when(i == 2 * m + 2)
        def _():
            finish(m)

    @pl.when(i == 6)
    def _():
        finish_out(1)

    @pl.when(i == 7)
    def _():
        finish(3)
        for m in (3, 0, 2):
            finish_out(m)
        total = part_ref[0].astype(F32)
        for m in (1, 2, 3):
            returned[m].wait_recv()
            total = total + back_ref[m].astype(F32)
        full_ref[rows(t), :] = total.astype(BF)
        last.start()
        for n in (0, 1):
            out_sent[n].wait_recv()
            out_ref[4 * n] = (out_ref[4 * n].astype(F32) + out_near[n].astype(F32)).astype(BF)
            out_stores[n].start()
        for made in out_crossed + out_sent:
            made.wait_send()
        for made in out_stores:
            made.wait()
        for made in [x_one, x_two, x_three, c_three] + x_swaps[1:] + c_swaps[1:] + crossed:
            made.wait_send()
        for made in returned[1:]:
            made.wait_send()
        last.wait_send()
        last.wait_recv()
        store.start()
        if carried:
            on_one.wait_recv()
            on_two.wait_recv()
            for made in carried:
                made.wait_send()
            own_shard.wait()

        def settle(step, carried):
            for made in keep(step):
                made.wait()
            return carried

        lax.fori_loop(0, 8, settle, 0)
        store.wait()


def experts(pieces, normed, cot, one, two, router, w, shard, count):
    rows, width = normed.shape
    half = rows // 2
    packed = cot.shape[1]
    hidden_columns = w.shape[1] // 3
    slot = lambda n: pl.BlockSpec((half, n), lambda i: (i, 0))
    anywhere = pl.BlockSpec(memory_space=pl.ANY)
    blocks = [2 * hidden_columns, hidden_columns]
    return pl.pallas_call(
        functools.partial(expert_kernel, count, pieces),
        grid=(8,),
        in_specs=[anywhere] * 4 + [pl.BlockSpec(router.shape, lambda i: (0, 0)), anywhere, anywhere],
        out_specs=[slot(n) for n in blocks] + [anywhere] * (2 * pieces + 4),
        out_shape=[
            jax.ShapeDtypeStruct((8 * half, n), BF) for n in blocks + [width // pieces] * (2 * pieces)
        ]
        + [
            jax.ShapeDtypeStruct((rows, packed), BF),
            jax.ShapeDtypeStruct((pieces * shard.shape[0], shard.shape[1]), BF),
            jax.ShapeDtypeStruct((half, width), BF),
            jax.ShapeDtypeStruct((half, width), BF),
        ],
        scratch_shapes=[
            pltpu.VMEM((8, half, width), BF),
            pltpu.VMEM((8, half, packed), BF),
            pltpu.VMEM(w.shape, BF),
            pltpu.VMEM((8, half, packed), BF),
            pltpu.VMEM((4, half, packed), BF),
            pltpu.VMEM((4, half, packed), BF),
            pltpu.VMEM((rows, packed), BF),
            pltpu.VMEM((8, half, width), BF),
            pltpu.VMEM((4, half, width), BF),
            pltpu.VMEM((2, half, width), BF),
            pltpu.SemaphoreType.DMA((11,)),
            pltpu.SemaphoreType.DMA((8, 2 * pieces)),
            pltpu.SemaphoreType.DMA((28,)),
            pltpu.SemaphoreType.DMA((28,)),
        ],
        compiler_params=params(collective_id=1, has_side_effects=True),
        cost_estimate=LIGHT,
    )(normed, cot, one, two, router, w, shard)


def adamw(master, first_moment, second_moment, gradient, rate, decay):
    moment_new = 0.9 * first_moment + 0.1 * gradient
    square_new = 0.95 * second_moment + 0.05 * gradient * gradient
    corrected = moment_new / (1.0 - 0.9**STEP) / (jnp.sqrt(square_new / (1.0 - 0.95**STEP)) + 1e-08)
    master_new = master - rate * (corrected + decay * master)
    return (master_new, moment_new, square_new, master_new.astype(BF))


def expert_adamw_kernel(rate, joined, *refs):
    p_ref, f_ref, s_ref, g_ref = refs[:4]
    master_ref, moment_ref, rounded_ref, square_ref, grad_ref = refs[-5:]
    parts, _, columns = g_ref.shape
    units = p_ref.shape[3]
    each = columns // units
    for k in range(parts):
        for e in range(each):
            grad_ref[:, k * each + e, :] = g_ref[k, :, e * units : (e + 1) * units].astype(F32)
    for at in range(0, parts * each, 8):
        rows = slice(at, at + 8)
        new = adamw(
            p_ref[:, 0, rows], f_ref[:, 0, rows], s_ref[:, 0, rows], grad_ref[:, rows], rate, 0.1
        )
        master_ref[:, 0, rows] = new[0]
        moment_ref[:, 0, rows] = new[1]
        rounded_ref[:, 0, rows] = new[3]
        if joined:
            square_ref[:, rows, 0] = refs[4][:, rows]
            square_ref[:, rows, 1] = new[2]
        else:
            square_ref[:, rows] = new[2]


def expert_adamw(slot, rate, weight, first, second, gradient, earlier, joined=None):
    rows, _, count, units = weight.shape
    parts = gradient.shape[0]
    tile = next(t for t in (32, 16, 8) if rows % t == 0)
    here = pl.BlockSpec((tile, 1, count, units), lambda i: (i, slot, 0, 0))
    plain = pl.BlockSpec((tile, count, units), lambda i: (i, 0, 0))
    pair = pl.BlockSpec((tile, count, 2, units), lambda i: (i, 0, 0, 0))
    shape = jax.ShapeDtypeStruct(weight.shape, F32)
    chained = len(earlier)
    more = [] if joined is None else [joined]
    square = (rows, count, units) if joined is None else (rows, count, 2, units)
    return pl.pallas_call(
        functools.partial(expert_adamw_kernel, rate, joined is not None),
        grid=(rows // tile,),
        in_specs=[here, here, here]
        + [pl.BlockSpec((parts, tile, gradient.shape[2]), lambda i: (0, i, 0))]
        + [plain] * len(more)
        + [pl.BlockSpec(memory_space=pl.ANY)] * chained,
        out_specs=[here, here, here, plain if joined is None else pair],
        out_shape=[
            shape,
            shape,
            jax.ShapeDtypeStruct(weight.shape, BF),
            jax.ShapeDtypeStruct(square, F32),
        ],
        scratch_shapes=[pltpu.VMEM((tile, count, units), F32)],
        input_output_aliases={4 + len(more) + k: k for k in range(chained)},
        compiler_params=params(),
        cost_estimate=pl.CostEstimate(
            flops=20 * rows * count * units,
            bytes_accessed=45 * rows * count * units,
            transcendentals=rows * count * units,
        ),
    )(weight, first, second, gradient, *more, *earlier)


def matrix_adamw_kernel(rate, p_ref, f_ref, s_ref, g_ref, *outs):
    grad = g_ref[...].astype(F32).T
    new = adamw(p_ref[...], f_ref[...], s_ref[...], grad, rate, 0.1)
    for ref, value in zip(outs, new):
        ref[...] = value


def matrix_adamw(rate, weight, first, second, turned):
    rows, columns = weight.shape
    if rows % LANES:
        return adamw(weight, first, second, turned[:columns].T.astype(F32), rate, 0.1)
    tile = 256
    here = pl.BlockSpec((rows, tile), lambda i: (0, i))
    shape = jax.ShapeDtypeStruct(weight.shape, F32)
    return pl.pallas_call(
        functools.partial(matrix_adamw_kernel, rate),
        grid=(columns // tile,),
        in_specs=[here, here, here, pl.BlockSpec((tile, rows), lambda i: (i, 0))],
        out_specs=[here] * 4,
        out_shape=[shape, shape, shape, jax.ShapeDtypeStruct(weight.shape, BF)],
        compiler_params=params(),
        cost_estimate=pl.CostEstimate(
            flops=20 * rows * columns, bytes_accessed=28 * rows * columns, transcendentals=0
        ),
    )(weight, first, second, turned)


def local(
    sizes,
    block_input,
    out_cotangent,
    block_ids,
    expert_routes,
    norm_gains,
    gains_first,
    gains_second,
    joint_weight,
    joint_first,
    joint_second,
    output_weight,
    output_first,
    output_second,
    router_weight,
    router_first,
    router_second,
    expert_weight,
    expert_first,
    expert_second,
):
    n_fsdp, n_ctx, n_tp = sizes
    z = lax.axis_index("ctx")
    t = lax.axis_index("tp")
    f = lax.axis_index("fsdp")
    tokens_low = block_input[0]
    cot_low = out_cotangent[0]
    count, width = tokens_low.shape
    half = count // n_tp
    length = n_ctx * count
    own_rows = width // n_fsdp
    each = E // n_ctx

    barrier = lax.optimization_barrier

    def beyond(x, m):
        return lax.ppermute(x, "ctx", [(i, i ^ m) for i in range(n_ctx)])

    def swap(x):
        return lax.ppermute(x, "tp", [(0, 1), (1, 0)])

    def across(x, m):
        return lax.ppermute(x, "fsdp", [(i, i ^ m) for i in range(n_fsdp)])

    def mine(x):
        return lax.dynamic_slice_in_dim(x, t * half, half, 0)

    def other(x):
        return lax.dynamic_slice_in_dim(x, (1 - t) * half, half, 0)

    def in_order(a, b):
        return jnp.where(t == 0, jnp.concatenate([a, b], 0), jnp.concatenate([b, a], 0))

    def put(buffer, x, place):
        return lax.dynamic_update_slice_in_dim(buffer, x[None], place, 0)

    def put_row(x, row, place):
        return lax.dynamic_update_slice(x, row[None], (place, 0))

    def take(x, place, places):
        return lax.dynamic_index_in_dim(
            x.reshape(places, x.shape[0] // places, x.shape[1]), place, 0, keepdims=False
        )

    def sent_to_owners(x):
        if n_fsdp != 4:
            return [lax.psum_scatter(x, "fsdp", scatter_dimension=1, tiled=True)]
        part = lambda k: lax.dynamic_slice_in_dim(x, (f ^ k) * own_rows, own_rows, 1)
        return [part(0)] + [across(part(k), k) for k in (1, 2, 3)]

    def added(came):
        return came[0] if len(came) == 1 else sum(x.astype(F32) for x in came).astype(BF)

    def spread(x):
        one, two = beyond(x, 1), beyond(x, 2)
        return {1: one, 2: two, 3: beyond(two, 1)}

    slots_first = jnp.transpose(expert_weight, (0, 2, 1, 3))
    units = expert_weight.shape[3]
    expert_part = (
        lax.dynamic_slice_in_dim(slots_first, z * each, each, 2)
        .astype(BF)
        .reshape(own_rows, 3 * each * units)
    )
    expert_full = lax.all_gather(expert_part, "fsdp", axis=0, tiled=True)

    group_columns = (GROUP + 2) * HEAD_SIZE
    head_columns = GROUP * HEAD_SIZE
    joint_low = joint_weight.astype(BF)
    output_columns = output_weight.shape[1]
    first_pack = jnp.concatenate(
        [
            router_weight.astype(BF),
            norm_gains.T.astype(BF),
            jnp.zeros((own_rows, LANES - E - 2), BF),
            lax.dynamic_slice_in_dim(joint_low, z * group_columns, group_columns, 1),
        ],
        axis=1,
    )
    first_pack, _ = barrier((first_pack, expert_part))
    sequence, first_full = first_gather(n_ctx, n_fsdp, tokens_low, first_pack)
    small_full = first_full[:, :LANES]
    router_full = small_full[:, :E]
    router_wide = jnp.where(jnp.arange(LANES)[None, :] < E, small_full, jnp.zeros((), BF))
    gain_first = small_full[:, E].astype(F32)[None, :]
    gain_second = small_full[:, E + 1].astype(F32)[None, :]

    route_rows = expert_routes[0]
    lane_row = jnp.arange(LANES, dtype=jnp.int32)[None, :]
    member = sum((route_rows[:, k : k + 1] == lane_row).astype(F32) for k in range(route_rows.shape[1]))
    cot_pack = jnp.concatenate([cot_low, member.astype(BF)], axis=1)
    cot_half, sequence = barrier((mine(cot_pack), sequence))
    cot_came = [beyond(cot_half, 1), beyond(cot_half, 2)]

    lanes = jnp.arange(LANES, dtype=jnp.int32) % (HEAD_SIZE // 2)
    frequency = jnp.exp(lanes.astype(F32) * (-2.0 * math.log(10000.0) / HEAD_SIZE))
    fine = 64
    small_angles = jnp.arange(fine, dtype=jnp.int32).astype(F32)[:, None] * frequency
    large_angles = (fine * jnp.arange(length // fine, dtype=jnp.int32)).astype(F32)[:, None] * frequency
    cos_a, sin_a = jnp.cos(large_angles)[:, None], jnp.sin(large_angles)[:, None]
    cos_b, sin_b = jnp.cos(small_angles)[None], jnp.sin(small_angles)[None]
    cosine = (cos_a * cos_b - sin_a * sin_b).reshape(length, LANES)
    sine = (sin_a * cos_b + cos_a * sin_b).reshape(length, LANES)
    cosine, sine, tokens_low = barrier((cosine, sine, tokens_low))
    id_row = block_ids
    id_column = block_ids.reshape(length, 1)
    normed_all, queries, keys, values = project(sequence, gain_first, first_full, cosine, sine)
    output_low = output_weight.astype(BF)
    attended_all, lse, attended_here, output_full = attend(
        n_fsdp, id_column, id_row, queries, keys, values, output_low
    )
    if n_fsdp != 4:
        output_full = lax.all_gather(output_low, "fsdp", axis=0, tiled=True)
    residual, normed_second, attended = project_out(
        attended_here, output_full, tokens_low, gain_second
    )

    pieces = n_fsdp if n_fsdp == 4 else 1
    pre_all, hidden_all, *kept, grad_rows, joint_full, out_here, out_two = experts(
        pieces, normed_second, cot_pack, *cot_came, router_wide, expert_full, joint_low, each
    )
    if pieces == 1:
        joint_full = lax.all_gather(joint_low, "fsdp", axis=0, tiled=True)
    x_parts, cot_parts = kept[:pieces], kept[pieces:]

    wide = each * units

    def expert_terms(j):
        left = cot_parts if j == 2 else x_parts
        right = hidden_all if j == 2 else pre_all[:, j * wide : (j + 1) * wide]
        return [
            lax.dot_general(left[k], right, TN, preferred_element_type=F32).astype(BF)
            for k in range(pieces)
        ]

    terms = {j: expert_terms(j) for j in (2, 0, 1)}
    pieces_came = {}
    for j in (2, 0, 1):
        if pieces > 1:
            pieces_came[j] = [terms[j][0]] + [across(terms[j][k], k) for k in range(1, pieces)]
        else:
            pieces_came[j] = [
                lax.psum_scatter(terms[j][0], "fsdp", scatter_dimension=0, tiled=True)
            ]

    def gathered(came):
        return lax.all_gather(added(came), "ctx", axis=0, tiled=False)

    grad_rows, terms[2] = barrier((grad_rows, terms[2]))
    residual_grads, residual_low, logit_grads, gain_second_grad, attended_grads_all = residual_back(
        grad_rows, residual, normed_second, cot_pack, router_wide, gain_second, output_full
    )
    attended_grads_all, pieces_came[2], *_ = barrier(
        (attended_grads_all, pieces_came[2], terms[0], terms[1])
    )
    expert_sums = {2: gathered(pieces_came[2])}
    step = 64
    few_rows = jnp.concatenate([logit_grads[:, :E], jnp.zeros((count, step - E), BF)], axis=1)
    rest_term = jnp.concatenate(
        [
            lax.dot_general(attended, residual_low, TN, preferred_element_type=F32).astype(BF),
            lax.dot_general(few_rows, normed_second, TN, preferred_element_type=F32).astype(BF),
        ],
        axis=0,
    )
    rest_term = lax.dynamic_update_slice(
        rest_term, gain_second_grad.astype(BF), (output_columns + E, 0)
    )
    rest_term, attended_grads_all = barrier((rest_term, attended_grads_all))
    dq, dk, dv = attend_back(
        id_column,
        id_row,
        queries,
        keys,
        values,
        attended_all,
        attended_grads_all.reshape(length, head_columns),
        lse,
    )
    dq, pieces_came[0] = barrier((dq, pieces_came[0]))
    expert_sums[0] = gathered(pieces_came[0])
    joint_grads, input_rows, gain_first_grad = joint_back(
        dq, dk, dv, cosine, sine, joint_full, tokens_low, gain_first, residual_grads
    )
    joint_grads, pieces_came[1], rest_term, out_two = barrier(
        (joint_grads, pieces_came[1], rest_term, out_two)
    )
    out_far = beyond(out_two, 2)
    expert_sums[1] = gathered(pieces_came[1])
    joint_grads_all = joint_grads.reshape(length, group_columns)

    first_view = jnp.transpose(expert_first, (0, 2, 1, 3))
    second_view = jnp.transpose(expert_second, (0, 2, 1, 3))
    made = []
    squares = {}

    def expert_step(j, joined=None):
        rate = 0.25 if j == 2 else 0.03
        *made[:], squares[j] = expert_adamw(
            j, rate, slots_first, first_view, second_view, expert_sums[j], tuple(made), joined
        )

    joint_term = lax.dot_general(joint_grads_all, normed_all, TN, preferred_element_type=F32)
    joint_term = jnp.concatenate(
        [
            joint_term.astype(BF),
            jnp.where(jnp.arange(16)[:, None] == 0, gain_first_grad, 0.0).astype(BF),
            rest_term,
        ],
        axis=0,
    )
    joint_came = sent_to_owners(joint_term)

    expert_step(2)
    joint_came, made[:], squares[2] = barrier((joint_came, made, squares[2]))
    joint_owned = added(joint_came)
    rest_owned = put_row(
        joint_owned[group_columns + 16 :], joint_owned[group_columns], output_columns + E + 1
    )
    joint_owned = joint_owned[:group_columns]
    rest_parts = [take(rest_owned, z, n_ctx)]
    rest_parts += [beyond(take(rest_owned, z ^ m, n_ctx), m) for m in range(1, n_ctx)]
    expert_step(0)
    rest_parts, made[:], squares[0] = barrier((rest_parts, made, squares[0]))
    rest_low = sum(x.astype(F32) for x in rest_parts).astype(BF)
    both = jnp.concatenate([joint_owned, rest_low], axis=0)
    both_all = {0: both, **spread(both)}
    expert_step(1, squares[0])
    both_all, out_far, made[:] = barrier((both_all, out_far, made))
    full = jnp.zeros((n_ctx, *both.shape), BF)
    for m, got in both_all.items():
        full = put(full, got, z ^ m)
    joint_sum = full[:, :group_columns].reshape(n_ctx * group_columns, own_rows)
    rest_full = full[:, group_columns:].reshape(output_columns + step, own_rows)
    moe_low = (out_here.astype(F32) + out_far.astype(F32)).astype(BF)
    moe_rows = in_order(moe_low, swap(moe_low)).astype(F32)
    block_output = (residual + moe_rows).astype(BF)[None]
    router_sum = rest_full[output_columns : output_columns + E].T.astype(F32)
    gains_sum = jnp.stack(
        [rest_full[output_columns + E + 1], rest_full[output_columns + E]]
    ).astype(F32)

    gains_new = adamw(norm_gains, gains_first, gains_second, gains_sum, 0.6, 0.0)
    joint_new = matrix_adamw(0.03, joint_weight, joint_first, joint_second, joint_sum)
    output_new = matrix_adamw(0.25, output_weight, output_first, output_second, rest_full)
    router_new = adamw(router_weight, router_first, router_second, router_sum, 0.015, 0.1)

    back = lambda x: jnp.transpose(x, (0, 2, 1, 3))
    return (
        block_output,
        input_rows[None],
        *gains_new,
        *joint_new,
        *output_new,
        *router_new,
        back(made[0]),
        back(made[1]),
        squares[1],
        squares[2],
        back(made[2]),
    )


def solution(mesh):
    rows = P("fsdp", "ctx", None)
    gains = P(None, "fsdp")
    matrix = P("fsdp", "tp")
    router = P("fsdp", None)
    expert = P("fsdp", None, None, "tp")
    sizes = (mesh.shape["fsdp"], mesh.shape["ctx"], mesh.shape["tp"])
    return jax.shard_map(
        functools.partial(local, sizes),
        mesh=mesh,
        in_specs=(rows, rows, P("fsdp", None), rows)
        + (gains,) * 3
        + (matrix,) * 6
        + (router,) * 3
        + (expert,) * 3,
        out_specs=(rows, rows)
        + (gains,) * 4
        + (matrix,) * 8
        + (router,) * 4
        + (expert, expert, expert, P("fsdp", None, "tp"), expert),
        check_vma=False,
    )
```

```python
import functools
import math

import jax
import jax.numpy as jnp
from jax import lax
from jax.experimental import pallas as pl
from jax.experimental.pallas import tpu as pltpu
from jax.sharding import PartitionSpec as P

QUERY_HEADS = 24
KEY_VALUE_HEADS = 8
HEAD_SIZE = 64
GROUP = QUERY_HEADS // KEY_VALUE_HEADS
E = 16
STEP = 10
SPAN = 256
LANES = 128
BF = jnp.bfloat16
F32 = jnp.float32
NT = (((1,), (1,)), ((), ()))
TN = (((0,), (0,)), ((), ()))
VMEM_LIMIT = 58 * 1024 * 1024
LIGHT = pl.CostEstimate(flops=10**9, bytes_accessed=10**6, transcendentals=0)
MESH = pl.DeviceIdType.MESH


def params(**more):
    return pltpu.CompilerParams(vmem_limit_bytes=VMEM_LIMIT, **more)


def inverse_rms(rows):
    return lax.rsqrt(jnp.mean(rows * rows, axis=-1, keepdims=True) + 1e-06)


def half_turn(x, inverse):
    lane = lax.broadcasted_iota(jnp.int32, x.shape, 1)
    first = (lane % HEAD_SIZE) < HEAD_SIZE // 2
    later = pltpu.roll(x, LANES - HEAD_SIZE // 2, 1)
    sooner = pltpu.roll(x, HEAD_SIZE // 2, 1)
    return jnp.where(first, later, -sooner) if inverse else jnp.where(first, -later, sooner)


def first_gather_kernel(weights, tok_ref, pack_ref, seq_ref, full_ref, local, send, recv):
    z, t, f = lax.axis_index("ctx"), lax.axis_index("tp"), lax.axis_index("fsdp")
    half = tok_ref.shape[0] // 2
    rows = pack_ref.shape[0]
    z1, z2, z3 = z + 1 - 2 * (z % 2), (z + 2) % 4, 3 - z
    near, far, core = {"ctx": z1}, {"ctx": z2}, {"tp": 1 - t}
    partners = [near, far, core]
    if weights:
        f1, f2 = f + 1 - 2 * (f % 2), (f + 2) % 4
        f3 = 3 - f
        partners += [{"fsdp": f1}, {"fsdp": f2}]
    barrier = pltpu.get_barrier_semaphore()
    for partner in partners:
        pl.semaphore_signal(barrier, inc=1, device_id=partner, device_id_type=MESH)
    pl.semaphore_wait(barrier, len(partners))

    def at(chunk, side):
        return seq_ref.at[pl.ds(pl.multiple_of((chunk * 2 + side) * half, half), half)]

    def held(owner, first, size):
        start = pl.multiple_of(owner * rows + first, 8)
        return full_ref.at[pl.ds(start, size)]

    def copy(k, source, target, device):
        made = pltpu.make_async_remote_copy(
            src_ref=source,
            dst_ref=target,
            send_sem=send.at[k],
            recv_sem=recv.at[k],
            device_id=device,
            device_id_type=MESH,
        )
        made.start()
        return made

    own_half = tok_ref.at[pl.ds(pl.multiple_of(t * half, half), half)]
    one = copy(0, own_half, at(z, t), near)
    two = copy(1, own_half, at(z, t), far)
    here = pltpu.make_async_copy(
        tok_ref, seq_ref.at[pl.ds(pl.multiple_of(z * 2 * half, half), 2 * half)], local.at[0]
    )
    here.start()
    sent = [one, two]
    came = []
    if weights:
        cut = rows // 2
        pack_one = copy(6, pack_ref, held(f, 0, rows), {"fsdp": f1})
        pack_two = copy(7, pack_ref, held(f, 0, rows), {"fsdp": f2})
        pack_here = pltpu.make_async_copy(pack_ref, held(f, 0, rows), local.at[1])
        pack_here.start()
        sent += [pack_one, pack_two]
    one.wait_recv()
    swap_one = copy(2, at(z1, t), at(z1, t), core)
    if weights:
        pack_one.wait_recv()
        on_one = copy(8, held(f1, 0, cut), held(f1, 0, cut), {"fsdp": f2})
        pack_two.wait_recv()
        on_two = copy(9, held(f2, cut, rows - cut), held(f2, cut, rows - cut), {"fsdp": f1})
        sent += [on_one, on_two]
        came += [on_one, on_two]
    two.wait_recv()
    three = copy(4, at(z2, t), at(z2, t), near)
    swap_two = copy(3, at(z2, t), at(z2, t), core)
    three.wait_recv()
    swap_three = copy(5, at(z3, t), at(z3, t), core)
    sent += [swap_one, three, swap_two, swap_three]
    for made in came + [swap_one, swap_two, swap_three]:
        made.wait_recv()
    for made in sent:
        made.wait_send()
    here.wait()
    if weights:
        pack_here.wait()


def first_gather(n_ctx, n_fsdp, tokens, pack):
    count, width = tokens.shape
    rows, columns = pack.shape
    weights = n_fsdp == 4
    sequence, full = pl.pallas_call(
        functools.partial(first_gather_kernel, weights),
        in_specs=[pl.BlockSpec(memory_space=pl.ANY)] * 2,
        out_specs=[pl.BlockSpec(memory_space=pl.ANY)] * 2,
        out_shape=[
            jax.ShapeDtypeStruct((n_ctx * count, width), tokens.dtype),
            jax.ShapeDtypeStruct((n_fsdp * rows if weights else rows, columns), pack.dtype),
        ],
        scratch_shapes=[
            pltpu.SemaphoreType.DMA((2,)),
            pltpu.SemaphoreType.DMA((10,)),
            pltpu.SemaphoreType.DMA((10,)),
        ],
        compiler_params=pltpu.CompilerParams(collective_id=0, has_side_effects=True),
        cost_estimate=LIGHT,
    )(tokens, pack)
    if not weights:
        full = lax.all_gather(pack, "fsdp", axis=0, tiled=True)
    return sequence, full


def project_kernel(x_ref, gain_ref, w_ref, cos_ref, sin_ref, n_ref, q_ref, k_ref, v_ref):
    x = x_ref[...].astype(F32)
    n = (x * inverse_rms(x) * gain_ref[...]).astype(BF)
    n_ref[...] = n
    c = jnp.dot(n, w_ref[:, LANES:], preferred_element_type=F32)
    cos, sin = cos_ref[...], sin_ref[...]
    a = c[:, :LANES]
    b = c[:, LANES : 2 * LANES]
    a = a * cos + half_turn(a, False) * sin
    b = b * cos + half_turn(b, False) * sin
    scale = 1.0 / math.sqrt(HEAD_SIZE)
    a = a.astype(BF) * jnp.asarray(scale, BF)
    q_ref[0] = a[:, :HEAD_SIZE]
    q_ref[1] = a[:, HEAD_SIZE:]
    b = b.astype(BF)
    q_ref[2] = b[:, :HEAD_SIZE] * jnp.asarray(scale, BF)
    k_ref[...] = b[:, HEAD_SIZE:]
    v_ref[...] = c[:, 2 * LANES :].astype(BF)


def project(x, gain, w, cos, sin):
    rows, width = x.shape
    tile = 512
    row = lambda n: pl.BlockSpec((tile, n), lambda i: (i, 0))
    whole = lambda s: pl.BlockSpec(s, lambda i: (0, 0))
    return pl.pallas_call(
        project_kernel,
        grid=(rows // tile,),
        in_specs=[row(width), whole(gain.shape), whole(w.shape), row(LANES), row(LANES)],
        out_specs=[
            row(width),
            pl.BlockSpec((GROUP, tile, HEAD_SIZE), lambda i: (0, i, 0)),
            row(HEAD_SIZE),
            row(HEAD_SIZE),
        ],
        out_shape=[
            jax.ShapeDtypeStruct((rows, width), BF),
            jax.ShapeDtypeStruct((GROUP, rows, HEAD_SIZE), BF),
            jax.ShapeDtypeStruct((rows, HEAD_SIZE), BF),
            jax.ShapeDtypeStruct((rows, HEAD_SIZE), BF),
        ],
        compiler_params=params(),
        cost_estimate=LIGHT,
    )(x, gain, w, cos, sin)


def to_row(column, eye):
    return jnp.sum(jnp.where(eye, column, 0.0), axis=0, keepdims=True)


def to_column(row, eye):
    return jnp.sum(jnp.where(eye, row, 0.0), axis=1, keepdims=True)


def identity_mask():
    return lax.broadcasted_iota(jnp.int32, (SPAN, SPAN), 0) == lax.broadcasted_iota(
        jnp.int32, (SPAN, SPAN), 1
    )


def attend_kernel(weights, *refs):
    idc_ref, idr_ref, q_ref, k_ref, v_ref, shard_ref, o_ref, lse_ref, att_ref, full_ref = refs[:10]
    s_ref, m_ref, l_ref, a_ref, oall_ref, local, send, recv = refs[10:]
    i = pl.program_id(0)
    blocks = pl.num_programs(0)
    z, f = lax.axis_index("ctx"), lax.axis_index("fsdp")
    rows = shard_ref.shape[0]
    cut = rows // 2
    f1, f2 = f + 1 - 2 * (f % 2), (f + 2) % 4
    f3 = 3 - f

    def remote(k, source, target, device):
        return pltpu.make_async_remote_copy(
            src_ref=source,
            dst_ref=target,
            send_sem=send.at[k],
            recv_sem=recv.at[k],
            device_id=device,
            device_id_type=MESH,
        )

    def held(owner, first, size):
        return full_ref.at[pl.ds(pl.multiple_of(owner * rows + first, 8), size)]

    own_weights = pltpu.make_async_copy(shard_ref, held(f, 0, rows), local.at[1])
    if weights:
        one = remote(4, shard_ref, held(f, 0, rows), {"fsdp": f1})
        two = remote(5, shard_ref, held(f, 0, rows), {"fsdp": f2})
        on_one = remote(6, held(f1, 0, cut), held(f1, 0, cut), {"fsdp": f2})
        on_two = remote(7, held(f2, cut, rows - cut), held(f2, cut, rows - cut), {"fsdp": f1})

    def to(c):
        return pltpu.make_async_remote_copy(
            src_ref=oall_ref.at[pl.ds(2 * c, 2)],
            dst_ref=att_ref.at[pl.ds(2 * z, 2)],
            send_sem=send.at[c],
            recv_sem=recv.at[z],
            device_id={"ctx": c},
            device_id_type=MESH,
        )

    def back_from(c):
        return pltpu.make_async_remote_copy(
            src_ref=oall_ref.at[pl.ds(2 * c, 2)],
            dst_ref=att_ref.at[pl.ds(2 * c, 2)],
            send_sem=send.at[c],
            recv_sem=recv.at[c],
            device_id={"ctx": c},
            device_id_type=MESH,
        )

    own_rows = pltpu.make_async_copy(
        oall_ref.at[pl.ds(2 * z, 2)], att_ref.at[pl.ds(2 * z, 2)], local.at[0]
    )

    @pl.when(i == 0)
    def _():
        barrier = pltpu.get_barrier_semaphore()
        partners = [{"ctx": (z + k) % 4} for k in (1, 2, 3)]
        if weights:
            partners += [{"fsdp": f1}, {"fsdp": f2}]
        for partner in partners:
            pl.semaphore_signal(barrier, inc=1, device_id=partner, device_id_type=MESH)
        pl.semaphore_wait(barrier, len(partners))
        if weights:
            one.start()
            two.start()
            own_weights.start()

    if weights:

        @pl.when(i == 6)
        def _():
            one.wait_recv()
            on_one.start()
            two.wait_recv()
            on_two.start()

    q = q_ref[...].reshape(GROUP * SPAN, HEAD_SIZE)
    m_ref[...] = jnp.full(m_ref.shape, -1e30, F32)
    l_ref[...] = jnp.zeros(l_ref.shape, F32)
    a_ref[...] = jnp.zeros(a_ref.shape, F32)

    def place(block):
        return pl.ds(pl.multiple_of(block * SPAN, SPAN), SPAN)

    def score(block, masked):
        at = place(block)
        s = lax.dot_general(k_ref[at, :], q, NT, preferred_element_type=F32)
        if masked:
            seen = (idc_ref[at, :] <= idr_ref[...]).astype(F32)
            s = jnp.where(jnp.concatenate([seen] * GROUP, axis=1) > 0.5, s, -1e30)
        s_ref[at, :] = s
        m_ref[...] = jnp.maximum(m_ref[...], jnp.max(s, axis=0, keepdims=True))

    def weigh(block):
        at = place(block)
        p = jnp.exp(s_ref[at, :] - m_ref[...])
        l_ref[...] += jnp.sum(p, axis=0, keepdims=True)
        a_ref[...] += lax.dot_general(p.astype(BF), v_ref[at, :], TN, preferred_element_type=F32)

    def open_score(block, carried):
        score(block, False)
        return carried

    def open_weigh(block, carried):
        weigh(block)
        return carried

    lax.fori_loop(0, i, open_score, 0)
    score(i, True)

    @pl.when(i + 1 < blocks)
    def _():
        score(i + 1, True)

    lax.fori_loop(0, jnp.minimum(i + 2, blocks), open_weigh, 0)

    total = l_ref[...]
    lse = m_ref[...] + jnp.log(total)
    eye = identity_mask()
    for g in range(GROUP):
        part = slice(g * SPAN, (g + 1) * SPAN)
        out = a_ref[part, :] / to_column(total[:, part], eye)
        o_ref[:, g * HEAD_SIZE : (g + 1) * HEAD_SIZE] = out.astype(BF)
        oall_ref[i, :, g * HEAD_SIZE : (g + 1) * HEAD_SIZE] = out.astype(BF)
        lse_ref[g] = lse[:, part]
    for c in range(4):

        @pl.when(jnp.logical_and(i == 2 * c + 1, z != c))
        def _():
            to(c).start()

    @pl.when(i == 7)
    def _():
        own_rows.start()
        own_rows.wait()
        if weights:
            on_one.wait_recv()
            on_two.wait_recv()
            for made in (one, two, on_one, on_two):
                made.wait_send()
            own_weights.wait()

    for c in range(4):

        @pl.when(jnp.logical_and(i == 7, z != c))
        def _():
            to(c).wait_send()
            back_from(c).wait_recv()


def attend(n_fsdp, id_column, id_row, q, k, v, shard):
    rows = k.shape[0]
    weights = n_fsdp == 4
    anywhere = pl.BlockSpec(memory_space=pl.ANY)
    full_rows = shard.shape[0] * (n_fsdp if weights else 1)
    whole = lambda s: pl.BlockSpec(s, lambda i: (0,) * len(s))
    return pl.pallas_call(
        functools.partial(attend_kernel, weights),
        grid=(rows // SPAN,),
        in_specs=[
            whole(id_column.shape),
            pl.BlockSpec((1, SPAN), lambda i: (0, i)),
            pl.BlockSpec((GROUP, SPAN, HEAD_SIZE), lambda i: (0, i, 0)),
            whole(k.shape),
            whole(v.shape),
            anywhere,
        ],
        out_specs=[
            pl.BlockSpec((SPAN, GROUP * HEAD_SIZE), lambda i: (i, 0)),
            pl.BlockSpec((GROUP, 1, SPAN), lambda i: (0, 0, i)),
            anywhere,
            anywhere,
        ],
        out_shape=[
            jax.ShapeDtypeStruct((rows, GROUP * HEAD_SIZE), BF),
            jax.ShapeDtypeStruct((GROUP, 1, rows), F32),
            jax.ShapeDtypeStruct((8, SPAN, GROUP * HEAD_SIZE), BF),
            jax.ShapeDtypeStruct((full_rows, shard.shape[1]), BF),
        ],
        scratch_shapes=[
            pltpu.VMEM((rows, GROUP * SPAN), F32),
            pltpu.VMEM((1, GROUP * SPAN), F32),
            pltpu.VMEM((1, GROUP * SPAN), F32),
            pltpu.VMEM((GROUP * SPAN, HEAD_SIZE), F32),
            pltpu.VMEM((8, SPAN, GROUP * HEAD_SIZE), BF),
            pltpu.SemaphoreType.DMA((2,)),
            pltpu.SemaphoreType.DMA((8,)),
            pltpu.SemaphoreType.DMA((8,)),
        ],
        compiler_params=params(collective_id=2, has_side_effects=True),
        cost_estimate=LIGHT,
    )(id_column, id_row, q, k, v, shard)


def attend_back_kernel(
    idc_ref, idr_ref, q_ref, k_ref, v_ref, o_ref, do_ref, lse_ref, dq_ref, dk_ref, dv_ref, a_ref
):
    i = pl.program_id(0)
    blocks = pl.num_programs(0)

    @pl.when(i == 0)
    def _():
        dk_ref[...] = jnp.zeros(dk_ref.shape, F32)
        dv_ref[...] = jnp.zeros(dv_ref.shape, F32)

    q = q_ref[...].reshape(GROUP * SPAN, HEAD_SIZE)
    eye = identity_mask()
    grads, deltas = [], []
    for g in range(GROUP):
        lanes = slice(g * HEAD_SIZE, (g + 1) * HEAD_SIZE)
        part = do_ref[:, lanes]
        grads.append(part)
        product = part.astype(F32) * o_ref[:, lanes].astype(F32)
        deltas.append(to_row(jnp.sum(product, axis=1, keepdims=True), eye))
    do = jnp.concatenate(grads, axis=0)
    delta = jnp.concatenate(deltas, axis=1)
    lse = jnp.concatenate([lse_ref[g] for g in range(GROUP)], axis=1)
    a_ref[...] = jnp.zeros(a_ref.shape, F32)

    def step(block, masked):
        at = pl.ds(pl.multiple_of(block * SPAN, SPAN), SPAN)
        k = k_ref[at, :]
        s = lax.dot_general(k, q, NT, preferred_element_type=F32)
        p = jnp.exp(s - lse)
        if masked:
            seen = idc_ref[at, :] <= idr_ref[...]
            p = jnp.where(jnp.concatenate([seen.astype(F32)] * GROUP, axis=1) > 0.5, p, 0.0)
        dp = lax.dot_general(v_ref[at, :], do, NT, preferred_element_type=F32)
        ds = (p * (dp - delta)).astype(BF)
        dv_ref[at, :] += jnp.dot(p.astype(BF), do, preferred_element_type=F32)
        dk_ref[at, :] += jnp.dot(ds, q, preferred_element_type=F32)
        a_ref[...] += lax.dot_general(ds, k, TN, preferred_element_type=F32)

    def open_step(block, carried):
        step(block, False)
        return carried

    lax.fori_loop(0, i, open_step, 0)
    step(i, True)

    @pl.when(i + 1 < blocks)
    def _():
        step(i + 1, True)

    dq_ref[...] = a_ref[...].reshape(GROUP, SPAN, HEAD_SIZE) * (1.0 / math.sqrt(HEAD_SIZE))


def attend_back(id_column, id_row, q, k, v, o, do, lse):
    rows = k.shape[0]
    whole = lambda s: pl.BlockSpec(s, lambda i: (0,) * len(s))
    heads = pl.BlockSpec((GROUP, SPAN, HEAD_SIZE), lambda i: (0, i, 0))
    flat = pl.BlockSpec((SPAN, GROUP * HEAD_SIZE), lambda i: (i, 0))
    return pl.pallas_call(
        attend_back_kernel,
        grid=(rows // SPAN,),
        in_specs=[
            whole(id_column.shape),
            pl.BlockSpec((1, SPAN), lambda i: (0, i)),
            heads,
            whole(k.shape),
            whole(v.shape),
            flat,
            flat,
            pl.BlockSpec((GROUP, 1, SPAN), lambda i: (0, 0, i)),
        ],
        out_specs=[heads, whole(k.shape), whole(v.shape)],
        out_shape=[
            jax.ShapeDtypeStruct((GROUP, rows, HEAD_SIZE), F32),
            jax.ShapeDtypeStruct(k.shape, F32),
            jax.ShapeDtypeStruct(v.shape, F32),
        ],
        scratch_shapes=[pltpu.VMEM((GROUP * SPAN, HEAD_SIZE), F32)],
        compiler_params=params(),
        cost_estimate=LIGHT,
    )(id_column, id_row, q, k, v, o, do, lse)


def project_out_kernel(att_ref, w_ref, tok_ref, gain_ref, res_ref, n_ref, a_ref, p_ref, o_ref, send, recv):
    t = lax.axis_index("tp")
    core = {"tp": 1 - t}
    barrier = pltpu.get_barrier_semaphore()
    pl.semaphore_signal(barrier, inc=1, device_id=core, device_id_type=MESH)
    pl.semaphore_wait(barrier, 1)
    columns = att_ref.shape[2]
    sent = []
    for side in (0, 1):
        rows = slice(side * SPAN, (side + 1) * SPAN)
        for c in range(4):
            a_ref[rows, c * columns : (c + 1) * columns] = att_ref[2 * c + side]
        p_ref[side] = lax.dot_general(a_ref[rows, :], w_ref[...], NT, preferred_element_type=F32)
        made = pltpu.make_async_remote_copy(
            src_ref=p_ref.at[side],
            dst_ref=o_ref.at[side],
            send_sem=send.at[side],
            recv_sem=recv.at[side],
            device_id=core,
            device_id_type=MESH,
        )
        made.start()
        sent.append(made)
    for side in (0, 1):
        rows = slice(side * SPAN, (side + 1) * SPAN)
        sent[side].wait_recv()
        residual = tok_ref[rows, :].astype(F32) + (p_ref[side] + o_ref[side])
        res_ref[rows, :] = residual
        n_ref[rows, :] = (residual * inverse_rms(residual) * gain_ref[...]).astype(BF)
    for made in sent:
        made.wait_send()


def project_out(att, w, tokens, gain):
    rows, width = tokens.shape
    columns = w.shape[1]
    return pl.pallas_call(
        project_out_kernel,
        in_specs=[pl.BlockSpec(memory_space=pltpu.VMEM)] * 4,
        out_specs=[pl.BlockSpec(memory_space=pltpu.VMEM)] * 3,
        out_shape=[
            jax.ShapeDtypeStruct((rows, width), F32),
            jax.ShapeDtypeStruct((rows, width), BF),
            jax.ShapeDtypeStruct((rows, columns), BF),
        ],
        scratch_shapes=[
            pltpu.VMEM((2, SPAN, width), F32),
            pltpu.VMEM((2, SPAN, width), F32),
            pltpu.SemaphoreType.DMA((2,)),
            pltpu.SemaphoreType.DMA((2,)),
        ],
        compiler_params=params(collective_id=3, has_side_effects=True),
        cost_estimate=LIGHT,
    )(att, w, tokens, gain)


def residual_back_kernel(
    g_ref, res_ref, n_ref, c_ref, r_ref, gain_ref, w_ref, rg_ref, low_ref, lg_ref, gg_ref, all_ref, p_ref, local, send, recv
):
    z = lax.axis_index("ctx")
    width = res_ref.shape[1]
    barrier = pltpu.get_barrier_semaphore()
    for k in (1, 2, 3):
        pl.semaphore_signal(barrier, inc=1, device_id={"ctx": (z + k) % 4}, device_id_type=MESH)
    pl.semaphore_wait(barrier, 3)
    gain = gain_ref[...]
    gain_grad = jnp.zeros(gain.shape, F32)
    columns = p_ref.shape[3]

    def to(c, side):
        return pltpu.make_async_remote_copy(
            src_ref=p_ref.at[side, c],
            dst_ref=all_ref.at[2 * z + side],
            send_sem=send.at[side, c],
            recv_sem=recv.at[side, z],
            device_id={"ctx": c},
            device_id_type=MESH,
        )

    def back_from(c, side):
        return pltpu.make_async_remote_copy(
            src_ref=p_ref.at[side, c],
            dst_ref=all_ref.at[2 * c + side],
            send_sem=send.at[side, c],
            recv_sem=recv.at[side, c],
            device_id={"ctx": c},
            device_id_type=MESH,
        )

    own = [
        pltpu.make_async_copy(p_ref.at[side, z], all_ref.at[2 * z + side], local.at[side])
        for side in (0, 1)
    ]
    for side in (0, 1):
        rows = slice(side * SPAN, (side + 1) * SPAN)
        named = c_ref[rows, width:].astype(F32) > 0.5
        logits = jnp.dot(n_ref[rows, :], r_ref[...], preferred_element_type=F32)
        logits = jnp.where(named, logits, -1e30)
        exponent = jnp.where(
            named, jnp.exp(logits - jnp.max(logits, axis=1, keepdims=True)), 0.0
        )
        gates = exponent / jnp.sum(exponent, axis=1, keepdims=True)
        found = g_ref[rows, width:].astype(F32)
        logit_grads = (gates * (found - jnp.sum(gates * found, axis=1, keepdims=True))).astype(BF)
        lg_ref[rows, :] = logit_grads
        grads = g_ref[rows, :width].astype(F32) + lax.dot_general(
            logit_grads, r_ref[...], NT, preferred_element_type=F32
        )
        residual = res_ref[rows, :]
        inverse = inverse_rms(residual)
        gain_grad = gain_grad + jnp.sum(grads * residual * inverse, axis=0, keepdims=True)
        scaled = gain * grads
        cube = inverse * inverse * inverse / width
        total = (
            c_ref[rows, :width].astype(F32)
            + inverse * scaled
            - residual * cube * jnp.sum(scaled * residual, axis=1, keepdims=True)
        )
        rg_ref[rows, :] = total
        low = total.astype(BF)
        low_ref[rows, :] = low
        attended = jnp.dot(low, w_ref[...], preferred_element_type=F32).astype(BF)
        for c in range(4):
            p_ref[side, c] = attended[:, c * columns : (c + 1) * columns]
        for c in range(4):

            @pl.when(z != c)
            def _():
                to(c, side).start()

        own[side].start()
    gg_ref[...] = gain_grad
    for side in (0, 1):
        own[side].wait()
        for c in range(4):

            @pl.when(z != c)
            def _():
                to(c, side).wait_send()
                back_from(c, side).wait_recv()


def residual_back(grad, residual, normed, cot, router, gain, w):
    rows, width = residual.shape
    columns = w.shape[1] // 4
    vmem = pl.BlockSpec(memory_space=pltpu.VMEM)
    return pl.pallas_call(
        residual_back_kernel,
        in_specs=[vmem] * 7,
        out_specs=[vmem] * 4 + [pl.BlockSpec(memory_space=pl.ANY)],
        out_shape=[
            jax.ShapeDtypeStruct((rows, width), F32),
            jax.ShapeDtypeStruct((rows, width), BF),
            jax.ShapeDtypeStruct((rows, LANES), BF),
            jax.ShapeDtypeStruct((1, width), F32),
            jax.ShapeDtypeStruct((8, SPAN, columns), BF),
        ],
        scratch_shapes=[
            pltpu.VMEM((2, 4, SPAN, columns), BF),
            pltpu.SemaphoreType.DMA((2,)),
            pltpu.SemaphoreType.DMA((2, 4)),
            pltpu.SemaphoreType.DMA((2, 4)),
        ],
        compiler_params=params(collective_id=4, has_side_effects=True),
        cost_estimate=LIGHT,
    )(grad, residual, normed, cot, router, gain, w)


def joint_back_kernel(
    dq_ref, dk_ref, dv_ref, cos_ref, sin_ref, w_ref, tok_ref, gain_ref, rg_ref,
    jg_ref, in_ref, gg_ref, land_ref, a_ref, p_ref, o_ref, send, recv, core_send, core_recv,
):
    z, t = lax.axis_index("ctx"), lax.axis_index("tp")
    core = {"tp": 1 - t}
    barrier = pltpu.get_barrier_semaphore()
    for partner in [{"ctx": (z + k) % 4} for k in (1, 2, 3)] + [core]:
        pl.semaphore_signal(barrier, inc=1, device_id=partner, device_id_type=MESH)
    pl.semaphore_wait(barrier, 4)
    columns = jg_ref.shape[2]
    rows_here = jg_ref.shape[1]

    def to(c):
        return pltpu.make_async_remote_copy(
            src_ref=jg_ref.at[c],
            dst_ref=land_ref.at[z],
            send_sem=send.at[c],
            recv_sem=recv.at[z],
            device_id={"ctx": c},
            device_id_type=MESH,
        )

    def back_from(c):
        return pltpu.make_async_remote_copy(
            src_ref=jg_ref.at[c],
            dst_ref=land_ref.at[c],
            send_sem=send.at[c],
            recv_sem=recv.at[c],
            device_id={"ctx": c},
            device_id_type=MESH,
        )

    for c in range(4):
        rows = slice(c * rows_here, (c + 1) * rows_here)
        cos, sin = cos_ref[rows, :], sin_ref[rows, :]
        a = jnp.concatenate([dq_ref[0, rows, :], dq_ref[1, rows, :]], axis=1)
        b = jnp.concatenate([dq_ref[2, rows, :], dk_ref[rows, :]], axis=1)
        jg_ref[c, :, :LANES] = (a * cos + half_turn(a, True) * sin).astype(BF)
        jg_ref[c, :, LANES : 2 * LANES] = (b * cos + half_turn(b, True) * sin).astype(BF)
        jg_ref[c, :, 2 * LANES :] = dv_ref[rows, :].astype(BF)

        @pl.when(z != c)
        def _():
            to(c).start()

    for c in range(4):
        place = slice(c * columns, (c + 1) * columns)

        @pl.when(z == c)
        def _():
            a_ref[:, place] = jg_ref[c]

        @pl.when(z != c)
        def _():
            back_from(c).wait_recv()
            a_ref[:, place] = land_ref[c]

    sent = []
    for side in (0, 1):
        rows = slice(side * SPAN, (side + 1) * SPAN)
        p_ref[side] = lax.dot_general(
            a_ref[rows, :], w_ref[...], NT, preferred_element_type=F32
        ).astype(BF)
        made = pltpu.make_async_remote_copy(
            src_ref=p_ref.at[side],
            dst_ref=o_ref.at[side],
            send_sem=core_send.at[side],
            recv_sem=core_recv.at[side],
            device_id=core,
            device_id_type=MESH,
        )
        made.start()
        sent.append(made)
    gain = gain_ref[...]
    width = gain.shape[1]
    gain_grad = jnp.zeros(gain.shape, F32)
    for side in (0, 1):
        rows = slice(side * SPAN, (side + 1) * SPAN)
        sent[side].wait_recv()
        grads = p_ref[side].astype(F32) + o_ref[side].astype(F32)
        tokens = tok_ref[rows, :].astype(F32)
        inverse = inverse_rms(tokens)
        gain_grad = gain_grad + jnp.sum(grads * tokens * inverse, axis=0, keepdims=True)
        scaled = gain * grads
        cube = inverse * inverse * inverse / width
        in_ref[rows, :] = (
            rg_ref[rows, :]
            + inverse * scaled
            - tokens * cube * jnp.sum(scaled * tokens, axis=1, keepdims=True)
        )
    gg_ref[...] = gain_grad
    for made in sent:
        made.wait_send()
    for c in range(4):

        @pl.when(z != c)
        def _():
            to(c).wait_send()


def joint_back(dq, dk, dv, cos, sin, w, tokens, gain, grads):
    rows, width = tokens.shape
    columns = (GROUP + 2) * HEAD_SIZE
    vmem = pl.BlockSpec(memory_space=pltpu.VMEM)
    return pl.pallas_call(
        joint_back_kernel,
        in_specs=[vmem] * 9,
        out_specs=[vmem] * 3,
        out_shape=[
            jax.ShapeDtypeStruct((4, rows, columns), BF),
            jax.ShapeDtypeStruct((rows, width), F32),
            jax.ShapeDtypeStruct((1, width), F32),
        ],
        scratch_shapes=[
            pltpu.VMEM((4, rows, columns), BF),
            pltpu.VMEM((rows, 4 * columns), BF),
            pltpu.VMEM((2, SPAN, width), BF),
            pltpu.VMEM((2, SPAN, width), BF),
            pltpu.SemaphoreType.DMA((4,)),
            pltpu.SemaphoreType.DMA((4,)),
            pltpu.SemaphoreType.DMA((2,)),
            pltpu.SemaphoreType.DMA((2,)),
        ],
        compiler_params=params(collective_id=5, has_side_effects=True),
        cost_estimate=LIGHT,
    )(dq, dk, dv, cos, sin, w, tokens, gain, grads)


def owner_of(f, k):
    return [f, f + 1 - 2 * (f % 2), (f + 2) % 4, 3 - f][k]


def expert_kernel(count, pieces, n_ref, cot_ref, one_ref, two_ref, r_ref, w_any, shard_ref, *refs):
    pre_ref, wh_ref = refs[:2]
    x_parts, cot_parts = refs[2 : 2 + pieces], refs[2 + pieces : 2 + 2 * pieces]
    grad_any, joint_ref, out_any, far_any = refs[2 + 2 * pieces : 6 + 2 * pieces]
    x_ref, c_ref, w_ref, part_ref, there_ref, back_ref, full_ref = refs[6 + 2 * pieces : -7]
    out_ref, out_there, out_near = refs[-7:-4]
    local, wrote, send, recv = refs[-4:]
    i = pl.program_id(0)
    z, t, f = lax.axis_index("ctx"), lax.axis_index("tp"), lax.axis_index("fsdp")
    z1, z2, z3 = z + 1 - 2 * (z % 2), (z + 2) % 4, 3 - z
    near, far, third, core = {"ctx": z1}, {"ctx": z2}, {"ctx": z3}, {"tp": 1 - t}
    half, width = x_ref.shape[1:]
    piece = width // pieces
    hidden_columns = wh_ref.shape[1]
    units = hidden_columns // count

    def rows(side):
        return pl.ds(pl.multiple_of(side * half, half), half)

    def remote(k, source, target, device):
        return pltpu.make_async_remote_copy(
            src_ref=source,
            dst_ref=target,
            send_sem=send.at[k],
            recv_sem=recv.at[k],
            device_id=device,
            device_id_type=MESH,
        )

    own = n_ref.at[rows(t)]
    x_one = remote(0, own, x_ref.at[2], near)
    x_two = remote(1, own, x_ref.at[4], far)
    x_three = remote(2, x_ref.at[4], x_ref.at[6], near)
    c_three = remote(3, two_ref, c_ref.at[6], near)
    x_swaps = [None] + [remote(3 + m, x_ref.at[2 * m], x_ref.at[2 * m + 1], core) for m in (1, 2, 3)]
    c_swaps = [
        None,
        remote(7, one_ref, c_ref.at[3], core),
        remote(8, two_ref, c_ref.at[5], core),
        remote(9, c_ref.at[6], c_ref.at[7], core),
    ]
    crossed = [remote(10 + m, part_ref.at[2 * m + 1], there_ref.at[m], core) for m in range(4)]
    returned = [None] + [
        remote(13 + m, part_ref.at[2 * m], back_ref.at[m], device)
        for m, device in ((1, near), (2, far), (3, third))
    ]
    out_crossed = [
        remote(22 + m, out_ref.at[2 * m + 1], out_there.at[m], core) for m in range(4)
    ]
    out_sent = [remote(26 + n, out_ref.at[4 * n + 2], out_near.at[n], near) for n in (0, 1)]
    out_stores = [
        pltpu.make_async_copy(out_ref.at[0], out_any, local.at[9]),
        pltpu.make_async_copy(out_ref.at[4], far_any, local.at[10]),
    ]
    last = remote(17, full_ref.at[rows(t)], full_ref.at[rows(t)], core)
    loads = [
        pltpu.make_async_copy(source, target, local.at[k])
        for k, (source, target) in enumerate(
            (
                (n_ref.at[rows(t)], x_ref.at[0]),
                (n_ref.at[rows(1 - t)], x_ref.at[1]),
                (cot_ref.at[rows(t)], c_ref.at[0]),
                (cot_ref.at[rows(1 - t)], c_ref.at[1]),
                (w_any, w_ref),
                (one_ref, c_ref.at[2]),
                (two_ref, c_ref.at[4]),
            )
        )
    ]
    store = pltpu.make_async_copy(full_ref, grad_any, local.at[7])
    carried = []
    if pieces > 1:
        shard_rows = shard_ref.shape[0]
        cut = shard_rows // 2
        f1, f2 = owner_of(f, 1), owner_of(f, 2)

        def held(place, first, size):
            return joint_ref.at[pl.ds(pl.multiple_of(place * shard_rows + first, 8), size)]

        own_shard = pltpu.make_async_copy(shard_ref, held(f, 0, shard_rows), local.at[8])
        joint_one = remote(18, shard_ref, held(f, 0, shard_rows), {"fsdp": f1})
        joint_two = remote(19, shard_ref, held(f, 0, shard_rows), {"fsdp": f2})
        later = shard_rows - cut
        on_one = remote(20, held(f1, 0, cut), held(f1, 0, cut), {"fsdp": f2})
        on_two = remote(21, held(f2, cut, later), held(f2, cut, later), {"fsdp": f1})
        carried = [joint_one, joint_two, on_one, on_two]

    def keep(step):
        made = []
        at_rows = pl.ds(pl.multiple_of(step * half, half), half)
        for k in range(pieces):
            owner = [f, f + 1 - 2 * (f % 2), (f + 2) % 4, 3 - f][k] if pieces > 1 else 0
            at = pl.ds(pl.multiple_of(owner * piece, piece), piece)
            for n, (source, target) in enumerate(((x_ref, x_parts[k]), (c_ref, cot_parts[k]))):
                made.append(
                    pltpu.make_async_copy(
                        source.at[step, :, at], target.at[at_rows], wrote.at[step, 2 * k + n]
                    )
                )
        return made

    def finish(m):
        crossed[m].wait_recv()
        part_ref[2 * m] = (part_ref[2 * m].astype(F32) + there_ref[m].astype(F32)).astype(BF)
        if m:
            returned[m].start()

    def finish_out(m):
        out_crossed[m].wait_recv()
        out_ref[2 * m] = (out_ref[2 * m].astype(F32) + out_there[m].astype(F32)).astype(BF)
        if m % 2:
            out_sent[m // 2].start()

    @pl.when(i == 0)
    def _():
        partners = [near, far, third, core]
        if carried:
            partners += [{"fsdp": f1}, {"fsdp": f2}]
        barrier = pltpu.get_barrier_semaphore()
        for partner in partners:
            pl.semaphore_signal(barrier, inc=1, device_id=partner, device_id_type=MESH)
        pl.semaphore_wait(barrier, len(partners))
        if carried:
            joint_one.start()
            joint_two.start()
            own_shard.start()
        for made in [x_one, x_two] + loads + [c_swaps[1], c_swaps[2], c_three]:
            made.start()
        for made in (loads[0], loads[2], loads[4]):
            made.wait()

    @pl.when(i == 1)
    def _():
        loads[1].wait()
        loads[3].wait()

    @pl.when(i == 2)
    def _():
        x_one.wait_recv()
        x_swaps[1].start()
        loads[5].wait()

    @pl.when(i == 3)
    def _():
        x_swaps[1].wait_recv()
        c_swaps[1].wait_recv()

    @pl.when(i == 4)
    def _():
        x_two.wait_recv()
        x_three.start()
        x_swaps[2].start()
        loads[6].wait()

    @pl.when(i == 5)
    def _():
        x_swaps[2].wait_recv()
        c_swaps[2].wait_recv()

    @pl.when(i == 6)
    def _():
        finish(2)
        x_three.wait_recv()
        x_swaps[3].start()
        c_three.wait_recv()
        c_swaps[3].start()

        if carried:
            joint_one.wait_recv()
            on_one.start()
            joint_two.wait_recv()
            on_two.start()

    @pl.when(i == 7)
    def _():
        x_swaps[3].wait_recv()
        c_swaps[3].wait_recv()

    for made in keep(i):
        made.start()

    def columns(j, e):
        return slice(j * hidden_columns + e * units, j * hidden_columns + (e + 1) * units)

    x = x_ref[i]
    both = c_ref[i]
    cot = both[:, :width]
    named = both[:, width:].astype(F32) > 0.5
    logits = jnp.where(named, jnp.dot(x, r_ref[...], preferred_element_type=F32), -1e30)
    top = jnp.max(logits, axis=1, keepdims=True)
    exponent = jnp.where(named, jnp.exp(logits - top), 0.0)
    gates = exponent / jnp.sum(exponent, axis=1, keepdims=True)
    lane = lax.broadcasted_iota(jnp.int32, gates.shape, 1)
    found = jnp.zeros(gates.shape, F32)
    for e in range(count):
        mine = lane == z * count + e
        gate_here = jnp.sum(jnp.where(mine, gates, 0.0), axis=1, keepdims=True)
        g = jnp.dot(x, w_ref[:, columns(0, e)], preferred_element_type=F32)
        u = jnp.dot(x, w_ref[:, columns(1, e)], preferred_element_type=F32)
        hg = jnp.dot(cot, w_ref[:, columns(2, e)], preferred_element_type=F32)
        s = 1.0 / (1.0 + jnp.exp(-g))
        gs = g * s
        h = (gs * u).astype(BF).astype(F32)
        found = found + jnp.where(mine, jnp.sum(h * hg, axis=1, keepdims=True), 0.0)
        wh_ref[:, columns(0, e)] = (h * gate_here).astype(BF)
        hg = hg * gate_here
        pre_ref[:, columns(0, e)] = (hg * u * s * (1.0 + g * (1.0 - s))).astype(BF)
        pre_ref[:, columns(1, e)] = (hg * gs).astype(BF)
    part_ref[i, :, width:] = found.astype(BF)
    part_ref[i, :, :width] = lax.dot_general(
        pre_ref[...], w_ref[:, : 2 * hidden_columns], NT, preferred_element_type=F32
    ).astype(BF)
    for m in range(4):

        @pl.when(i == 2 * m + 1)
        def _():
            crossed[m].start()

    out_ref[i] = lax.dot_general(
        wh_ref[...], w_ref[:, 2 * hidden_columns :], NT, preferred_element_type=F32
    ).astype(BF)
    for m in range(4):

        @pl.when(i == 2 * m + 1)
        def _():
            out_crossed[m].start()

    for m in range(2):

        @pl.when(i == 2 * m + 2)
        def _():
            finish(m)

    @pl.when(i == 6)
    def _():
        finish_out(1)

    @pl.when(i == 7)
    def _():
        finish(3)
        for m in (3, 0, 2):
            finish_out(m)
        total = part_ref[0].astype(F32)
        for m in (1, 2, 3):
            returned[m].wait_recv()
            total = total + back_ref[m].astype(F32)
        full_ref[rows(t), :] = total.astype(BF)
        last.start()
        for n in (0, 1):
            out_sent[n].wait_recv()
            out_ref[4 * n] = (out_ref[4 * n].astype(F32) + out_near[n].astype(F32)).astype(BF)
            out_stores[n].start()
        for made in out_crossed + out_sent:
            made.wait_send()
        for made in out_stores:
            made.wait()
        for made in [x_one, x_two, x_three, c_three] + x_swaps[1:] + c_swaps[1:] + crossed:
            made.wait_send()
        for made in returned[1:]:
            made.wait_send()
        last.wait_send()
        last.wait_recv()
        store.start()
        if carried:
            on_one.wait_recv()
            on_two.wait_recv()
            for made in carried:
                made.wait_send()
            own_shard.wait()

        def settle(step, carried):
            for made in keep(step):
                made.wait()
            return carried

        lax.fori_loop(0, 8, settle, 0)
        store.wait()


def experts(pieces, normed, cot, one, two, router, w, shard, count):
    rows, width = normed.shape
    half = rows // 2
    packed = cot.shape[1]
    hidden_columns = w.shape[1] // 3
    slot = lambda n: pl.BlockSpec((half, n), lambda i: (i, 0))
    anywhere = pl.BlockSpec(memory_space=pl.ANY)
    blocks = [2 * hidden_columns, hidden_columns]
    return pl.pallas_call(
        functools.partial(expert_kernel, count, pieces),
        grid=(8,),
        in_specs=[anywhere] * 4 + [pl.BlockSpec(router.shape, lambda i: (0, 0)), anywhere, anywhere],
        out_specs=[slot(n) for n in blocks] + [anywhere] * (2 * pieces + 4),
        out_shape=[
            jax.ShapeDtypeStruct((8 * half, n), BF) for n in blocks + [width // pieces] * (2 * pieces)
        ]
        + [
            jax.ShapeDtypeStruct((rows, packed), BF),
            jax.ShapeDtypeStruct((pieces * shard.shape[0], shard.shape[1]), BF),
            jax.ShapeDtypeStruct((half, width), BF),
            jax.ShapeDtypeStruct((half, width), BF),
        ],
        scratch_shapes=[
            pltpu.VMEM((8, half, width), BF),
            pltpu.VMEM((8, half, packed), BF),
            pltpu.VMEM(w.shape, BF),
            pltpu.VMEM((8, half, packed), BF),
            pltpu.VMEM((4, half, packed), BF),
            pltpu.VMEM((4, half, packed), BF),
            pltpu.VMEM((rows, packed), BF),
            pltpu.VMEM((8, half, width), BF),
            pltpu.VMEM((4, half, width), BF),
            pltpu.VMEM((2, half, width), BF),
            pltpu.SemaphoreType.DMA((11,)),
            pltpu.SemaphoreType.DMA((8, 2 * pieces)),
            pltpu.SemaphoreType.DMA((28,)),
            pltpu.SemaphoreType.DMA((28,)),
        ],
        compiler_params=params(collective_id=1, has_side_effects=True),
        cost_estimate=LIGHT,
    )(normed, cot, one, two, router, w, shard)


def adamw(master, first_moment, second_moment, gradient, rate, decay):
    moment_new = 0.9 * first_moment + 0.1 * gradient
    square_new = 0.95 * second_moment + 0.05 * gradient * gradient
    corrected = moment_new / (1.0 - 0.9**STEP) / (jnp.sqrt(square_new / (1.0 - 0.95**STEP)) + 1e-08)
    master_new = master - rate * (corrected + decay * master)
    return (master_new, moment_new, square_new, master_new.astype(BF))


def expert_adamw_kernel(rate, joined, *refs):
    p_ref, f_ref, s_ref, g_ref = refs[:4]
    master_ref, moment_ref, rounded_ref, square_ref, grad_ref = refs[-5:]
    parts, _, columns = g_ref.shape
    units = p_ref.shape[3]
    each = columns // units
    for k in range(parts):
        for e in range(each):
            grad_ref[:, k * each + e, :] = g_ref[k, :, e * units : (e + 1) * units].astype(F32)
    for at in range(0, parts * each, 8):
        rows = slice(at, at + 8)
        new = adamw(
            p_ref[:, 0, rows], f_ref[:, 0, rows], s_ref[:, 0, rows], grad_ref[:, rows], rate, 0.1
        )
        master_ref[:, 0, rows] = new[0]
        moment_ref[:, 0, rows] = new[1]
        rounded_ref[:, 0, rows] = new[3]
        if joined:
            square_ref[:, rows, 0] = refs[4][:, rows]
            square_ref[:, rows, 1] = new[2]
        else:
            square_ref[:, rows] = new[2]


def expert_adamw(slot, rate, weight, first, second, gradient, earlier, joined=None):
    rows, _, count, units = weight.shape
    parts = gradient.shape[0]
    tile = next(t for t in (64, 16, 8) if rows % t == 0)
    here = pl.BlockSpec((tile, 1, count, units), lambda i: (i, slot, 0, 0))
    plain = pl.BlockSpec((tile, count, units), lambda i: (i, 0, 0))
    pair = pl.BlockSpec((tile, count, 2, units), lambda i: (i, 0, 0, 0))
    shape = jax.ShapeDtypeStruct(weight.shape, F32)
    chained = len(earlier)
    more = [] if joined is None else [joined]
    square = (rows, count, units) if joined is None else (rows, count, 2, units)
    return pl.pallas_call(
        functools.partial(expert_adamw_kernel, rate, joined is not None),
        grid=(rows // tile,),
        in_specs=[here, here, here]
        + [pl.BlockSpec((parts, tile, gradient.shape[2]), lambda i: (0, i, 0))]
        + [plain] * len(more)
        + [pl.BlockSpec(memory_space=pl.ANY)] * chained,
        out_specs=[here, here, here, plain if joined is None else pair],
        out_shape=[
            shape,
            shape,
            jax.ShapeDtypeStruct(weight.shape, BF),
            jax.ShapeDtypeStruct(square, F32),
        ],
        scratch_shapes=[pltpu.VMEM((tile, count, units), F32)],
        input_output_aliases={4 + len(more) + k: k for k in range(chained)},
        compiler_params=params(),
        cost_estimate=pl.CostEstimate(
            flops=20 * rows * count * units,
            bytes_accessed=45 * rows * count * units,
            transcendentals=rows * count * units,
        ),
    )(weight, first, second, gradient, *more, *earlier)


def matrix_adamw_kernel(rate, p_ref, f_ref, s_ref, g_ref, *outs):
    grad = g_ref[...].astype(F32).T
    new = adamw(p_ref[...], f_ref[...], s_ref[...], grad, rate, 0.1)
    for ref, value in zip(outs, new):
        ref[...] = value


def matrix_adamw(rate, weight, first, second, turned):
    rows, columns = weight.shape
    if rows % LANES:
        return adamw(weight, first, second, turned[:columns].T.astype(F32), rate, 0.1)
    tile = 256
    here = pl.BlockSpec((rows, tile), lambda i: (0, i))
    shape = jax.ShapeDtypeStruct(weight.shape, F32)
    return pl.pallas_call(
        functools.partial(matrix_adamw_kernel, rate),
        grid=(columns // tile,),
        in_specs=[here, here, here, pl.BlockSpec((tile, rows), lambda i: (i, 0))],
        out_specs=[here] * 4,
        out_shape=[shape, shape, shape, jax.ShapeDtypeStruct(weight.shape, BF)],
        compiler_params=params(),
        cost_estimate=pl.CostEstimate(
            flops=20 * rows * columns, bytes_accessed=28 * rows * columns, transcendentals=0
        ),
    )(weight, first, second, turned)


def local(
    sizes,
    block_input,
    out_cotangent,
    block_ids,
    expert_routes,
    norm_gains,
    gains_first,
    gains_second,
    joint_weight,
    joint_first,
    joint_second,
    output_weight,
    output_first,
    output_second,
    router_weight,
    router_first,
    router_second,
    expert_weight,
    expert_first,
    expert_second,
):
    n_fsdp, n_ctx, n_tp = sizes
    z = lax.axis_index("ctx")
    t = lax.axis_index("tp")
    f = lax.axis_index("fsdp")
    tokens_low = block_input[0]
    cot_low = out_cotangent[0]
    count, width = tokens_low.shape
    half = count // n_tp
    length = n_ctx * count
    own_rows = width // n_fsdp
    each = E // n_ctx

    barrier = lax.optimization_barrier

    def beyond(x, m):
        return lax.ppermute(x, "ctx", [(i, i ^ m) for i in range(n_ctx)])

    def swap(x):
        return lax.ppermute(x, "tp", [(0, 1), (1, 0)])

    def across(x, m):
        return lax.ppermute(x, "fsdp", [(i, i ^ m) for i in range(n_fsdp)])

    def mine(x):
        return lax.dynamic_slice_in_dim(x, t * half, half, 0)

    def other(x):
        return lax.dynamic_slice_in_dim(x, (1 - t) * half, half, 0)

    def in_order(a, b):
        return jnp.where(t == 0, jnp.concatenate([a, b], 0), jnp.concatenate([b, a], 0))

    def put(buffer, x, place):
        return lax.dynamic_update_slice_in_dim(buffer, x[None], place, 0)

    def put_row(x, row, place):
        return lax.dynamic_update_slice(x, row[None], (place, 0))

    def take(x, place, places):
        return lax.dynamic_index_in_dim(
            x.reshape(places, x.shape[0] // places, x.shape[1]), place, 0, keepdims=False
        )

    def sent_to_owners(x):
        if n_fsdp != 4:
            return [lax.psum_scatter(x, "fsdp", scatter_dimension=1, tiled=True)]
        part = lambda k: lax.dynamic_slice_in_dim(x, (f ^ k) * own_rows, own_rows, 1)
        return [part(0)] + [across(part(k), k) for k in (1, 2, 3)]

    def added(came):
        return came[0] if len(came) == 1 else sum(x.astype(F32) for x in came).astype(BF)

    def spread(x):
        one, two = beyond(x, 1), beyond(x, 2)
        return {1: one, 2: two, 3: beyond(two, 1)}

    slots_first = jnp.transpose(expert_weight, (0, 2, 1, 3))
    units = expert_weight.shape[3]
    expert_part = (
        lax.dynamic_slice_in_dim(slots_first, z * each, each, 2)
        .astype(BF)
        .reshape(own_rows, 3 * each * units)
    )
    expert_full = lax.all_gather(expert_part, "fsdp", axis=0, tiled=True)

    group_columns = (GROUP + 2) * HEAD_SIZE
    head_columns = GROUP * HEAD_SIZE
    joint_low = joint_weight.astype(BF)
    output_columns = output_weight.shape[1]
    first_pack = jnp.concatenate(
        [
            router_weight.astype(BF),
            norm_gains.T.astype(BF),
            jnp.zeros((own_rows, LANES - E - 2), BF),
            lax.dynamic_slice_in_dim(joint_low, z * group_columns, group_columns, 1),
        ],
        axis=1,
    )
    first_pack, _ = barrier((first_pack, expert_part))
    sequence, first_full = first_gather(n_ctx, n_fsdp, tokens_low, first_pack)
    small_full = first_full[:, :LANES]
    router_full = small_full[:, :E]
    router_wide = jnp.where(jnp.arange(LANES)[None, :] < E, small_full, jnp.zeros((), BF))
    gain_first = small_full[:, E].astype(F32)[None, :]
    gain_second = small_full[:, E + 1].astype(F32)[None, :]

    route_rows = expert_routes[0]
    lane_row = jnp.arange(LANES, dtype=jnp.int32)[None, :]
    member = sum((route_rows[:, k : k + 1] == lane_row).astype(F32) for k in range(route_rows.shape[1]))
    cot_pack = jnp.concatenate([cot_low, member.astype(BF)], axis=1)
    cot_half, sequence = barrier((mine(cot_pack), sequence))
    cot_came = [beyond(cot_half, 1), beyond(cot_half, 2)]

    lanes = jnp.arange(LANES, dtype=jnp.int32) % (HEAD_SIZE // 2)
    frequency = jnp.exp(lanes.astype(F32) * (-2.0 * math.log(10000.0) / HEAD_SIZE))
    fine = 64
    small_angles = jnp.arange(fine, dtype=jnp.int32).astype(F32)[:, None] * frequency
    large_angles = (fine * jnp.arange(length // fine, dtype=jnp.int32)).astype(F32)[:, None] * frequency
    cos_a, sin_a = jnp.cos(large_angles)[:, None], jnp.sin(large_angles)[:, None]
    cos_b, sin_b = jnp.cos(small_angles)[None], jnp.sin(small_angles)[None]
    cosine = (cos_a * cos_b - sin_a * sin_b).reshape(length, LANES)
    sine = (sin_a * cos_b + cos_a * sin_b).reshape(length, LANES)
    cosine, sine, tokens_low = barrier((cosine, sine, tokens_low))
    id_row = block_ids
    id_column = block_ids.reshape(length, 1)
    normed_all, queries, keys, values = project(sequence, gain_first, first_full, cosine, sine)
    output_low = output_weight.astype(BF)
    attended_all, lse, attended_here, output_full = attend(
        n_fsdp, id_column, id_row, queries, keys, values, output_low
    )
    if n_fsdp != 4:
        output_full = lax.all_gather(output_low, "fsdp", axis=0, tiled=True)
    residual, normed_second, attended = project_out(
        attended_here, output_full, tokens_low, gain_second
    )

    pieces = n_fsdp if n_fsdp == 4 else 1
    pre_all, hidden_all, *kept, grad_rows, joint_full, out_here, out_two = experts(
        pieces, normed_second, cot_pack, *cot_came, router_wide, expert_full, joint_low, each
    )
    if pieces == 1:
        joint_full = lax.all_gather(joint_low, "fsdp", axis=0, tiled=True)
    x_parts, cot_parts = kept[:pieces], kept[pieces:]

    wide = each * units

    def expert_terms(j):
        left = cot_parts if j == 2 else x_parts
        right = hidden_all if j == 2 else pre_all[:, j * wide : (j + 1) * wide]
        return [
            lax.dot_general(left[k], right, TN, preferred_element_type=F32).astype(BF)
            for k in range(pieces)
        ]

    terms = {j: expert_terms(j) for j in (2, 0, 1)}
    pieces_came = {}
    for j in (2, 0, 1):
        if pieces > 1:
            pieces_came[j] = [terms[j][0]] + [across(terms[j][k], k) for k in range(1, pieces)]
        else:
            pieces_came[j] = [
                lax.psum_scatter(terms[j][0], "fsdp", scatter_dimension=0, tiled=True)
            ]

    def gathered(came):
        return lax.all_gather(added(came), "ctx", axis=0, tiled=False)

    grad_rows, terms[2] = barrier((grad_rows, terms[2]))
    residual_grads, residual_low, logit_grads, gain_second_grad, attended_grads_all = residual_back(
        grad_rows, residual, normed_second, cot_pack, router_wide, gain_second, output_full
    )
    attended_grads_all, pieces_came[2], *_ = barrier(
        (attended_grads_all, pieces_came[2], terms[0], terms[1])
    )
    expert_sums = {2: gathered(pieces_came[2])}
    step = 64
    few_rows = jnp.concatenate([logit_grads[:, :E], jnp.zeros((count, step - E), BF)], axis=1)
    rest_term = jnp.concatenate(
        [
            lax.dot_general(attended, residual_low, TN, preferred_element_type=F32).astype(BF),
            lax.dot_general(few_rows, normed_second, TN, preferred_element_type=F32).astype(BF),
        ],
        axis=0,
    )
    rest_term = lax.dynamic_update_slice(
        rest_term, gain_second_grad.astype(BF), (output_columns + E, 0)
    )
    rest_term, attended_grads_all = barrier((rest_term, attended_grads_all))
    dq, dk, dv = attend_back(
        id_column,
        id_row,
        queries,
        keys,
        values,
        attended_all,
        attended_grads_all.reshape(length, head_columns),
        lse,
    )
    dq, pieces_came[0] = barrier((dq, pieces_came[0]))
    expert_sums[0] = gathered(pieces_came[0])
    joint_grads, input_rows, gain_first_grad = joint_back(
        dq, dk, dv, cosine, sine, joint_full, tokens_low, gain_first, residual_grads
    )
    joint_grads, pieces_came[1], rest_term, out_two = barrier(
        (joint_grads, pieces_came[1], rest_term, out_two)
    )
    out_far = beyond(out_two, 2)
    expert_sums[1] = gathered(pieces_came[1])
    joint_grads_all = joint_grads.reshape(length, group_columns)

    first_view = jnp.transpose(expert_first, (0, 2, 1, 3))
    second_view = jnp.transpose(expert_second, (0, 2, 1, 3))
    made = []
    squares = {}

    def expert_step(j, joined=None):
        rate = 0.25 if j == 2 else 0.03
        *made[:], squares[j] = expert_adamw(
            j, rate, slots_first, first_view, second_view, expert_sums[j], tuple(made), joined
        )

    joint_term = lax.dot_general(joint_grads_all, normed_all, TN, preferred_element_type=F32)
    joint_term = jnp.concatenate(
        [
            joint_term.astype(BF),
            jnp.where(jnp.arange(16)[:, None] == 0, gain_first_grad, 0.0).astype(BF),
            rest_term,
        ],
        axis=0,
    )
    joint_came = sent_to_owners(joint_term)

    expert_step(2)
    joint_came, made[:], squares[2] = barrier((joint_came, made, squares[2]))
    joint_owned = added(joint_came)
    rest_owned = put_row(
        joint_owned[group_columns + 16 :], joint_owned[group_columns], output_columns + E + 1
    )
    joint_owned = joint_owned[:group_columns]
    rest_parts = [take(rest_owned, z, n_ctx)]
    rest_parts += [beyond(take(rest_owned, z ^ m, n_ctx), m) for m in range(1, n_ctx)]
    expert_step(0)
    rest_parts, made[:], squares[0] = barrier((rest_parts, made, squares[0]))
    rest_low = sum(x.astype(F32) for x in rest_parts).astype(BF)
    both = jnp.concatenate([joint_owned, rest_low], axis=0)
    both_all = {0: both, **spread(both)}
    expert_step(1, squares[0])
    both_all, out_far, made[:] = barrier((both_all, out_far, made))
    full = jnp.zeros((n_ctx, *both.shape), BF)
    for m, got in both_all.items():
        full = put(full, got, z ^ m)
    joint_sum = full[:, :group_columns].reshape(n_ctx * group_columns, own_rows)
    rest_full = full[:, group_columns:].reshape(output_columns + step, own_rows)
    moe_low = (out_here.astype(F32) + out_far.astype(F32)).astype(BF)
    moe_rows = in_order(moe_low, swap(moe_low)).astype(F32)
    block_output = (residual + moe_rows).astype(BF)[None]
    router_sum = rest_full[output_columns : output_columns + E].T.astype(F32)
    gains_sum = jnp.stack(
        [rest_full[output_columns + E + 1], rest_full[output_columns + E]]
    ).astype(F32)

    gains_new = adamw(norm_gains, gains_first, gains_second, gains_sum, 0.6, 0.0)
    joint_new = matrix_adamw(0.03, joint_weight, joint_first, joint_second, joint_sum)
    output_new = matrix_adamw(0.25, output_weight, output_first, output_second, rest_full)
    router_new = adamw(router_weight, router_first, router_second, router_sum, 0.015, 0.1)

    back = lambda x: jnp.transpose(x, (0, 2, 1, 3))
    return (
        block_output,
        input_rows[None],
        *gains_new,
        *joint_new,
        *output_new,
        *router_new,
        back(made[0]),
        back(made[1]),
        squares[1],
        squares[2],
        back(made[2]),
    )


def solution(mesh):
    rows = P("fsdp", "ctx", None)
    gains = P(None, "fsdp")
    matrix = P("fsdp", "tp")
    router = P("fsdp", None)
    expert = P("fsdp", None, None, "tp")
    sizes = (mesh.shape["fsdp"], mesh.shape["ctx"], mesh.shape["tp"])
    return jax.shard_map(
        functools.partial(local, sizes),
        mesh=mesh,
        in_specs=(rows, rows, P("fsdp", None), rows)
        + (gains,) * 3
        + (matrix,) * 6
        + (router,) * 3
        + (expert,) * 3,
        out_specs=(rows, rows)
        + (gains,) * 4
        + (matrix,) * 8
        + (router,) * 4
        + (expert, expert, expert, P("fsdp", None, "tp"), expert),
        check_vma=False,
    )
```
